128 devices in a mesh: lat: 8 (over y_lo, z), lon: 16 (over x, y_hi, core).
Axes of the slice: x: 4, y: 4 (y_hi: 2, y_lo: 2; y = y_hi * 2 + y_lo), z: 4, core: 2. Of those that a mesh axis runs over, the one named last changes fastest.
Arguments:
- queries: bfloat16 [2, 384, 384, 512], P(None, 'lat', 'lon'), may hold values from -160 to 160
- key_tokens: bfloat16 [2, 384, 384, 512], P(None, 'lat', 'lon'), may hold values from -6 to 6
- value_tokens: bfloat16 [2, 384, 384, 512], P(None, 'lat', 'lon'), may hold values from -6 to 6
- out_grad: bfloat16 [2, 384, 384, 512], P(None, 'lat', 'lon'), may hold values from -6 to 6
- land_mask: int32 [384, 384], P('lat', 'lon'), may hold values 0 or 1
- land_embed: float32 [512], replicated, may hold values from -4 to 4
- rel_table: float32 [8, 759], replicated, may hold values from -4 to 4
Outputs:
- attended: bfloat16 [2, 384, 384, 512], P(None, 'lat', 'lon')
- grad_queries: bfloat16 [2, 384, 384, 512], P(None, 'lat', 'lon')
- grad_keys: bfloat16 [2, 384, 384, 512], P(None, 'lat', 'lon')
- grad_values: bfloat16 [2, 384, 384, 512], P(None, 'lat', 'lon')
The draws below stay inside these ranges and needn't reach their ends.
All inputs are finite; a program needn't handle non-finite values. No bound on the sum of `land_mask` on one device may be relied on, other than what follows from the above.
Results may differ from the reference program's by a relative error of at most 0.034.
The reference program's roundings to bfloat16 on the way (of `keyed`, `probs_low` and `grad_scores`) count: a program that leaves them out, or rounds other values in their place, can miss the bound.
Values may be sent and summed in bfloat16 or wider, within the bound.
A program may use at most 256 MiB of HBM per device.

```python
import jax
import jax.numpy as jnp
import numpy as np
from jax import lax

D = 512
HEADS = 8
LEV = 2
TABLE = 759
LATS = 384
LONS = 384


def common_normal(key):
    return jnp.clip(jax.random.normal(key, (LEV, LATS, LONS, D), jnp.float32), -6.0, 6.0)


def draw_key_tokens(key, part):
    shared = common_normal(key)
    return shared.astype(jnp.bfloat16)


def draw_queries(key, part):
    key = jax.random.fold_in(key, 12)
    shape = (LEV, LATS, LONS, D)
    return jnp.clip(jax.random.normal(key, shape, jnp.float32), -6.0, 6.0).astype(jnp.bfloat16)


def with_ends(values, stream_key, least, high):
    place = [jax.random.randint(jax.random.fold_in(stream_key, axis), (), 0, length) for axis, length in enumerate(values.shape)]
    widest = values.shape.index(max(values.shape))
    next_to = place[:widest] + [(place[widest] + 1) % values.shape[widest]] + place[widest + 1:]
    return values.at[tuple(place)].set(least).at[tuple(next_to)].set(high)


def block_scale(stream_key, shape, pieces, smallest, largest):
    level = 1.0
    for position, parts in pieces:
        steps = jax.random.uniform(jax.random.fold_in(jax.random.fold_in(stream_key, 6), position), (parts,), jnp.float32, smallest / len(pieces), largest / len(pieces))
        level = level * jnp.repeat(jnp.exp(steps), shape[position] // parts).reshape((-1,) + (1,) * (len(shape) - 1 - position))
    return level


def noise(key, extent, scale, bound, pieces=(), dtype=jnp.bfloat16):
    factor_of = block_scale(key, extent, pieces, -0.22, 0.18) if pieces else 1.0
    values = jax.random.normal(key, extent, jnp.float32) * scale * factor_of
    return jnp.minimum(jnp.maximum(values, -bound), bound).astype(dtype)


def setup_inputs(seed: int = 0) -> dict:
    key_of = jax.random.split(jax.random.key(seed), 8)
    queries = draw_queries(jax.random.fold_in(key_of[7], 71), 0)
    key_tokens = draw_key_tokens(jax.random.fold_in(key_of[7], 71), 0)
    value_tokens = noise(key_of[2], (LEV, LATS, LONS, D), 1.0, 6.0, ((1, 8), (2, 16)))
    out_grad = noise(key_of[3], (LEV, LATS, LONS, D), 1.0, 6.0, ((1, 8), (2, 16)))
    land_mask = with_ends((jax.random.randint(key_of[4], (LATS, LONS), 0, 3) < 1).astype(jnp.int32), jax.random.fold_in(key_of[4], 1), 0, 1)
    land_embed = noise(key_of[5], (D,), 1.0, 4.0, (), jnp.float32)
    rel_table = noise(key_of[6], (HEADS, TABLE), 1.0, 4.0, (), jnp.float32)
    return dict(queries=queries, key_tokens=key_tokens, value_tokens=value_tokens, out_grad=out_grad, land_mask=land_mask, land_embed=land_embed, rel_table=rel_table)


def index_table():
    pos = np.arange(144)
    level = pos // 72
    row = (pos // 12) % 6
    col = pos % 12
    return ((level[:, None] - level[None, :] + 1) * 11 + row[:, None] - row[None, :] + 5) * 23 + col[:, None] - col[None, :] + 11


def attend(query, keyed, valued, grad_out, bias, keep):
    count, tokens, width = query.shape
    heads = bias.shape[0]
    size = width // heads
    scale = float(size) ** -0.5
    q_heads = query.astype(jnp.float32).reshape(count, tokens, heads, size)
    k_heads = keyed.astype(jnp.float32).reshape(count, tokens, heads, size)
    v_heads = valued.astype(jnp.float32).reshape(count, tokens, heads, size)
    g_heads = grad_out.astype(jnp.float32).reshape(count, tokens, heads, size)
    scores = jnp.einsum('wihc,wjhc->whij', q_heads, k_heads) * scale + bias[None]
    scores = jnp.where(keep[None, None], scores, -jnp.inf)
    peak = jnp.max(scores, axis=-1, keepdims=True)
    expo = jnp.exp(scores - peak)
    probs = expo / jnp.sum(expo, axis=-1, keepdims=True)
    probs_low = lax.optimization_barrier(probs.astype(jnp.bfloat16)).astype(jnp.float32)
    attended = jnp.einsum('whij,wjhc->wihc', probs_low, v_heads).astype(jnp.bfloat16)
    attended_f = lax.optimization_barrier(attended).astype(jnp.float32)
    grad_probs = jnp.einsum('wihc,wjhc->whij', g_heads, v_heads)
    delta = jnp.einsum('wihc,wihc->whi', g_heads, attended_f)
    grad_scores = lax.optimization_barrier((probs * (grad_probs - delta[..., None])).astype(jnp.bfloat16)).astype(jnp.float32)
    grad_query = (jnp.einsum('whij,wjhc->wihc', grad_scores, k_heads) * scale).astype(jnp.bfloat16)
    grad_key = (jnp.einsum('whij,wihc->wjhc', grad_scores, q_heads) * scale).astype(jnp.bfloat16)
    grad_value = jnp.einsum('whij,wihc->wjhc', probs_low, g_heads).astype(jnp.bfloat16)
    result = jnp.stack([attended, grad_query, grad_key, grad_value], 1)
    return result.reshape(count, 4, tokens, width)


def reference(queries, key_tokens, value_tokens, out_grad, land_mask, land_embed, rel_table):
    lev, rows, cols, width = queries.shape
    keyed = (key_tokens.astype(jnp.float32) + land_mask.astype(jnp.float32)[None, :, :, None] * land_embed).astype(jnp.bfloat16)
    stacked = jnp.stack([queries, keyed, value_tokens, out_grad])
    rolled = jnp.roll(stacked, (-3, -6), axis=(2, 3))
    bias = rel_table[:, index_table()]
    groups = cols // 12
    bands = rows // 6
    row_of = (np.arange(72 * lev) // 12) % 6

    def one_band(index):
        band = lax.dynamic_slice_in_dim(rolled, index * 6, 6, axis=2)
        band = band.reshape(4, lev, 6, groups, 12, width).transpose(3, 0, 1, 2, 4, 5).reshape(groups, 4, lev * 72, width)
        global_row = index * 6 + row_of
        region = global_row >= rows - 3
        keep = region[:, None] == region[None, :]
        result = attend(band[:, 0], band[:, 1], band[:, 2], band[:, 3], bias, keep)
        return result.reshape(groups, 4, lev, 6, 12, width).transpose(1, 2, 3, 0, 4, 5).reshape(4, lev, 6, cols, width)

    outputs = lax.map(one_band, jnp.arange(bands))
    outputs = outputs.transpose(1, 2, 0, 3, 4, 5).reshape(4, lev, rows, cols, width)
    final = jnp.roll(outputs, (3, 6), axis=(2, 3))
    return final[0], final[1], final[2], final[3]
```

```python
import functools

import jax
import jax.numpy as jnp
import numpy as np
from jax import lax
from jax.experimental import pallas as pl
from jax.experimental.pallas import tpu as pltpu
from jax.sharding import PartitionSpec as P

F32 = jnp.float32
BF16 = jnp.bfloat16
HALF = 36
STRIP = 72
WIN = 144
GROUP = 256
MIB = 1 << 20


def strip_matrix(strips):
    out = np.zeros((len(strips), 2, 2, 3, 6, 2, 2, 3, 24), np.float32)
    for place, strip in enumerate(strips):
        for part in range(2):
            for lev in range(2):
                for row in range(3):
                    for col in range(6):
                        out[place, part, lev, row, col, part, lev, row, 6 * strip + col] = 1
    return out.reshape(len(strips) * STRIP, 2 * WIN)


def window_place(first_is_left):
    pos = np.arange(WIN)
    first = (pos // STRIP) == 0
    inside = pos % STRIP
    part = inside // HALF
    lev = (inside % HALF) // 18
    row = (inside % 18) // 6 + 3 * (1 - part)
    col = inside % 6 + 6 * np.where(first == first_is_left, 0, 1)
    return lev, row, col, part


def dot(a, b, ca=1, cb=0):
    return lax.dot_general(a, b, (((ca,), (cb,)), ((), ())), preferred_element_type=F32)


def keyed_rows(key, mask, embed):
    wide = jnp.concatenate([mask] * 4, axis=1)
    return (key + (wide * embed)[None]).astype(BF16).astype(F32)


def pack_body(sizes, q0, q1, k0, k1, v0, v1, g0, g1, m0, m1, embed, perm, *outs):
    def natural(first, second):
        return jnp.concatenate(
            [first[0], first[1], second[0], second[1]], axis=0
        ).astype(BF16)

    pairs = ((q0, q1), (k0, k1), (v0, v1), (g0, g1))
    for index, (first, second) in enumerate(pairs):
        first = first[:, 0].astype(F32)
        second = second[:, 0].astype(F32)
        if index == 1:
            first = keyed_rows(first, m0[0], embed[...])
            second = keyed_rows(second, m1[0], embed[...])
        packed = dot(perm[...], natural(first, second))
        if index == 0:
            packed = packed * 0.125
        start = 0
        for out, size in zip(outs, sizes):
            out[0, index] = packed[start : start + size].astype(BF16)
            start += size


def pack(arrays, mask, embed, perm, sizes):
    block = (2, 1, STRIP, 512)
    opening = pl.BlockSpec(block, lambda b: (0, 2 * b, 0, 0))
    closing = pl.BlockSpec(block, lambda b: (0, (2 * b + 15) % 16, 0, 0))
    mask_opening = pl.BlockSpec((1, STRIP, 128), lambda b: (2 * b, 0, 0))
    mask_closing = pl.BlockSpec((1, STRIP, 128), lambda b: ((2 * b + 15) % 16, 0, 0))
    operands, specs = [], []
    for array in arrays:
        operands += [array, array]
        specs += [opening, closing]
    total = sum(sizes)
    return pl.pallas_call(
        functools.partial(pack_body, sizes),
        grid=(8,),
        in_specs=specs
        + [
            mask_opening,
            mask_closing,
            pl.BlockSpec((1, 512), lambda b: (0, 0)),
            pl.BlockSpec(perm.shape, lambda b: (0, 0)),
        ],
        out_specs=[pl.BlockSpec((1, 4, size, 512), lambda b: (b, 0, 0, 0)) for size in sizes],
        out_shape=[jax.ShapeDtypeStruct((8, 4, size, 512), BF16) for size in sizes],
        compiler_params=pltpu.CompilerParams(vmem_limit_bytes=32 * MIB),
        cost_estimate=pl.CostEstimate(
            flops=2 * 8 * 4 * total * 288 * 512,
            bytes_accessed=8 * 4 * (288 + total) * 1024,
            transcendentals=0,
        ),
        name="pack_strips",
    )(*operands, mask, mask, embed, perm)


def pack_halo_body(sizes, below, above, perm, *outs):
    for index in range(4):
        first = below[index].astype(F32)
        second = above[index].astype(F32)
        tokens = jnp.concatenate([first[0], first[1], second[0], second[1]], axis=0)
        packed = dot(perm[...], tokens.astype(BF16))
        if index == 0:
            packed = packed * 0.125
        start = 0
        for out, size in zip(outs, sizes):
            out[index] = packed[start : start + size].astype(BF16)
            start += size


def pack_halo(below, above, perm, sizes):
    return pl.pallas_call(
        functools.partial(pack_halo_body, sizes),
        out_shape=[jax.ShapeDtypeStruct((4, size, 512), BF16) for size in sizes],
        compiler_params=pltpu.CompilerParams(vmem_limit_bytes=32 * MIB),
        cost_estimate=pl.CostEstimate(
            flops=2 * 4 * 288 * 288 * 512, bytes_accessed=4 * 2 * 288 * 1024, transcendentals=0
        ),
        name="pack_halo",
    )(below, above, perm)


def window(win, slot, bias, scores, grads, low, dlow, store):
    lane = lax.broadcasted_iota(jnp.int32, (1, GROUP), 1) // 64
    for group in range(2):
        cols = slice(GROUP * group, GROUP * (group + 1))
        q, k, v, g = (win[slot, index, :, cols] for index in range(4))

        def spread(x):
            return jnp.concatenate(
                [x * jnp.where(lane == h, 1.0, 0.0).astype(BF16) for h in range(4)], axis=0
            )

        q_wide, g_wide = spread(q), spread(g)
        scores[...] = dot(k, q_wide, 1, 1)
        grads[...] = dot(v, g_wide, 1, 1)
        for start in range(0, 576, 128):
            part = slice(start, min(start + 128, 576))
            s = scores[:, part] + bias[0, group, :, part]
            e = jnp.exp(s - jnp.max(s, axis=0, keepdims=True))
            p = e * (1.0 / jnp.sum(e, axis=0, keepdims=True))
            gp = grads[:, part]
            delta = jnp.sum(p * gp, axis=0, keepdims=True)
            low[:, part] = p.astype(BF16)
            dlow[:, part] = (p * (gp - delta)).astype(BF16)
        p_low, d_low = low[...], dlow[...]

        def by_head(wide):
            total = None
            for h in range(4):
                piece = jnp.where(lane == h, wide[WIN * h : WIN * (h + 1)], 0.0)
                total = piece if total is None else total + piece
            return total

        store(0, cols, by_head(dot(p_low, v, 0, 0)))
        store(1, cols, by_head(dot(d_low, k, 0, 0)) * 0.125)
        store(2, cols, dot(d_low, q_wide))
        store(3, cols, dot(p_low, g_wide))


def step_band(t):
    return jnp.where(t < 14, 1 + t // 2, 0)


def row_block(t):
    return jnp.where(t < 14, 2 * (1 + t // 2) - t % 2, jnp.where(t == 14, 0, 15))


def bias_pick(t):
    return jnp.maximum(t - 13, 0)


def place(win, slot, rows, own, other, t):
    count = own.shape[2]

    @pl.when(t < 14)
    def _():
        for index in range(4):
            win[slot, index, rows] = own[0, index]

    @pl.when(t >= 14)
    def _():
        pos = lax.broadcasted_iota(jnp.int32, (count, 1), 0) % STRIP
        keep = (pos < HALF) == (t == 14)
        for index in range(4):
            mixed = jnp.where(keep, own[0, index].astype(F32), other[index].astype(F32))
            win[slot, index, rows] = mixed.astype(BF16)


def place_pair(win, slot, own, own_other, halo, halo_other, t):
    @pl.when(t < 14)
    def _():
        for index in range(4):
            both = jnp.concatenate(
                [own[0, index].astype(F32), halo[0, index].astype(F32)], axis=0
            )
            win[slot, index] = both.astype(BF16)

    @pl.when(t >= 14)
    def _():
        pos = lax.broadcasted_iota(jnp.int32, (WIN, 1), 0) % STRIP
        keep = (pos < HALF) == (t == 14)
        for index in range(4):
            both = jnp.concatenate(
                [own[0, index].astype(F32), halo[0, index].astype(F32)], axis=0
            )
            other = jnp.concatenate(
                [own_other[index].astype(F32), halo_other[index].astype(F32)], axis=0
            )
            win[slot, index] = jnp.where(keep, both, other).astype(BF16)


def computes(t):
    return (t % 2 == 0) | (t >= 14)


def inner_body(mid, mid_o, own, own_o, halo, halo_o, bias, back, out, win, result, scores, grads, low, dlow):
    t = pl.program_id(0)

    @pl.when(computes(t))
    def _():
        place(win, 0, slice(0, WIN), mid, mid_o, t)
        place_pair(win, 1, own, own_o, halo, halo_o, t)

        def keep_mid(index, cols, value):
            result[index, 80:224, cols] = value.astype(BF16)

        def keep_own(index, cols, value):
            result[index, 0:80, cols] = value[:80].astype(BF16)

        window(win, 0, bias, scores, grads, low, dlow, keep_mid)
        window(win, 1, bias, scores, grads, low, dlow, keep_own)

    for index in range(4):
        out[0, index] = dot(back[0], result[index]).astype(BF16)


def outer_body(partial, own, own_o, halo, halo_o, bias, back, o0, o1, o2, o3, win, result, scores, grads, low, dlow):
    t = pl.program_id(0)

    @pl.when(computes(t))
    def _():
        place_pair(win, 0, own, own_o, halo, halo_o, t)

        def keep(index, cols, value):
            result[index, :, cols] = value[:80].astype(BF16)

        window(win, 0, bias, scores, grads, low, dlow, keep)

    for index, out in enumerate((o0, o1, o2, o3)):
        full = dot(back[0], result[index]) + partial[0, index].astype(F32)
        out[0, 0] = full[:STRIP].astype(BF16)
        out[1, 0] = full[STRIP:].astype(BF16)


def band_spec(size):
    return pl.BlockSpec((1, 4, size, 512), lambda t: (step_band(t), 0, 0, 0))


def fixed_spec(size):
    return pl.BlockSpec((4, size, 512), lambda t: (0, 0, 0))


BIAS_SPEC = pl.BlockSpec((1, 2, WIN, 576), lambda t: (bias_pick(t), 0, 0, 0))


def back_spec(width):
    def pick(t):
        opening = jnp.where(t < 14, t % 2 == 0, t == 14)
        return (jnp.where(opening, 0, 1), 0, 0)

    return pl.BlockSpec((1, WIN, width), pick)


def work_scratch():
    return [
        pltpu.VMEM((WIN, 576), F32),
        pltpu.VMEM((WIN, 576), F32),
        pltpu.VMEM((WIN, 576), BF16),
        pltpu.VMEM((WIN, 576), BF16),
    ]


def window_cost(windows, moved):
    return pl.CostEstimate(
        flops=windows * 6 * 2 * WIN * WIN * 512 * 4,
        bytes_accessed=moved,
        transcendentals=windows * 8 * WIN * WIN,
    )


def inner(mid, mid_o, own, own_o, halo, halo_o, bias, back):
    return pl.pallas_call(
        inner_body,
        grid=(16,),
        in_specs=[
            band_spec(WIN),
            fixed_spec(WIN),
            band_spec(STRIP),
            fixed_spec(STRIP),
            band_spec(STRIP),
            fixed_spec(STRIP),
            BIAS_SPEC,
            back_spec(224),
        ],
        out_specs=pl.BlockSpec((1, 4, WIN, 512), lambda t: (row_block(t), 0, 0, 0)),
        out_shape=jax.ShapeDtypeStruct((16, 4, WIN, 512), BF16),
        scratch_shapes=[pltpu.VMEM((2, 4, WIN, 512), BF16), pltpu.VMEM((4, 224, 512), BF16)]
        + work_scratch(),
        compiler_params=pltpu.CompilerParams(vmem_limit_bytes=48 * MIB),
        cost_estimate=window_cost(18, 20 * MIB),
        name="inner_windows",
    )(mid, mid_o, own, own_o, halo, halo_o, bias, back)


def outer(partial, own, own_o, halo, halo_o, bias, back):
    out = pl.BlockSpec((2, 1, STRIP, 512), lambda t: (0, row_block(t), 0, 0))
    return pl.pallas_call(
        outer_body,
        grid=(16,),
        in_specs=[
            pl.BlockSpec((1, 4, WIN, 512), lambda t: (row_block(t), 0, 0, 0)),
            band_spec(STRIP),
            fixed_spec(STRIP),
            band_spec(STRIP),
            fixed_spec(STRIP),
            BIAS_SPEC,
            back_spec(80),
        ],
        out_specs=[out] * 4,
        out_shape=[jax.ShapeDtypeStruct((2, 16, STRIP, 512), BF16)] * 4,
        scratch_shapes=[pltpu.VMEM((1, 4, WIN, 512), BF16), pltpu.VMEM((4, 80, 512), BF16)]
        + work_scratch(),
        compiler_params=pltpu.CompilerParams(vmem_limit_bytes=48 * MIB),
        cost_estimate=window_cost(9, 24 * MIB),
        name="outer_windows",
    )(partial, own, own_o, halo, halo_o, bias, back)


def difference_hot(pos, count, offset):
    diff = pos[None, :] - pos[:, None] + offset
    return (np.arange(count)[:, None, None] == diff[None]).astype(np.float32)


def transposed_bias(rel_table, sign):
    best = lax.Precision.HIGHEST
    table = rel_table.reshape(8, 3, 11, 23)
    col = np.arange(12)
    left = difference_hot(col, 23, 11)
    right = difference_hot((col + 6) % 12, 23, 11)
    cols = jnp.where(sign > 0, left, right)
    rows = difference_hot(np.array([3, 4, 5, 0, 1, 2]), 11, 5)
    levs = difference_hot(np.arange(2), 3, 1)
    first = jnp.einsum("hxyz,zab->hxyab", table, cols, precision=best)
    second = jnp.einsum("hxyab,ycd->hxcdab", first, rows, precision=best)
    third = jnp.einsum("hxcdab,xef->hefcdab", second, levs, precision=best)
    wide = third.reshape(2, 4, 2, 2, 2, 3, 2, 3, 2, 6, 2, 6)
    wide = wide.transpose(0, 8, 4, 2, 5, 9, 1, 10, 6, 3, 7, 11)
    return wide.reshape(2, WIN, 576)


def with_regions(bias, top, bottom):
    part = (np.arange(WIN) % STRIP) // HALF
    differ = np.tile(part[:, None] != part[None, :], (1, 4))[None]
    cut = jnp.where(differ, -jnp.inf, bias)
    return jnp.stack([bias, jnp.where(top, cut, bias), jnp.where(bottom, cut, bias)])


def shards(queries, key_tokens, value_tokens, out_grad, land_mask, land_embed, rel_table):
    lev, rows, cols, width = queries.shape
    lat, core = lax.axis_index("lat"), lax.axis_index("lon") % 2
    bands = lax.axis_size("lat")
    sectors = lax.axis_size("lon")
    shape = (lev, rows // 3, STRIP, width)
    arrays = [x.reshape(shape) for x in (queries, key_tokens, value_tokens, out_grad)]
    mask = jnp.broadcast_to(
        land_mask.astype(F32).reshape(rows // 3, STRIP, 1), (rows // 3, STRIP, 128)
    )
    embed = land_embed.reshape(1, width)

    far = np.stack([strip_matrix([0]), strip_matrix([3])])
    near = np.stack([strip_matrix([3, 1, 2]), strip_matrix([0, 2, 1])])
    far_perm = jnp.asarray(far, BF16)[core]
    near_perm = jnp.asarray(near, BF16)[core]
    all_perm = jnp.concatenate([far_perm, near_perm], axis=0)
    far_back = np.zeros((2, 2, WIN, 80), np.float32)
    near_back = np.zeros((2, 2, WIN, 224), np.float32)
    for side in range(2):
        for part in range(2):
            span = slice(WIN * part, WIN * (part + 1))
            far_back[side, part, :, :STRIP] = far[side].T[span]
            near_back[side, part, :, :STRIP] = near[side].T[span, :STRIP]
            near_back[side, part, :, 80:] = near[side].T[span, STRIP:]
    far_back = jnp.asarray(far_back, BF16)[core]
    near_back = jnp.asarray(near_back, BF16)[core]

    to_far = [((2 * k + 1) % sectors, (2 * k + 2) % sectors) for k in range(sectors // 2)]
    to_far += [(b, a) for a, b in to_far]
    to_near = [(i, i ^ 1) for i in range(sectors)]

    (far_own,) = pack(arrays, mask, embed, far_perm, (STRIP,))
    far_halo = lax.ppermute(far_own, "lon", to_far)

    def edge(block):
        keyed = (
            arrays[1][:, block].astype(F32) + mask[block, :, :1] * embed
        ).astype(BF16)
        return jnp.stack([arrays[0][:, block], keyed, arrays[2][:, block], arrays[3][:, block]])

    below = lax.ppermute(edge(0), "lat", [(i, i - 1) for i in range(1, bands)])
    above = lax.ppermute(edge(rows // 3 - 1), "lat", [(i, i + 1) for i in range(bands - 1)])

    near_own, mid = pack(arrays, mask, embed, near_perm, (STRIP, WIN))
    near_halo = lax.ppermute(near_own, "lon", to_near)

    far_own_o, near_own_o, mid_o = pack_halo(below, above, all_perm, (STRIP, STRIP, WIN))
    far_halo_o = lax.ppermute(far_own_o, "lon", to_far)
    near_halo_o = lax.ppermute(near_own_o, "lon", to_near)

    sign = 1 - 2 * core
    top, bottom = lat == 0, lat == bands - 1
    near_bias = with_regions(transposed_bias(rel_table, sign), top, bottom)
    far_bias = with_regions(transposed_bias(rel_table, -sign), top, bottom)

    partial = inner(mid, mid_o, near_own, near_own_o, near_halo, near_halo_o, near_bias, near_back)
    final = outer(partial, far_own, far_own_o, far_halo, far_halo_o, far_bias, far_back)
    return tuple(x.reshape(queries.shape) for x in final)


def solution(mesh):
    tokens = P(None, "lat", "lon", None)
    return jax.shard_map(
        shards,
        mesh=mesh,
        in_specs=(tokens, tokens, tokens, tokens, P("lat", "lon"), P(), P()),
        out_specs=(tokens,) * 4,
        check_vma=False,
    )
```

```python
import functools

import jax
import jax.numpy as jnp
import numpy as np
from jax import lax
from jax.experimental import pallas as pl
from jax.experimental.pallas import tpu as pltpu
from jax.sharding import PartitionSpec as P

F32 = jnp.float32
BF16 = jnp.bfloat16
HALF = 36
STRIP = 72
WIN = 144
GROUP = 256
MIB = 1 << 20
VMEM_BYTES = 60 * MIB


def strip_matrix(strips):
    out = np.zeros((len(strips), 2, 2, 3, 6, 2, 2, 3, 24), np.float32)
    for place, strip in enumerate(strips):
        for part in range(2):
            for lev in range(2):
                for row in range(3):
                    for col in range(6):
                        out[place, part, lev, row, col, part, lev, row, 6 * strip + col] = 1
    return out.reshape(len(strips) * STRIP, 2 * WIN)


def far_matrix(strip, tile):
    full = strip_matrix([strip]).reshape(STRIP, 2, 2, 3, 3, 8)
    return full[:, :, :, :, tile].reshape(STRIP, 96)


def run_bases():
    run = np.arange(24)
    half, part, lev, row = run // 12, run // 6 % 2, run // 3 % 2, run % 3
    return lev * 253 + (row + 3 * (1 - part)) * 23 + 6 * half


def dot(a, b, ca=1, cb=0):
    return lax.dot_general(a, b, (((ca,), (cb,)), ((), ())), preferred_element_type=F32)


def keyed_rows(key, mask, embed):
    wide = jnp.concatenate([mask] * 4, axis=-1)
    return (key + (wide * embed)[None]).astype(BF16).astype(F32)


def far_body(tile, q0, q1, k0, k1, v0, v1, g0, g1, m0, m1, embed, perm, out):
    pairs = ((q0, q1), (k0, k1), (v0, v1), (g0, g1))
    for index, (first, second) in enumerate(pairs):
        first = first[:, :, 0].astype(F32)
        second = second[:, :, 0].astype(F32)
        if index == 1:
            first = keyed_rows(first, m0[:, 0], embed[...])
            second = keyed_rows(second, m1[:, 0], embed[...])
        tokens = jnp.concatenate([first.reshape(48, 512), second.reshape(48, 512)], axis=0)
        packed = dot(perm[...], tokens.astype(BF16))
        if index == 0:
            packed = packed * 0.125
        out[0, index] = packed.astype(BF16)


def pack_far(arrays, mask, embed, perm, tile):
    block = (2, 3, 1, 8, 512)
    opening = pl.BlockSpec(block, lambda b, tile: (0, 2 * b, tile[0], 0, 0))
    closing = pl.BlockSpec(block, lambda b, tile: (0, (2 * b + 15) % 16, tile[0], 0, 0))
    mask_block = (3, 1, 8, 128)
    mask_opening = pl.BlockSpec(mask_block, lambda b, tile: (2 * b, tile[0], 0, 0))
    mask_closing = pl.BlockSpec(mask_block, lambda b, tile: ((2 * b + 15) % 16, tile[0], 0, 0))
    operands, specs = [], []
    for array in arrays:
        array = array.reshape(2, 48, 3, 8, 512)
        operands += [array, array]
        specs += [opening, closing]
    mask = mask.reshape(48, 3, 8, 128)
    return pl.pallas_call(
        far_body,
        grid_spec=pltpu.PrefetchScalarGridSpec(
            num_scalar_prefetch=1,
            grid=(8,),
            in_specs=specs
            + [
                mask_opening,
                mask_closing,
                pl.BlockSpec((1, 512), lambda b, tile: (0, 0)),
                pl.BlockSpec(perm.shape, lambda b, tile: (0, 0)),
            ],
            out_specs=pl.BlockSpec((1, 4, STRIP, 512), lambda b, tile: (b, 0, 0, 0)),
        ),
        out_shape=jax.ShapeDtypeStruct((8, 4, STRIP, 512), BF16),
        compiler_params=pltpu.CompilerParams(vmem_limit_bytes=VMEM_BYTES),
        cost_estimate=pl.CostEstimate(
            flops=2 * 8 * 4 * STRIP * 96 * 512,
            bytes_accessed=8 * 4 * (96 + STRIP) * 1024,
            transcendentals=0,
        ),
        name="pack_far",
    )(tile, *operands, mask, mask, embed, perm)


def pack_body(sizes, q0, q1, k0, k1, v0, v1, g0, g1, m0, m1, embed, perm, *outs):
    def natural(first, second):
        return jnp.concatenate(
            [first[0], first[1], second[0], second[1]], axis=0
        ).astype(BF16)

    pairs = ((q0, q1), (k0, k1), (v0, v1), (g0, g1))
    for index, (first, second) in enumerate(pairs):
        first = first[:, 0].astype(F32)
        second = second[:, 0].astype(F32)
        if index == 1:
            first = keyed_rows(first, m0[0], embed[...])
            second = keyed_rows(second, m1[0], embed[...])
        packed = dot(perm[...], natural(first, second))
        if index == 0:
            packed = packed * 0.125
        start = 0
        for out, size in zip(outs, sizes):
            out[0, index] = packed[start : start + size].astype(BF16)
            start += size


def pack(arrays, mask, embed, perm, sizes):
    block = (2, 1, STRIP, 512)
    opening = pl.BlockSpec(block, lambda b: (0, 2 * b, 0, 0))
    closing = pl.BlockSpec(block, lambda b: (0, (2 * b + 15) % 16, 0, 0))
    mask_opening = pl.BlockSpec((1, STRIP, 128), lambda b: (2 * b, 0, 0))
    mask_closing = pl.BlockSpec((1, STRIP, 128), lambda b: ((2 * b + 15) % 16, 0, 0))
    operands, specs = [], []
    for array in arrays:
        operands += [array, array]
        specs += [opening, closing]
    total = sum(sizes)
    return pl.pallas_call(
        functools.partial(pack_body, sizes),
        grid=(8,),
        in_specs=specs
        + [
            mask_opening,
            mask_closing,
            pl.BlockSpec((1, 512), lambda b: (0, 0)),
            pl.BlockSpec(perm.shape, lambda b: (0, 0)),
        ],
        out_specs=[pl.BlockSpec((1, 4, size, 512), lambda b: (b, 0, 0, 0)) for size in sizes],
        out_shape=[jax.ShapeDtypeStruct((8, 4, size, 512), BF16) for size in sizes],
        compiler_params=pltpu.CompilerParams(vmem_limit_bytes=VMEM_BYTES),
        cost_estimate=pl.CostEstimate(
            flops=2 * 8 * 4 * total * 288 * 512,
            bytes_accessed=8 * 4 * (288 + total) * 1024,
            transcendentals=0,
        ),
        name="pack_strips",
    )(*operands, mask, mask, embed, perm)


def pack_halo_body(sizes, below, above, perm, *outs):
    for index in range(4):
        first = below[index].astype(F32)
        second = above[index].astype(F32)
        tokens = jnp.concatenate([first[0], first[1], second[0], second[1]], axis=0)
        packed = dot(perm[...], tokens.astype(BF16))
        if index == 0:
            packed = packed * 0.125
        start = 0
        for out, size in zip(outs, sizes):
            out[index] = packed[start : start + size].astype(BF16)
            start += size


def pack_halo(below, above, perm, sizes):
    return pl.pallas_call(
        functools.partial(pack_halo_body, sizes),
        out_shape=[jax.ShapeDtypeStruct((4, size, 512), BF16) for size in sizes],
        compiler_params=pltpu.CompilerParams(vmem_limit_bytes=VMEM_BYTES),
        cost_estimate=pl.CostEstimate(
            flops=2 * 4 * 288 * 288 * 512, bytes_accessed=4 * 2 * 288 * 1024, transcendentals=0
        ),
        name="pack_halo",
    )(below, above, perm)


def window(win, slot, bias, scores, grads, low, dlow, store):
    lane = lax.broadcasted_iota(jnp.int32, (1, GROUP), 1) // 64
    for group in range(2):
        cols = slice(GROUP * group, GROUP * (group + 1))
        q, k, v, g = (win[slot, index, :, cols] for index in range(4))

        def spread(x):
            return jnp.concatenate(
                [x * jnp.where(lane == h, 1.0, 0.0).astype(BF16) for h in range(4)], axis=0
            )

        q_wide, g_wide = spread(q), spread(g)
        scores[...] = dot(k, q_wide, 1, 1)
        grads[...] = dot(v, g_wide, 1, 1)
        for start in range(0, 576, 128):
            part = slice(start, min(start + 128, 576))
            s = scores[:, part] + bias[0, group, :, part]
            e = jnp.exp(s - jnp.max(s, axis=0, keepdims=True))
            p = e * (1.0 / jnp.sum(e, axis=0, keepdims=True))
            gp = grads[:, part]
            delta = jnp.sum(p * gp, axis=0, keepdims=True)
            low[:, part] = p.astype(BF16)
            dlow[:, part] = (p * (gp - delta)).astype(BF16)
        p_low, d_low = low[...], dlow[...]

        def by_head(wide):
            total = None
            for h in range(4):
                piece = jnp.where(lane == h, wide[WIN * h : WIN * (h + 1)], 0.0)
                total = piece if total is None else total + piece
            return total

        store(0, cols, by_head(dot(p_low, v, 0, 0)))
        store(1, cols, by_head(dot(d_low, k, 0, 0)) * 0.125)
        store(2, cols, dot(d_low, q_wide))
        store(3, cols, dot(p_low, g_wide))


def step_band(t):
    return jnp.where(t < 14, 1 + t // 2, 0)


def row_block(t):
    return jnp.where(t < 14, 2 * (1 + t // 2) - t % 2, jnp.where(t == 14, 0, 15))


def bias_pick(t):
    return jnp.maximum(t - 13, 0)


def place(win, slot, rows, own, other, t):
    count = own.shape[2]

    @pl.when(t < 14)
    def _():
        for index in range(4):
            win[slot, index, rows] = own[0, index]

    @pl.when(t >= 14)
    def _():
        pos = lax.broadcasted_iota(jnp.int32, (count, 1), 0) % STRIP
        keep = (pos < HALF) == (t == 14)
        for index in range(4):
            mixed = jnp.where(keep, own[0, index].astype(F32), other[index].astype(F32))
            win[slot, index, rows] = mixed.astype(BF16)


def place_pair(win, slot, own, own_other, halo, halo_other, t, own_left):
    def both(first, second):
        return jnp.concatenate([first.astype(F32), second.astype(F32)], axis=0)

    def put(left, left_other, right, right_other):
        @pl.when(t < 14)
        def _():
            for index in range(4):
                win[slot, index] = both(left[0, index], right[0, index]).astype(BF16)

        @pl.when(t >= 14)
        def _():
            pos = lax.broadcasted_iota(jnp.int32, (WIN, 1), 0) % STRIP
            keep = (pos < HALF) == (t == 14)
            for index in range(4):
                here = both(left[0, index], right[0, index])
                there = both(left_other[index], right_other[index])
                win[slot, index] = jnp.where(keep, here, there).astype(BF16)

    @pl.when(own_left)
    def _():
        put(own, own_other, halo, halo_other)

    @pl.when(jnp.logical_not(own_left))
    def _():
        put(halo, halo_other, own, own_other)


def computes(t):
    return (t % 2 == 0) | (t >= 14)


def inner_body(mid, mid_o, own, own_o, halo, halo_o, bias, back, out, win, result, *work):
    t = pl.program_id(0)
    core = lax.axis_index("lon") % 2
    mid_at = pl.multiple_of(WIN * core, 16)
    own_at = pl.multiple_of(WIN * (1 - core), 16)

    @pl.when(computes(t))
    def _():
        place(win, 0, slice(0, WIN), mid, mid_o, t)
        place_pair(win, 1, own, own_o, halo, halo_o, t, core == 0)

        def keep_mid(index, cols, value):
            result[index, pl.ds(mid_at, WIN), cols] = value.astype(BF16)

        def keep_own(index, cols, value):
            result[index, pl.ds(own_at, WIN), cols] = value.astype(BF16)

        window(win, 0, bias, *work, keep_mid)
        window(win, 1, bias, *work, keep_own)

    used = pl.ds(pl.multiple_of(64 * core, 16), 224)
    for index in range(4):
        out[0, index] = dot(back[0], result[index, used]).astype(BF16)


def outer_body(partial, own, own_o, halo, halo_o, bias, back, o0, o1, o2, o3, win, result, *work):
    t = pl.program_id(0)
    core = lax.axis_index("lon") % 2

    @pl.when(computes(t))
    def _():
        place_pair(win, 0, own, own_o, halo, halo_o, t, core == 1)

        def keep(index, cols, value):
            result[index, :, cols] = value.astype(BF16)

        window(win, 0, bias, *work, keep)

    used = pl.ds(pl.multiple_of(64 * (1 - core), 16), 80)
    for index, out in enumerate((o0, o1, o2, o3)):
        full = dot(back[0], result[index, used]) + partial[0, index].astype(F32)
        out[0, 0] = full[:STRIP].astype(BF16)
        out[1, 0] = full[STRIP:].astype(BF16)


def band_spec(size):
    return pl.BlockSpec((1, 4, size, 512), lambda t: (step_band(t), 0, 0, 0))


def fixed_spec(size):
    return pl.BlockSpec((4, size, 512), lambda t: (0, 0, 0))


BIAS_SPEC = pl.BlockSpec((1, 2, WIN, 576), lambda t: (bias_pick(t), 0, 0, 0))


def back_spec(width):
    def pick(t):
        opening = jnp.where(t < 14, t % 2 == 0, t == 14)
        return (jnp.where(opening, 0, 1), 0, 0)

    return pl.BlockSpec((1, WIN, width), pick)


def work_scratch():
    return [
        pltpu.VMEM((WIN, 576), F32),
        pltpu.VMEM((WIN, 576), F32),
        pltpu.VMEM((WIN, 576), BF16),
        pltpu.VMEM((WIN, 576), BF16),
    ]


def window_cost(windows, moved):
    return pl.CostEstimate(
        flops=windows * 6 * 2 * WIN * WIN * 512 * 4,
        bytes_accessed=moved,
        transcendentals=windows * 8 * WIN * WIN,
    )


def inner(mid, mid_o, own, own_o, halo, halo_o, bias, back):
    return pl.pallas_call(
        inner_body,
        grid=(16,),
        in_specs=[
            band_spec(WIN),
            fixed_spec(WIN),
            band_spec(STRIP),
            fixed_spec(STRIP),
            band_spec(STRIP),
            fixed_spec(STRIP),
            BIAS_SPEC,
            back_spec(224),
        ],
        out_specs=pl.BlockSpec((1, 4, WIN, 512), lambda t: (row_block(t), 0, 0, 0)),
        out_shape=jax.ShapeDtypeStruct((16, 4, WIN, 512), BF16),
        scratch_shapes=[pltpu.VMEM((2, 4, WIN, 512), BF16), pltpu.VMEM((4, 2 * WIN, 512), BF16)]
        + work_scratch(),
        compiler_params=pltpu.CompilerParams(vmem_limit_bytes=VMEM_BYTES),
        cost_estimate=window_cost(18, 20 * MIB),
        name="inner_windows",
    )(mid, mid_o, own, own_o, halo, halo_o, bias, back)


def outer(partial, own, own_o, halo, halo_o, bias, back):
    out = pl.BlockSpec((2, 1, STRIP, 512), lambda t: (0, row_block(t), 0, 0))
    return pl.pallas_call(
        outer_body,
        grid=(16,),
        in_specs=[
            pl.BlockSpec((1, 4, WIN, 512), lambda t: (row_block(t), 0, 0, 0)),
            band_spec(STRIP),
            fixed_spec(STRIP),
            band_spec(STRIP),
            fixed_spec(STRIP),
            BIAS_SPEC,
            back_spec(80),
        ],
        out_specs=[out] * 4,
        out_shape=[jax.ShapeDtypeStruct((2, 16, STRIP, 512), BF16)] * 4,
        scratch_shapes=[pltpu.VMEM((1, 4, WIN, 512), BF16), pltpu.VMEM((4, WIN, 512), BF16)]
        + work_scratch(),
        compiler_params=pltpu.CompilerParams(vmem_limit_bytes=VMEM_BYTES),
        cost_estimate=window_cost(9, 24 * MIB),
        name="outer_windows",
    )(partial, own, own_o, halo, halo_o, bias, back)


def bias_body(flags, table, hot, squeeze, out, wide, part, whole):
    variant = pl.program_id(0)

    @pl.when(variant == 0)
    def _():
        for head in range(8):
            line = jnp.broadcast_to(table[head : head + 1], (8, 768))
            line = pltpu.roll(line, 0, 1, stride=1, stride_axis=0)
            for run, base in enumerate(run_bases()):
                turn = int(base - 379) % 768
                turned = pltpu.roll(line, turn, 1)
                wide[head // 4, 8 * run : 8 * run + 8, 384 * (head % 4) : 384 * (head % 4) + 384] = turned[:, :384]
        for group in range(2):
            total = None
            for _ in range(3):
                part[...] = wide[group].astype(BF16)
                wide[group] = wide[group] - part[...].astype(F32)
                spread = dot(part[...], hot[...]).astype(BF16)
                piece = dot(squeeze[...], spread)
                total = piece if total is None else total + piece
            whole[group] = total

    @pl.when((variant == 0) | (flags[variant] == 0))
    def _():
        out[0] = whole[...]

    @pl.when((variant > 0) & (flags[variant] != 0))
    def _():
        upper = lax.broadcasted_iota(jnp.int32, (WIN, 576), 0) % STRIP < HALF
        upper_i = lax.broadcasted_iota(jnp.int32, (WIN, 576), 1) % STRIP < HALF
        for group in range(2):
            out[0, group] = jnp.where(upper == upper_i, whole[group], -jnp.inf)


def window_bias(rel_table, flags):
    tokens = (run_bases()[:, None] + np.arange(6)).reshape(WIN)
    hot = np.zeros((4, 384, 4, WIN), np.float32)
    for head in range(4):
        hot[head, tokens, head, np.arange(WIN)] = 1
    squeeze = np.zeros((24, 6, 24, 8), np.float32)
    for run in range(24):
        squeeze[run, np.arange(6), run, np.arange(6)] = 1
    hot = jnp.asarray(hot.reshape(4 * 384, 4 * WIN), BF16)
    squeeze = jnp.asarray(squeeze.reshape(WIN, 192), BF16)
    table = jnp.pad(rel_table, ((0, 0), (0, 768 - rel_table.shape[1])))
    return pl.pallas_call(
        bias_body,
        grid_spec=pltpu.PrefetchScalarGridSpec(
            num_scalar_prefetch=1,
            grid=(3,),
            in_specs=[
                pl.BlockSpec((8, 768), lambda v, flags: (0, 0)),
                pl.BlockSpec((4 * 384, 576), lambda v, flags: (0, 0)),
                pl.BlockSpec((WIN, 192), lambda v, flags: (0, 0)),
            ],
            out_specs=pl.BlockSpec((1, 2, WIN, 576), lambda v, flags: (v, 0, 0, 0)),
            scratch_shapes=[
                pltpu.VMEM((2, 192, 4 * 384), F32),
                pltpu.VMEM((192, 4 * 384), BF16),
                pltpu.VMEM((2, WIN, 576), F32),
            ],
        ),
        out_shape=jax.ShapeDtypeStruct((3, 2, WIN, 576), F32),
        compiler_params=pltpu.CompilerParams(vmem_limit_bytes=VMEM_BYTES),
        cost_estimate=pl.CostEstimate(
            flops=6 * 2 * 192 * 1536 * 576, bytes_accessed=4 * MIB, transcendentals=0
        ),
        name="window_bias",
    )(flags, table, hot, squeeze)


def shards(queries, key_tokens, value_tokens, out_grad, land_mask, land_embed, rel_table):
    lev, rows, cols, width = queries.shape
    lat, core = lax.axis_index("lat"), lax.axis_index("lon") % 2
    bands = lax.axis_size("lat")
    sectors = lax.axis_size("lon")
    shape = (lev, rows // 3, STRIP, width)
    arrays = [x.reshape(shape) for x in (queries, key_tokens, value_tokens, out_grad)]
    mask = jnp.broadcast_to(
        land_mask.astype(F32).reshape(rows // 3, STRIP, 1), (rows // 3, STRIP, 128)
    )
    embed = land_embed.reshape(1, width)

    far = [strip_matrix([0]), strip_matrix([3])]
    near = [strip_matrix([3, 1, 2]), strip_matrix([0, 1, 2])]
    far_back = np.zeros((2, 2, WIN, 80), np.float32)
    near_back = np.zeros((2, 2, WIN, 224), np.float32)
    for side in range(2):
        for part in range(2):
            span = slice(WIN * part, WIN * (part + 1))
            own = near[side].T[span, :STRIP]
            mid_part = near[side].T[span, STRIP:]
            pad = np.zeros((WIN, 8), np.float32)
            far_own_part = far[side].T[span]
            if side == 0:
                near_back[side, part] = np.concatenate([mid_part, own, pad], axis=1)
                far_back[side, part] = np.concatenate([pad, far_own_part], axis=1)
            else:
                near_back[side, part] = np.concatenate([pad, own, mid_part], axis=1)
                far_back[side, part] = np.concatenate([far_own_part, pad], axis=1)
    far_tile = np.stack([far_matrix(0, 0), far_matrix(3, 2)])
    whole = np.stack([np.concatenate([far[side], near[side]]) for side in range(2)])
    far_perm = jnp.asarray(far_tile, BF16)[core]
    all_perm = jnp.asarray(whole, BF16)[core]
    near_perm = all_perm[STRIP:]
    far_back = jnp.asarray(far_back, BF16)[core]
    near_back = jnp.asarray(near_back, BF16)[core]

    to_far = [((2 * k + 1) % sectors, (2 * k + 2) % sectors) for k in range(sectors // 2)]
    to_far += [(b, a) for a, b in to_far]
    to_near = [(i, i ^ 1) for i in range(sectors)]

    far_own = pack_far(arrays, mask, embed, far_perm, jnp.reshape(2 * core, (1,)))
    far_halo = lax.ppermute(far_own, "lon", to_far)

    def edge(block):
        keyed = (
            arrays[1][:, block].astype(F32) + mask[block, :, :1] * embed
        ).astype(BF16)
        return jnp.stack([arrays[0][:, block], keyed, arrays[2][:, block], arrays[3][:, block]])

    below = lax.ppermute(edge(0), "lat", [(i, i - 1) for i in range(1, bands)])
    above = lax.ppermute(edge(rows // 3 - 1), "lat", [(i, i + 1) for i in range(bands - 1)])

    near_own, mid = pack(arrays, mask, embed, near_perm, (STRIP, WIN))
    near_halo = lax.ppermute(near_own, "lon", to_near)

    far_own_o, near_own_o, mid_o = pack_halo(below, above, all_perm, (STRIP, STRIP, WIN))
    far_halo_o = lax.ppermute(far_own_o, "lon", to_far)
    near_halo_o = lax.ppermute(near_own_o, "lon", to_near)

    flags = jnp.stack([0 * lat, lat == 0, lat == bands - 1]).astype(jnp.int32)
    bias = window_bias(rel_table, flags)

    partial = inner(mid, mid_o, near_own, near_own_o, near_halo, near_halo_o, bias, near_back)
    final = outer(partial, far_own, far_own_o, far_halo, far_halo_o, bias, far_back)
    return tuple(x.reshape(queries.shape) for x in final)


def solution(mesh):
    tokens = P(None, "lat", "lon", None)
    return jax.shard_map(
        shards,
        mesh=mesh,
        in_specs=(tokens, tokens, tokens, tokens, P("lat", "lon"), P(), P()),
        out_specs=(tokens,) * 4,
        check_vma=False,
    )
```

```python
import functools

import jax
import jax.numpy as jnp
import numpy as np
from jax import lax
from jax.experimental import pallas as pl
from jax.experimental.pallas import tpu as pltpu
from jax.sharding import PartitionSpec as P

F32 = jnp.float32
BF16 = jnp.bfloat16
HALF = 36
STRIP = 72
WIN = 144
GROUP = 256
MIB = 1 << 20
VMEM_BYTES = 60 * MIB


def strip_matrix(strips):
    out = np.zeros((len(strips), 2, 2, 3, 6, 2, 2, 3, 24), np.float32)
    for place, strip in enumerate(strips):
        for part in range(2):
            for lev in range(2):
                for row in range(3):
                    for col in range(6):
                        out[place, part, lev, row, col, part, lev, row, 6 * strip + col] = 1
    return out.reshape(len(strips) * STRIP, 2 * WIN)


def far_matrix(strip, tile):
    full = strip_matrix([strip]).reshape(STRIP, 2, 2, 3, 3, 8)
    return full[:, :, :, :, tile].reshape(STRIP, 96)


def run_bases():
    run = np.arange(24)
    half, part, lev, row = run // 12, run // 6 % 2, run // 3 % 2, run % 3
    return lev * 253 + (row + 3 * (1 - part)) * 23 + 6 * half


def dot(a, b, ca=1, cb=0):
    return lax.dot_general(a, b, (((ca,), (cb,)), ((), ())), preferred_element_type=F32)


def keyed_rows(key, mask, embed):
    wide = jnp.concatenate([mask] * 4, axis=-1)
    return (key + (wide * embed)[None]).astype(BF16).astype(F32)


def side_spec(shape):
    return pl.BlockSpec((1, *shape), lambda s, core: (core[0],) + (0,) * len(shape))


def fixed_spec(shape):
    return pl.BlockSpec(shape, lambda s, core: (0,) * len(shape))


def params():
    return pltpu.CompilerParams(vmem_limit_bytes=VMEM_BYTES)


def rows_body(q0, q1, k0, k1, v0, v1, g0, g1, m0, m1, embed, top, bottom):
    for index, pair in enumerate(((q0, q1), (k0, k1), (v0, v1), (g0, g1))):
        for source, mask, out in zip(pair, (m0, m1), (top, bottom)):
            if index == 1:
                keyed = keyed_rows(source[:, 0].astype(F32), mask[0], embed[...])
                out[index] = keyed.astype(BF16)
            else:
                out[index] = source[:, 0]


def edge_rows(arrays, mask, embed):
    operands, specs = [], []
    for array in arrays:
        array = array.reshape(2, 16, STRIP, 512)
        operands += [array, array]
        specs += [
            pl.BlockSpec((2, 1, STRIP, 512), lambda s: (0, 0, 0, 0)),
            pl.BlockSpec((2, 1, STRIP, 512), lambda s: (0, 15, 0, 0)),
        ]
    mask = mask.reshape(16, STRIP, 128)
    return pl.pallas_call(
        rows_body,
        grid=(1,),
        in_specs=specs
        + [
            pl.BlockSpec((1, STRIP, 128), lambda s: (0, 0, 0)),
            pl.BlockSpec((1, STRIP, 128), lambda s: (15, 0, 0)),
            pl.BlockSpec((1, 512), lambda s: (0, 0)),
        ],
        out_specs=[pl.BlockSpec((4, 2, STRIP, 512), lambda s: (0, 0, 0, 0))] * 2,
        out_shape=[jax.ShapeDtypeStruct((4, 2, STRIP, 512), BF16)] * 2,
        compiler_params=params(),
        cost_estimate=pl.CostEstimate(flops=0, bytes_accessed=5 * MIB, transcendentals=0),
        name="edge_rows",
    )(*operands, mask, mask, embed)


def strips_body(flip, core, q, k, v, g, mask, embed, perm, out, held, packed, came, gone):
    tile = 2 * jnp.where(flip, 1 - core[0], core[0])
    arrivals = []
    for index, source in enumerate((q, k, v, g)):
        copy = pltpu.make_async_copy(source.at[:, :, tile], held.at[index], came.at[index])
        copy.start()
        arrivals.append(copy)
    departures = []
    for index in range(4):
        arrivals[index].wait()
        for band in range(1, 8):
            opening = held[index, :, 6 * band : 6 * band + 3].astype(F32)
            closing = held[index, :, 6 * band - 3 : 6 * band].astype(F32)
            if index == 1:
                opening = keyed_rows(opening, mask[6 * band : 6 * band + 3, 0], embed[...])
                closing = keyed_rows(closing, mask[6 * band - 3 : 6 * band, 0], embed[...])
            tokens = jnp.concatenate([opening.reshape(48, 512), closing.reshape(48, 512)], axis=0)
            strip = dot(perm[0], tokens.astype(BF16))
            if index == 0:
                strip = strip * 0.125
            packed[index, band - 1] = strip.astype(BF16)
        copy = pltpu.make_async_copy(packed.at[index], out.at[index], gone.at[index])
        copy.start()
        departures.append(copy)
    for copy in departures:
        copy.wait()


def pack_strips(arrays, mask, embed, perm, core, flip):
    tiles = [array.reshape(2, 48, 3, 8, 512) for array in arrays]

    def mask_pick(s, core):
        return (0, 2 * jnp.where(flip, 1 - core[0], core[0]), 0, 0)

    anywhere = pl.BlockSpec(memory_space=pl.ANY)
    return pl.pallas_call(
        functools.partial(strips_body, flip),
        grid_spec=pltpu.PrefetchScalarGridSpec(
            num_scalar_prefetch=1,
            grid=(1,),
            in_specs=[anywhere] * 4
            + [
                pl.BlockSpec((48, 1, 8, 128), mask_pick),
                fixed_spec((1, 512)),
                side_spec((STRIP, 96)),
            ],
            out_specs=anywhere,
            scratch_shapes=[
                pltpu.VMEM((4, 2, 48, 8, 512), BF16),
                pltpu.VMEM((4, 7, STRIP, 512), BF16),
                pltpu.SemaphoreType.DMA((4,)),
                pltpu.SemaphoreType.DMA((4,)),
            ],
        ),
        out_shape=jax.ShapeDtypeStruct((4, 7, STRIP, 512), BF16),
        compiler_params=params(),
        cost_estimate=pl.CostEstimate(
            flops=2 * 28 * STRIP * 96 * 512, bytes_accessed=6 * MIB, transcendentals=0
        ),
        name="pack_near" if flip else "pack_far",
    )(core, *tiles, mask.reshape(48, 3, 8, 128), embed, perm)


def corners_body(core, top, bottom, below, above, perm, far, near, mid):
    for index in range(4):
        for place, (first, second) in enumerate(((top, above), (below, bottom))):
            first = first[index].astype(F32)
            second = second[index].astype(F32)
            tokens = jnp.concatenate([first[0], first[1], second[0], second[1]], axis=0)
            strips = dot(perm[0], tokens.astype(BF16))
            if index == 0:
                strips = strips * 0.125
            far[index, place] = strips[:STRIP].astype(BF16)
            near[index, place] = strips[STRIP : 2 * STRIP].astype(BF16)
            mid[index, place] = strips[2 * STRIP :].astype(BF16)


def pack_corners(top, bottom, below, above, perm, core):
    sizes = (STRIP, STRIP, WIN)
    return pl.pallas_call(
        corners_body,
        grid_spec=pltpu.PrefetchScalarGridSpec(
            num_scalar_prefetch=1,
            grid=(1,),
            in_specs=[fixed_spec((4, 2, STRIP, 512))] * 4 + [side_spec((2 * WIN, 2 * WIN))],
            out_specs=[fixed_spec((4, 2, size, 512)) for size in sizes],
        ),
        out_shape=[jax.ShapeDtypeStruct((4, 2, size, 512), BF16) for size in sizes],
        compiler_params=params(),
        cost_estimate=pl.CostEstimate(
            flops=2 * 8 * 288 * 288 * 512, bytes_accessed=5 * MIB, transcendentals=0
        ),
        name="pack_corners",
    )(core, top, bottom, below, above, perm)


def windows(win, slots, bias, scores, grads, low, dlow, store):
    lane = lax.broadcasted_iota(jnp.int32, (1, GROUP), 1) // 64

    def spread(x):
        return jnp.concatenate(
            [x * jnp.where(lane == h, 1.0, 0.0).astype(BF16) for h in range(4)], axis=0
        )

    def by_head(wide):
        total = None
        for h in range(4):
            piece = jnp.where(lane == h, wide[WIN * h : WIN * (h + 1)], 0.0)
            total = piece if total is None else total + piece
        return total

    jobs = []
    for slot in range(slots):
        for group in range(2):
            cols = slice(GROUP * group, GROUP * (group + 1))
            q, k, v, g = (win[slot, index, :, cols] for index in range(4))
            q_wide, g_wide = spread(q), spread(g)
            place = 2 * slot + group
            scores[place] = dot(k, q_wide, 1, 1)
            grads[place] = dot(v, g_wide, 1, 1)
            jobs.append((slot, group, place, cols, k, v, q_wide, g_wide))
    for slot, group, place, cols, k, v, q_wide, g_wide in jobs:
        for start in range(0, 576, 128):
            part = slice(start, min(start + 128, 576))
            s = scores[place, :, part] + bias[0, group, :, part]
            e = jnp.exp(s - jnp.max(s, axis=0, keepdims=True))
            p = e * (1.0 / jnp.sum(e, axis=0, keepdims=True))
            gp = grads[place, :, part]
            delta = jnp.sum(p * gp, axis=0, keepdims=True)
            low[place, :, part] = p.astype(BF16)
            dlow[place, :, part] = (p * (gp - delta)).astype(BF16)
        p_low, d_low = low[place], dlow[place]
        store(slot, 0, cols, by_head(dot(p_low, v, 0, 0)))
        store(slot, 1, cols, by_head(dot(d_low, k, 0, 0)) * 0.125)
        store(slot, 2, cols, dot(d_low, q_wide))
        store(slot, 3, cols, dot(p_low, g_wide))


def place_pair(win, slot, own, halo, own_left):
    def put(left, right):
        for index in range(4):
            both = jnp.concatenate(
                [left[index, 0].astype(F32), right[index, 0].astype(F32)], axis=0
            )
            win[slot, index] = both.astype(BF16)

    @pl.when(own_left)
    def _():
        put(own, halo)

    @pl.when(jnp.logical_not(own_left))
    def _():
        put(halo, own)


def inner_body(core, q0, q1, k0, k1, v0, v1, g0, g1, m0, m1, embed, perm, mid_c, own, own_c, halo, halo_c, bias, back, *rest):
    outs, (win, result, ready, gone), work = rest[:4], rest[4:8], rest[8:]
    s = pl.program_id(0)
    left = core[0] == 0
    corner = s < 2

    @pl.when(corner)
    def _():
        for index in range(4):
            win[0, index] = mid_c[index, 0]
        place_pair(win, 1, own_c, halo_c, left)

    @pl.when(jnp.logical_not(corner))
    def _():
        for index, pair in enumerate(((q0, q1), (k0, k1), (v0, v1), (g0, g1))):
            first, second = (source[:, 0].astype(F32) for source in pair)
            if index == 1:
                first = keyed_rows(first, m0[0], embed[...])
                second = keyed_rows(second, m1[0], embed[...])
            tokens = jnp.concatenate([first[0], first[1], second[0], second[1]], axis=0)
            packed = dot(perm[...], tokens.astype(BF16))
            if index == 0:
                packed = packed * 0.125
            win[0, index] = packed.astype(BF16)
        place_pair(win, 1, own, halo, left)

    starts = (pl.multiple_of(WIN * core[0], 16), pl.multiple_of(WIN * (1 - core[0]), 16))

    def keep(slot, index, cols, value):
        result[index, pl.ds(starts[slot], WIN), cols] = value.astype(BF16)

    windows(win, 2, bias, *work, keep)

    def leave(slot, first, second):
        copies = []
        for index, out in enumerate(outs):
            for part, block in enumerate((first, second)):
                copies.append(
                    pltpu.make_async_copy(
                        ready.at[slot, index, part], out.at[:, block], gone.at[slot, index, part]
                    )
                )
        return copies

    slot = jnp.where(corner, 0, (s + 1) % 2)

    @pl.when(s >= 3)
    def _():
        for copy in leave(slot, 0, 15):
            copy.wait()

    used = pl.ds(pl.multiple_of(64 * core[0], 16), 224)
    for index in range(4):
        full = dot(back[0], result[index, used]).reshape(2, 2, STRIP, 512).astype(BF16)

        @pl.when(s != 1)
        def _():
            ready[slot, index, 0] = full[0]

        @pl.when(s != 0)
        def _():
            ready[slot, index, 1] = full[1]

    @pl.when(s > 0)
    def _():
        first = jnp.where(corner, 0, 2 * (s - 1))
        second = jnp.where(corner, 15, 2 * (s - 1) - 1)
        for copy in leave(slot, first, second):
            copy.start()

    @pl.when(s == 8)
    def _():
        for copy in leave(0, 0, 15) + leave(1, 0, 15):
            copy.wait()


def work_scratch(places):
    return [
        pltpu.VMEM((places, WIN, 576), F32),
        pltpu.VMEM((places, WIN, 576), F32),
        pltpu.VMEM((places, WIN, 576), BF16),
        pltpu.VMEM((places, WIN, 576), BF16),
    ]


def window_cost(count, moved):
    return pl.CostEstimate(
        flops=count * 6 * 2 * WIN * WIN * 512 * 4,
        bytes_accessed=moved,
        transcendentals=count * 8 * WIN * WIN,
    )


def inner(arrays, mask, embed, perm, mid_c, own, own_c, halo, halo_c, bias, back, core):
    operands, specs = [], []
    block = (2, 1, STRIP, 512)
    mask = mask.reshape(16, STRIP, 128)

    def opening(s):
        return jnp.maximum(2 * (s - 1), 2)

    def closing(s):
        return opening(s) - 1

    for array in arrays:
        array = array.reshape(2, 16, STRIP, 512)
        operands += [array, array]
        specs += [
            pl.BlockSpec(block, lambda s, core: (0, opening(s), 0, 0)),
            pl.BlockSpec(block, lambda s, core: (0, closing(s), 0, 0)),
        ]

    def band(size):
        return pl.BlockSpec((4, 1, size, 512), lambda s, core: (0, jnp.maximum(s - 2, 0), 0, 0))

    def corner(size):
        return pl.BlockSpec((4, 1, size, 512), lambda s, core: (0, jnp.minimum(s, 1), 0, 0))

    anywhere = pl.BlockSpec(memory_space=pl.ANY)
    return pl.pallas_call(
        inner_body,
        grid_spec=pltpu.PrefetchScalarGridSpec(
            num_scalar_prefetch=1,
            grid=(9,),
            in_specs=specs
            + [
                pl.BlockSpec((1, STRIP, 128), lambda s, core: (opening(s), 0, 0)),
                pl.BlockSpec((1, STRIP, 128), lambda s, core: (closing(s), 0, 0)),
                fixed_spec((1, 512)),
                fixed_spec((WIN, 2 * WIN)),
                corner(WIN),
                band(STRIP),
                corner(STRIP),
                band(STRIP),
                corner(STRIP),
                pl.BlockSpec(
                    (1, 2, WIN, 576), lambda s, core: (jnp.where(s < 2, s + 1, 0), 0, 0, 0)
                ),
                side_spec((2 * WIN, 224)),
            ],
            out_specs=[anywhere] * 4,
            scratch_shapes=[
                pltpu.VMEM((2, 4, WIN, 512), BF16),
                pltpu.VMEM((4, 2 * WIN, 512), BF16),
                pltpu.VMEM((2, 4, 2, 2, STRIP, 512), BF16),
                pltpu.SemaphoreType.DMA((2, 4, 2)),
            ]
            + work_scratch(4),
        ),
        out_shape=[jax.ShapeDtypeStruct((2, 16, STRIP, 512), BF16)] * 4,
        compiler_params=params(),
        cost_estimate=window_cost(18, 24 * MIB),
        name="inner_windows",
    )(core, *operands, mask, mask, embed, perm, mid_c, own, own_c, halo, halo_c, bias, back)


def outer_body(core, own, own_c, halo, halo_c, bias, back, p0, p1, p2, p3, o0, o1, o2, o3, win, result, tiles, came, gone, *work):
    s = pl.program_id(0)
    left = core[0] == 1
    tile = 2 * core[0]
    outs = (o0, o1, o2, o3)

    def arrivals():
        return [
            pltpu.make_async_copy(out.at[:, :, tile], tiles.at[index], came.at[index])
            for index, out in enumerate(outs)
        ]

    @pl.when(s == 0)
    def _():
        for copy in arrivals():
            copy.start()

    @pl.when(s < 7)
    def _():
        place_pair(win, 0, own, halo, left)

    @pl.when(s >= 7)
    def _():
        place_pair(win, 0, own_c, halo_c, left)

    def keep(slot, index, cols, value):
        result[index, :, cols] = value.astype(BF16)

    windows(win, 1, bias, *work, keep)

    @pl.when(s == 0)
    def _():
        for copy in arrivals():
            copy.wait()

    used = pl.ds(pl.multiple_of(64 * (1 - core[0]), 16), 80)

    def leave(step, index, row, count):
        span = pl.ds(row, count)
        return pltpu.make_async_copy(
            tiles.at[index, :, span], outs[index].at[:, span, tile], gone.at[step, index]
        )

    for index in range(4):
        full = dot(back[0], result[index, used]).reshape(2, 2, 3, 8, 512)

        def add(part, row, index=index, full=full):
            span = pl.ds(row, 3)
            total = tiles[index, :, span].astype(F32) + full[part]
            tiles[index, :, span] = total.astype(BF16)

        @pl.when(s < 7)
        def _():
            add(0, 6 * s + 6)
            add(1, 6 * s + 3)
            leave(s, index, 6 * s + 3, 6).start()

        @pl.when(s == 7)
        def _():
            add(0, 0)
            leave(7, index, 0, 3).start()

        @pl.when(s == 8)
        def _():
            add(1, 45)
            leave(8, index, 45, 3).start()

    @pl.when(s == 8)
    def _():
        for index in range(4):
            for step in range(7):
                leave(step, index, 6 * step + 3, 6).wait()
            leave(7, index, 0, 3).wait()
            leave(8, index, 45, 3).wait()


def outer(partial, own, own_c, halo, halo_c, bias, back, core):
    def band(size):
        return pl.BlockSpec((4, 1, size, 512), lambda s, core: (0, jnp.minimum(s, 6), 0, 0))

    def corner(size):
        return pl.BlockSpec((4, 1, size, 512), lambda s, core: (0, jnp.maximum(s - 7, 0), 0, 0))

    anywhere = pl.BlockSpec(memory_space=pl.ANY)
    shape = (2, 48, 3, 8, 512)
    return pl.pallas_call(
        outer_body,
        grid_spec=pltpu.PrefetchScalarGridSpec(
            num_scalar_prefetch=1,
            grid=(9,),
            in_specs=[
                band(STRIP),
                corner(STRIP),
                band(STRIP),
                corner(STRIP),
                pl.BlockSpec(
                    (1, 2, WIN, 576), lambda s, core: (jnp.maximum(s - 6, 0), 0, 0, 0)
                ),
                side_spec((96, 80)),
            ]
            + [anywhere] * 4,
            out_specs=[anywhere] * 4,
            scratch_shapes=[
                pltpu.VMEM((1, 4, WIN, 512), BF16),
                pltpu.VMEM((4, WIN, 512), BF16),
                pltpu.VMEM((4, 2, 48, 8, 512), BF16),
                pltpu.SemaphoreType.DMA((4,)),
                pltpu.SemaphoreType.DMA((9, 4)),
            ]
            + work_scratch(2),
        ),
        out_shape=[jax.ShapeDtypeStruct(shape, BF16)] * 4,
        input_output_aliases={7 + index: index for index in range(4)},
        compiler_params=params(),
        cost_estimate=window_cost(9, 12 * MIB),
        name="outer_windows",
    )(core, own, own_c, halo, halo_c, bias, back, *[x.reshape(shape) for x in partial])


def bias_body(flags, table, hot, squeeze, out, wide, part, whole):
    variant = pl.program_id(0)

    @pl.when(variant == 0)
    def _():
        for head in range(8):
            line = jnp.broadcast_to(table[head : head + 1], (8, 768))
            line = pltpu.roll(line, 0, 1, stride=1, stride_axis=0)
            for run, base in enumerate(run_bases()):
                turn = int(base - 379) % 768
                turned = pltpu.roll(line, turn, 1)
                wide[head // 4, 8 * run : 8 * run + 8, 384 * (head % 4) : 384 * (head % 4) + 384] = turned[:, :384]
        for group in range(2):
            total = None
            for _ in range(3):
                part[...] = wide[group].astype(BF16)
                wide[group] = wide[group] - part[...].astype(F32)
                spread = dot(part[...], hot[...]).astype(BF16)
                piece = dot(squeeze[...], spread)
                total = piece if total is None else total + piece
            whole[group] = total

    @pl.when((variant == 0) | (flags[variant] == 0))
    def _():
        out[0] = whole[...]

    @pl.when((variant > 0) & (flags[variant] != 0))
    def _():
        upper = lax.broadcasted_iota(jnp.int32, (WIN, 576), 0) % STRIP < HALF
        upper_i = lax.broadcasted_iota(jnp.int32, (WIN, 576), 1) % STRIP < HALF
        for group in range(2):
            out[0, group] = jnp.where(upper == upper_i, whole[group], -jnp.inf)


def window_bias(rel_table, flags):
    tokens = (run_bases()[:, None] + np.arange(6)).reshape(WIN)
    hot = np.zeros((4, 384, 4, WIN), np.float32)
    for head in range(4):
        hot[head, tokens, head, np.arange(WIN)] = 1
    squeeze = np.zeros((24, 6, 24, 8), np.float32)
    for run in range(24):
        squeeze[run, np.arange(6), run, np.arange(6)] = 1
    hot = jnp.asarray(hot.reshape(4 * 384, 4 * WIN), BF16)
    squeeze = jnp.asarray(squeeze.reshape(WIN, 192), BF16)
    table = jnp.pad(rel_table, ((0, 0), (0, 768 - rel_table.shape[1])))
    return pl.pallas_call(
        bias_body,
        grid_spec=pltpu.PrefetchScalarGridSpec(
            num_scalar_prefetch=1,
            grid=(3,),
            in_specs=[
                pl.BlockSpec((8, 768), lambda v, flags: (0, 0)),
                pl.BlockSpec((4 * 384, 576), lambda v, flags: (0, 0)),
                pl.BlockSpec((WIN, 192), lambda v, flags: (0, 0)),
            ],
            out_specs=pl.BlockSpec((1, 2, WIN, 576), lambda v, flags: (v, 0, 0, 0)),
            scratch_shapes=[
                pltpu.VMEM((2, 192, 4 * 384), F32),
                pltpu.VMEM((192, 4 * 384), BF16),
                pltpu.VMEM((2, WIN, 576), F32),
            ],
        ),
        out_shape=jax.ShapeDtypeStruct((3, 2, WIN, 576), F32),
        compiler_params=pltpu.CompilerParams(vmem_limit_bytes=VMEM_BYTES),
        cost_estimate=pl.CostEstimate(
            flops=6 * 2 * 192 * 1536 * 576, bytes_accessed=4 * MIB, transcendentals=0
        ),
        name="window_bias",
    )(flags, table, hot, squeeze)


def side_tables():
    far_strip, near_strip = (0, 3), (3, 0)
    far, near, whole, near_back, far_back = [], [], [], [], []
    for side in range(2):
        far.append(far_matrix(far_strip[side], 2 * side))
        near.append(far_matrix(near_strip[side], 2 - 2 * side))
        whole.append(strip_matrix([far_strip[side], near_strip[side], 1, 2]))
        own = strip_matrix([near_strip[side]]).T
        middle = strip_matrix([1, 2]).T
        pad = np.zeros((2 * WIN, 8), np.float32)
        pad_far = np.zeros((96, 8), np.float32)
        if side == 0:
            near_back.append(np.concatenate([middle, own, pad], axis=1))
            far_back.append(np.concatenate([pad_far, far[0].T], axis=1))
        else:
            near_back.append(np.concatenate([pad, own, middle], axis=1))
            far_back.append(np.concatenate([far[1].T, pad_far], axis=1))
    stacked = (far, near, whole, near_back, far_back)
    return [jnp.asarray(np.stack(table), BF16) for table in stacked]


def after(value, earlier):
    return lax.optimization_barrier((value, earlier))[0]


def shards(queries, key_tokens, value_tokens, out_grad, land_mask, land_embed, rel_table):
    lev, rows, cols, width = queries.shape
    lat = lax.axis_index("lat")
    core = jnp.reshape(lax.axis_index("lon") % 2, (1,))
    bands = lax.axis_size("lat")
    sectors = lax.axis_size("lon")
    arrays = (queries, key_tokens, value_tokens, out_grad)
    mask = jnp.broadcast_to(
        land_mask.astype(F32).reshape(rows // 3, STRIP, 1), (rows // 3, STRIP, 128)
    )
    embed = land_embed.reshape(1, width)
    far_perm, near_perm, all_perm, near_back, far_back = side_tables()
    mid_perm = jnp.asarray(strip_matrix([1, 2]), BF16)

    to_far = [((2 * k + 1) % sectors, (2 * k + 2) % sectors) for k in range(sectors // 2)]
    to_far += [(b, a) for a, b in to_far]
    to_near = [(i, i ^ 1) for i in range(sectors)]

    top, bottom = edge_rows(arrays, mask, embed)
    below = lax.ppermute(top, "lat", [(i, i - 1) for i in range(1, bands)])
    above = lax.ppermute(bottom, "lat", [(i, i + 1) for i in range(bands - 1)])

    far = pack_strips(arrays, mask, after(embed, top), far_perm, core, False)
    far_halo = lax.ppermute(far, "lon", to_far)
    near = pack_strips(arrays, mask, after(embed, far), near_perm, core, True)
    near_halo = lax.ppermute(near, "lon", to_near)

    flags = jnp.stack([0 * lat, lat == 0, lat == bands - 1]).astype(jnp.int32)
    bias = window_bias(after(rel_table, near), flags)

    far_c, near_c, mid_c = pack_corners(top, bottom, below, above, all_perm, core)
    far_halo_c = lax.ppermute(far_c, "lon", to_far)
    near_halo_c = lax.ppermute(near_c, "lon", to_near)

    partial = inner(
        arrays, mask, embed, mid_perm, mid_c, near, near_c, near_halo, near_halo_c, bias,
        near_back, core,
    )
    final = outer(partial, far, far_c, far_halo, far_halo_c, bias, far_back, core)
    return tuple(x.reshape(queries.shape) for x in final)


def solution(mesh):
    tokens = P(None, "lat", "lon", None)
    return jax.shard_map(
        shards,
        mesh=mesh,
        in_specs=(tokens, tokens, tokens, tokens, P("lat", "lon"), P(), P()),
        out_specs=(tokens,) * 4,
        check_vma=False,
    )
```

```python
import functools

import jax
import jax.numpy as jnp
import numpy as np
from jax import lax
from jax.experimental import pallas as pl
from jax.experimental.pallas import tpu as pltpu
from jax.sharding import PartitionSpec as P

F32 = jnp.float32
BF16 = jnp.bfloat16
HALF = 36
STRIP = 72
WIN = 144
GROUP = 256
MIB = 1 << 20
VMEM_BYTES = 60 * MIB


def strip_matrix(strips):
    out = np.zeros((len(strips), 2, 2, 3, 6, 2, 2, 3, 24), np.float32)
    for place, strip in enumerate(strips):
        for part in range(2):
            for lev in range(2):
                for row in range(3):
                    for col in range(6):
                        out[place, part, lev, row, col, part, lev, row, 6 * strip + col] = 1
    return out.reshape(len(strips) * STRIP, 2 * WIN)


def far_matrix(strip, tile):
    full = strip_matrix([strip]).reshape(STRIP, 2, 2, 3, 3, 8)
    return full[:, :, :, :, tile].reshape(STRIP, 96)


def run_bases():
    run = np.arange(24)
    half, part, lev, row = run // 12, run // 6 % 2, run // 3 % 2, run % 3
    return lev * 253 + (row + 3 * (1 - part)) * 23 + 6 * half


def dot(a, b, ca=1, cb=0):
    return lax.dot_general(a, b, (((ca,), (cb,)), ((), ())), preferred_element_type=F32)


def keyed_rows(key, mask, embed):
    wide = jnp.concatenate([mask] * 4, axis=-1)
    return (key + (wide * embed)[None]).astype(BF16).astype(F32)


def side_spec(shape):
    return pl.BlockSpec((1, *shape), lambda s, core: (core[0],) + (0,) * len(shape))


def fixed_spec(shape):
    return pl.BlockSpec(shape, lambda s, core: (0,) * len(shape))


def params():
    return pltpu.CompilerParams(vmem_limit_bytes=VMEM_BYTES)


def edges_body(core, q, k, v, g, mask, embed, far_perm, near_perm, far, near, top, bottom, held, packed, rows, came, gone, rows_came, rows_gone):
    sources = (q, k, v, g)
    tiles = (2 * core[0], 2 - 2 * core[0])

    def fetch(side, index):
        return pltpu.make_async_copy(
            sources[index].at[:, :, tiles[side]], held.at[side, index], came.at[side, index]
        )

    def send_off(side, index):
        return pltpu.make_async_copy(
            packed.at[side, index], (far, near)[side].at[index], gone.at[side, index]
        )

    ends = ((top, 0), (bottom, 45))

    def end_rows(end, index):
        out, row = ends[end]
        if index == 1:
            return pltpu.make_async_copy(rows.at[end], out.at[1], rows_gone.at[end, 1])
        return pltpu.make_async_copy(
            sources[index].at[:, row : row + 3], out.at[index], rows_gone.at[end, index]
        )

    def key_rows(end):
        row = ends[end][1]
        return pltpu.make_async_copy(k.at[:, row : row + 3], rows.at[end], rows_came.at[end])

    for index in range(4):
        fetch(0, index).start()
    for end in range(2):
        key_rows(end).start()
    for index in range(4):
        fetch(1, index).start()
    for end in range(2):
        for index in (0, 2, 3):
            end_rows(end, index).start()
    for side in range(2):
        perm = (far_perm, near_perm)[side]
        for index in range(4):
            fetch(side, index).wait()
            for band in range(1, 8):
                lower, upper = 6 * band, 6 * band - 3
                opening = held[side, index, :, lower : lower + 3].astype(F32)
                closing = held[side, index, :, upper : upper + 3].astype(F32)
                if index == 1:
                    opening = keyed_rows(
                        opening, mask[lower : lower + 3, pl.ds(tiles[side], 1)][:, 0], embed[...]
                    )
                    closing = keyed_rows(
                        closing, mask[upper : upper + 3, pl.ds(tiles[side], 1)][:, 0], embed[...]
                    )
                tokens = jnp.concatenate(
                    [opening.reshape(48, 512), closing.reshape(48, 512)], axis=0
                )
                strip = dot(perm[0], tokens.astype(BF16))
                if index == 0:
                    strip = strip * 0.125
                packed[side, index, band - 1] = strip.astype(BF16)
            send_off(side, index).start()
        if side == 0:
            for end in range(2):
                key_rows(end).wait()
                row = ends[end][1]
                keyed = keyed_rows(rows[end].astype(F32), mask[row : row + 3], embed[...])
                rows[end] = keyed.astype(BF16)
                end_rows(end, 1).start()
    for index in range(4):
        for side in range(2):
            send_off(side, index).wait()
        for end in range(2):
            end_rows(end, index).wait()


def pack_edges(arrays, mask, embed, far_perm, near_perm, core):
    tiles = [array.reshape(2, 48, 3, 8, 512) for array in arrays]
    anywhere = pl.BlockSpec(memory_space=pl.ANY)
    strips = jax.ShapeDtypeStruct((4, 7, STRIP, 512), BF16)
    ends = jax.ShapeDtypeStruct((4, 2, 3, 3, 8, 512), BF16)
    return pl.pallas_call(
        edges_body,
        grid_spec=pltpu.PrefetchScalarGridSpec(
            num_scalar_prefetch=1,
            grid=(1,),
            in_specs=[anywhere] * 4
            + [
                fixed_spec((48, 3, 8, 128)),
                fixed_spec((1, 512)),
                side_spec((STRIP, 96)),
                side_spec((STRIP, 96)),
            ],
            out_specs=[anywhere] * 4,
            scratch_shapes=[
                pltpu.VMEM((2, 4, 2, 48, 8, 512), BF16),
                pltpu.VMEM((2, 4, 7, STRIP, 512), BF16),
                pltpu.VMEM((2, 2, 3, 3, 8, 512), BF16),
                pltpu.SemaphoreType.DMA((2, 4)),
                pltpu.SemaphoreType.DMA((2, 4)),
                pltpu.SemaphoreType.DMA((2,)),
                pltpu.SemaphoreType.DMA((2, 4)),
            ],
        ),
        out_shape=[strips, strips, ends, ends],
        compiler_params=params(),
        cost_estimate=pl.CostEstimate(
            flops=2 * 56 * STRIP * 96 * 512, bytes_accessed=16 * MIB, transcendentals=0
        ),
        name="pack_edges",
    )(core, *tiles, mask.reshape(48, 3, 8, 128), embed, far_perm, near_perm)


def corners_body(core, top, bottom, below, above, perm, far, near, mid):
    for index in range(4):
        for place, (first, second) in enumerate(((top, above), (below, bottom))):
            first = first[index].astype(F32)
            second = second[index].astype(F32)
            tokens = jnp.concatenate([first[0], first[1], second[0], second[1]], axis=0)
            strips = dot(perm[0], tokens.astype(BF16))
            if index == 0:
                strips = strips * 0.125
            far[index, place] = strips[:STRIP].astype(BF16)
            near[index, place] = strips[STRIP : 2 * STRIP].astype(BF16)
            mid[index, place] = strips[2 * STRIP :].astype(BF16)


def pack_corners(top, bottom, below, above, perm, core):
    sizes = (STRIP, STRIP, WIN)
    return pl.pallas_call(
        corners_body,
        grid_spec=pltpu.PrefetchScalarGridSpec(
            num_scalar_prefetch=1,
            grid=(1,),
            in_specs=[fixed_spec((4, 2, STRIP, 512))] * 4 + [side_spec((2 * WIN, 2 * WIN))],
            out_specs=[fixed_spec((4, 2, size, 512)) for size in sizes],
        ),
        out_shape=[jax.ShapeDtypeStruct((4, 2, size, 512), BF16) for size in sizes],
        compiler_params=params(),
        cost_estimate=pl.CostEstimate(
            flops=2 * 8 * 288 * 288 * 512, bytes_accessed=5 * MIB, transcendentals=0
        ),
        name="pack_corners",
    )(core, top, bottom, below, above, perm)


def windows(win, slots, bias, scores, grads, low, dlow, store):
    lane = lax.broadcasted_iota(jnp.int32, (1, GROUP), 1) // 64

    def spread(x):
        return jnp.concatenate(
            [x * jnp.where(lane == h, 1.0, 0.0).astype(BF16) for h in range(4)], axis=0
        )

    def by_head(wide):
        total = None
        for h in range(4):
            piece = jnp.where(lane == h, wide[WIN * h : WIN * (h + 1)], 0.0)
            total = piece if total is None else total + piece
        return total

    jobs = []
    for slot in range(slots):
        for group in range(2):
            cols = slice(GROUP * group, GROUP * (group + 1))
            q, k, v, g = (win[slot, index, :, cols] for index in range(4))
            q_wide, g_wide = spread(q), spread(g)
            place = 2 * slot + group
            scores[place] = dot(k, q_wide, 1, 1)
            grads[place] = dot(v, g_wide, 1, 1)
            jobs.append((slot, group, place, cols, k, v, q_wide, g_wide))
    for slot, group, place, cols, k, v, q_wide, g_wide in jobs:
        for start in range(0, 576, 128):
            part = slice(start, min(start + 128, 576))
            s = scores[place, :, part] + bias[0, group, :, part]
            e = jnp.exp(s - jnp.max(s, axis=0, keepdims=True))
            p = e * (1.0 / jnp.sum(e, axis=0, keepdims=True))
            gp = grads[place, :, part]
            delta = jnp.sum(p * gp, axis=0, keepdims=True)
            low[place, :, part] = p.astype(BF16)
            dlow[place, :, part] = (p * (gp - delta)).astype(BF16)
        p_low, d_low = low[place], dlow[place]
        store(slot, 0, cols, by_head(dot(p_low, v, 0, 0)))
        store(slot, 1, cols, by_head(dot(d_low, k, 0, 0)) * 0.125)
        store(slot, 2, cols, dot(d_low, q_wide))
        store(slot, 3, cols, dot(p_low, g_wide))


def place_pair(win, slot, own, halo, own_left):
    def put(left, right):
        for index in range(4):
            both = jnp.concatenate(
                [left[index, 0].astype(F32), right[index, 0].astype(F32)], axis=0
            )
            win[slot, index] = both.astype(BF16)

    @pl.when(own_left)
    def _():
        put(own, halo)

    @pl.when(jnp.logical_not(own_left))
    def _():
        put(halo, own)


def inner_body(core, q0, q1, k0, k1, v0, v1, g0, g1, m0, m1, embed, perm, own, halo, bias, back, *rest):
    outs, token, (win, result, ready, gone), work = rest[:4], rest[4], rest[5:9], rest[9:]
    s = pl.program_id(0)
    for index, pair in enumerate(((q0, q1), (k0, k1), (v0, v1), (g0, g1))):
        first, second = (source[:, 0].astype(F32) for source in pair)
        if index == 1:
            first = keyed_rows(first, m0[0], embed[...])
            second = keyed_rows(second, m1[0], embed[...])
        tokens = jnp.concatenate([first[0], first[1], second[0], second[1]], axis=0)
        packed = dot(perm[...], tokens.astype(BF16))
        if index == 0:
            packed = packed * 0.125
        win[0, index] = packed.astype(BF16)
    place_pair(win, 1, own, halo, core[0] == 0)

    starts = (pl.multiple_of(WIN * core[0], 16), pl.multiple_of(WIN * (1 - core[0]), 16))

    def keep(slot, index, cols, value):
        result[index, pl.ds(starts[slot], WIN), cols] = value.astype(BF16)

    windows(win, 2, bias, *work, keep)

    def leave(slot, step):
        copies = []
        for index, out in enumerate(outs):
            for part in range(2):
                copies.append(
                    pltpu.make_async_copy(
                        ready.at[slot, index, part],
                        out.at[:, 2 * step + 2 - part],
                        gone.at[slot, index, part],
                    )
                )
        return copies

    slot = s % 2

    @pl.when(s >= 2)
    def _():
        for copy in leave(slot, s - 2):
            copy.wait()

    used = pl.ds(pl.multiple_of(64 * core[0], 16), 224)
    for index in range(4):
        full = dot(back[0], result[index, used])
        ready[slot, index] = full.reshape(2, 2, STRIP, 512).astype(BF16)
    for copy in leave(slot, s):
        copy.start()

    @pl.when(s == 6)
    def _():
        token[...] = jnp.zeros_like(token)
        for copy in leave(1, 5) + leave(0, 6):
            copy.wait()


def work_scratch(places):
    return [
        pltpu.VMEM((places, WIN, 576), F32),
        pltpu.VMEM((places, WIN, 576), F32),
        pltpu.VMEM((places, WIN, 576), BF16),
        pltpu.VMEM((places, WIN, 576), BF16),
    ]


def window_cost(count, moved):
    return pl.CostEstimate(
        flops=count * 6 * 2 * WIN * WIN * 512 * 4,
        bytes_accessed=moved,
        transcendentals=count * 8 * WIN * WIN,
    )


def inner(arrays, mask, embed, perm, own, halo, bias, back, core):
    operands, specs = [], []
    block = (2, 1, STRIP, 512)
    for array in arrays:
        array = array.reshape(2, 16, STRIP, 512)
        operands += [array, array]
        specs += [
            pl.BlockSpec(block, lambda s, core: (0, 2 * s + 2, 0, 0)),
            pl.BlockSpec(block, lambda s, core: (0, 2 * s + 1, 0, 0)),
        ]
    anywhere = pl.BlockSpec(memory_space=pl.ANY)
    return pl.pallas_call(
        inner_body,
        grid_spec=pltpu.PrefetchScalarGridSpec(
            num_scalar_prefetch=1,
            grid=(7,),
            in_specs=specs
            + [
                pl.BlockSpec((1, STRIP, 128), lambda s, core: (2 * s + 2, 0, 0)),
                pl.BlockSpec((1, STRIP, 128), lambda s, core: (2 * s + 1, 0, 0)),
                fixed_spec((1, 512)),
                fixed_spec((WIN, 2 * WIN)),
                band_spec(),
                band_spec(),
                fixed_spec((1, 2, WIN, 576)),
                side_spec((2 * WIN, 224)),
            ],
            out_specs=[anywhere] * 4 + [fixed_spec((8, 128))],
            scratch_shapes=[
                pltpu.VMEM((2, 4, WIN, 512), BF16),
                pltpu.VMEM((4, 2 * WIN, 512), BF16),
                pltpu.VMEM((2, 4, 2, 2, STRIP, 512), BF16),
                pltpu.SemaphoreType.DMA((2, 4, 2)),
            ]
            + work_scratch(4),
        ),
        out_shape=[jax.ShapeDtypeStruct((2, 16, STRIP, 512), BF16)] * 4
        + [jax.ShapeDtypeStruct((8, 128), F32)],
        compiler_params=params(),
        cost_estimate=window_cost(14, 24 * MIB),
        name="inner_windows",
    )(core, *operands, mask, mask, embed, perm, own, halo, bias, back)


def band_spec():
    return pl.BlockSpec((4, 1, STRIP, 512), lambda s, core: (0, s, 0, 0))


def outer_body(core, own, halo, bias, back, p0, p1, p2, p3, o0, o1, o2, o3, win, result, tiles, came, gone, *work):
    s = pl.program_id(0)
    tile = 2 * core[0]
    outs = (o0, o1, o2, o3)

    def arrivals():
        return [
            pltpu.make_async_copy(out.at[:, 3:45, tile], tiles.at[index], came.at[index])
            for index, out in enumerate(outs)
        ]

    @pl.when(s == 0)
    def _():
        for copy in arrivals():
            copy.start()

    place_pair(win, 0, own, halo, core[0] == 1)

    def keep(slot, index, cols, value):
        result[index, :, cols] = value.astype(BF16)

    windows(win, 1, bias, *work, keep)

    @pl.when(s == 0)
    def _():
        for copy in arrivals():
            copy.wait()

    used = pl.ds(pl.multiple_of(64 * (1 - core[0]), 16), 80)

    def leave(step, index):
        return pltpu.make_async_copy(
            tiles.at[index, :, pl.ds(6 * step, 6)],
            outs[index].at[:, pl.ds(6 * step + 3, 6), tile],
            gone.at[step, index],
        )

    for index in range(4):
        full = dot(back[0], result[index, used]).reshape(2, 2, 3, 8, 512)
        for part in range(2):
            span = pl.ds(6 * s + 3 * (1 - part), 3)
            total = tiles[index, :, span].astype(F32) + full[part]
            tiles[index, :, span] = total.astype(BF16)
        leave(s, index).start()

    @pl.when(s == 6)
    def _():
        for index in range(4):
            for step in range(7):
                leave(step, index).wait()


def outer(partial, own, halo, bias, back, core):
    anywhere = pl.BlockSpec(memory_space=pl.ANY)
    shape = (2, 48, 3, 8, 512)
    return pl.pallas_call(
        outer_body,
        grid_spec=pltpu.PrefetchScalarGridSpec(
            num_scalar_prefetch=1,
            grid=(7,),
            in_specs=[
                band_spec(),
                band_spec(),
                fixed_spec((1, 2, WIN, 576)),
                side_spec((96, 80)),
            ]
            + [anywhere] * 4,
            out_specs=[anywhere] * 4,
            scratch_shapes=[
                pltpu.VMEM((1, 4, WIN, 512), BF16),
                pltpu.VMEM((4, WIN, 512), BF16),
                pltpu.VMEM((4, 2, 42, 8, 512), BF16),
                pltpu.SemaphoreType.DMA((4,)),
                pltpu.SemaphoreType.DMA((7, 4)),
            ]
            + work_scratch(2),
        ),
        out_shape=[jax.ShapeDtypeStruct(shape, BF16)] * 4,
        input_output_aliases={5 + index: index for index in range(4)},
        compiler_params=params(),
        cost_estimate=window_cost(7, 12 * MIB),
        name="outer_windows",
    )(core, own, halo, bias, back, *[x.reshape(shape) for x in partial])


def corner_body(core, flags, mid, near, near_halo, far, far_halo, bias, back, p0, p1, p2, p3, o0, o1, o2, o3, win, result, cut, *work):
    s = pl.program_id(0)
    left = core[0] == 0
    for index in range(4):
        win[1, index] = mid[index, 0]
    place_pair(win, 0, far, far_halo, jnp.logical_not(left))
    place_pair(win, 2, near, near_halo, left)

    key_part = lax.broadcasted_iota(jnp.int32, (WIN, 576), 0) % STRIP < HALF
    query_part = lax.broadcasted_iota(jnp.int32, (WIN, 576), 1) % STRIP < HALF
    apart = (key_part != query_part) & (flags[s] != 0)
    for group in range(2):
        cut[0, group] = jnp.where(apart, -jnp.inf, bias[0, group])

    starts = (
        pl.multiple_of(2 * WIN * core[0], 16),
        WIN,
        pl.multiple_of(2 * WIN * (1 - core[0]), 16),
    )

    def keep(slot, index, cols, value):
        result[index, pl.ds(starts[slot], WIN), cols] = value.astype(BF16)

    windows(win, 3, cut, *work, keep)
    for index, out in enumerate((o0, o1, o2, o3)):
        full = dot(back[0], result[index, 64:368])
        out[:, 0] = full.reshape(2, STRIP, 512).astype(BF16)


def corners(partial, flags, mid, near, near_halo, far, far_halo, bias, back, core):
    anywhere = pl.BlockSpec(memory_space=pl.ANY)
    shape = (2, 16, STRIP, 512)

    def edge(size):
        return pl.BlockSpec((4, 1, size, 512), lambda s, core, flags: (0, s, 0, 0))

    return pl.pallas_call(
        corner_body,
        grid_spec=pltpu.PrefetchScalarGridSpec(
            num_scalar_prefetch=2,
            grid=(2,),
            in_specs=[
                edge(WIN),
                edge(STRIP),
                edge(STRIP),
                edge(STRIP),
                edge(STRIP),
                pl.BlockSpec((1, 2, WIN, 576), lambda s, core, flags: (0, 0, 0, 0)),
                pl.BlockSpec((1, WIN, 304), lambda s, core, flags: (s, 0, 0)),
            ]
            + [anywhere] * 4,
            out_specs=[
                pl.BlockSpec((2, 1, STRIP, 512), lambda s, core, flags: (0, 15 * s, 0, 0))
            ]
            * 4,
            scratch_shapes=[
                pltpu.VMEM((3, 4, WIN, 512), BF16),
                pltpu.VMEM((4, 3 * WIN, 512), BF16),
                pltpu.VMEM((1, 2, WIN, 576), F32),
            ]
            + work_scratch(6),
        ),
        out_shape=[jax.ShapeDtypeStruct(shape, BF16)] * 4,
        input_output_aliases={9 + index: index for index in range(4)},
        compiler_params=params(),
        cost_estimate=window_cost(6, 8 * MIB),
        name="corner_windows",
    )(
        core, flags, mid, near, near_halo, far, far_halo, bias, back,
        *[x.reshape(shape) for x in partial],
    )


def bias_body(table, hot, squeeze, out, wide, part):
    for head in range(8):
        line = jnp.broadcast_to(table[head : head + 1], (8, 768))
        line = pltpu.roll(line, 0, 1, stride=1, stride_axis=0)
        for run, base in enumerate(run_bases()):
            turn = int(base - 379) % 768
            turned = pltpu.roll(line, turn, 1)
            group, cols = head // 4, slice(384 * (head % 4), 384 * (head % 4) + 384)
            wide[group, 8 * run : 8 * run + 8, cols] = turned[:, :384]
    for group in range(2):
        high = wide[group].astype(BF16)
        part[0, group] = high
        part[1, group] = (wide[group] - high.astype(F32)).astype(BF16)
    for group in range(2):
        total = None
        for order in range(2):
            spread = dot(part[order, group], hot[...]).astype(BF16)
            piece = dot(squeeze[...], spread)
            total = piece if total is None else total + piece
        out[0, group] = total


def window_bias(rel_table):
    tokens = (run_bases()[:, None] + np.arange(6)).reshape(WIN)
    hot = np.zeros((4, 384, 4, WIN), np.float32)
    for head in range(4):
        hot[head, tokens, head, np.arange(WIN)] = 1
    squeeze = np.zeros((24, 6, 24, 8), np.float32)
    for run in range(24):
        squeeze[run, np.arange(6), run, np.arange(6)] = 1
    hot = jnp.asarray(hot.reshape(4 * 384, 4 * WIN), BF16)
    squeeze = jnp.asarray(squeeze.reshape(WIN, 192), BF16)
    table = jnp.pad(rel_table, ((0, 0), (0, 768 - rel_table.shape[1])))
    return pl.pallas_call(
        bias_body,
        out_shape=jax.ShapeDtypeStruct((1, 2, WIN, 576), F32),
        scratch_shapes=[
            pltpu.VMEM((2, 192, 4 * 384), F32),
            pltpu.VMEM((2, 2, 192, 4 * 384), BF16),
        ],
        compiler_params=params(),
        cost_estimate=pl.CostEstimate(
            flops=4 * 2 * 192 * 1536 * 576, bytes_accessed=3 * MIB, transcendentals=0
        ),
        name="window_bias",
    )(table, hot, squeeze)


def side_tables():
    far_strip, near_strip = (0, 3), (3, 0)
    far, near, whole, near_back, far_back = [], [], [], [], []
    for side in range(2):
        far.append(far_matrix(far_strip[side], 2 * side))
        near.append(far_matrix(near_strip[side], 2 - 2 * side))
        whole.append(strip_matrix([far_strip[side], near_strip[side], 1, 2]))
        own = strip_matrix([near_strip[side]]).T
        middle = strip_matrix([1, 2]).T
        pad = np.zeros((2 * WIN, 8), np.float32)
        pad_far = np.zeros((96, 8), np.float32)
        if side == 0:
            near_back.append(np.concatenate([middle, own, pad], axis=1))
            far_back.append(np.concatenate([pad_far, far[0].T], axis=1))
        else:
            near_back.append(np.concatenate([pad, own, middle], axis=1))
            far_back.append(np.concatenate([far[1].T, pad_far], axis=1))
    natural = strip_matrix([0, 1, 2, 3]).T.reshape(2, WIN, 2 * WIN)
    corner_back = np.pad(natural, ((0, 0), (0, 0), (8, 8)))
    stacked = (far, near, whole, near_back, far_back, corner_back)
    return [jnp.asarray(np.stack(table), BF16) for table in stacked]


def after(value, earlier):
    return lax.optimization_barrier((value, earlier))[0]


def shards(queries, key_tokens, value_tokens, out_grad, land_mask, land_embed, rel_table):
    lev, rows, cols, width = queries.shape
    lat = lax.axis_index("lat")
    core = jnp.reshape(lax.axis_index("lon") % 2, (1,))
    bands = lax.axis_size("lat")
    sectors = lax.axis_size("lon")
    arrays = (queries, key_tokens, value_tokens, out_grad)
    mask = jnp.broadcast_to(
        land_mask.astype(F32).reshape(rows // 3, STRIP, 1), (rows // 3, STRIP, 128)
    )
    embed = land_embed.reshape(1, width)
    far_perm, near_perm, all_perm, near_back, far_back, corner_back = side_tables()
    mid_perm = jnp.asarray(strip_matrix([1, 2]), BF16)

    to_far = [((2 * k + 1) % sectors, (2 * k + 2) % sectors) for k in range(sectors // 2)]
    to_far += [(b, a) for a, b in to_far]
    to_near = [(i, i ^ 1) for i in range(sectors)]

    far, near, top, bottom = pack_edges(arrays, mask, embed, far_perm, near_perm, core)
    ends = (4, 2, STRIP, width)
    top, bottom = top.reshape(ends), bottom.reshape(ends)
    far_halo = lax.ppermute(far, "lon", to_far)
    near_halo = lax.ppermute(near, "lon", to_near)
    below = lax.ppermute(top, "lat", [(i, i - 1) for i in range(1, bands)])
    above = lax.ppermute(bottom, "lat", [(i, i + 1) for i in range(bands - 1)])

    bias = window_bias(after(rel_table, far))
    *partial, done = inner(
        arrays, mask, embed, mid_perm, near, near_halo, bias, near_back, core
    )

    far_c, near_c, mid_c = pack_corners(top, bottom, below, above, all_perm, after(core, done))
    far_halo_c = lax.ppermute(far_c, "lon", to_far)
    near_halo_c = lax.ppermute(near_c, "lon", to_near)

    partial = outer(partial, far, far_halo, bias, far_back, core)
    flags = jnp.stack([lat == 0, lat == bands - 1]).astype(jnp.int32)
    final = corners(
        partial, flags, mid_c, near_c, near_halo_c, far_c, far_halo_c, bias, corner_back, core
    )
    return tuple(x.reshape(queries.shape) for x in final)


def solution(mesh):
    tokens = P(None, "lat", "lon", None)
    return jax.shard_map(
        shards,
        mesh=mesh,
        in_specs=(tokens, tokens, tokens, tokens, P("lat", "lon"), P(), P()),
        out_specs=(tokens,) * 4,
        check_vma=False,
    )
```

```python
import functools

import jax
import jax.numpy as jnp
import numpy as np
from jax import lax
from jax.experimental import pallas as pl
from jax.experimental.pallas import tpu as pltpu
from jax.sharding import PartitionSpec as P

F32 = jnp.float32
BF16 = jnp.bfloat16
HALF = 36
STRIP = 72
WIN = 144
GROUP = 256
MIB = 1 << 20
VMEM_BYTES = 60 * MIB


def strip_matrix(strips):
    out = np.zeros((len(strips), 2, 2, 3, 6, 2, 2, 3, 24), np.float32)
    for place, strip in enumerate(strips):
        for part in range(2):
            for lev in range(2):
                for row in range(3):
                    for col in range(6):
                        out[place, part, lev, row, col, part, lev, row, 6 * strip + col] = 1
    return out.reshape(len(strips) * STRIP, 2 * WIN)


def far_matrix(strip, tile):
    full = strip_matrix([strip]).reshape(STRIP, 2, 2, 3, 3, 8)
    return full[:, :, :, :, tile].reshape(STRIP, 96)


def run_bases():
    run = np.arange(24)
    half, part, lev, row = run // 12, run // 6 % 2, run // 3 % 2, run % 3
    return lev * 253 + (row + 3 * (1 - part)) * 23 + 6 * half


def dot(a, b, ca=1, cb=0):
    return lax.dot_general(a, b, (((ca,), (cb,)), ((), ())), preferred_element_type=F32)


def keyed_rows(key, mask, embed):
    wide = jnp.concatenate([mask] * 4, axis=-1)
    return (key + (wide * embed)[None]).astype(BF16).astype(F32)


def side_spec(shape):
    return pl.BlockSpec((1, *shape), lambda s, core: (core[0],) + (0,) * len(shape))


def fixed_spec(shape):
    return pl.BlockSpec(shape, lambda s, core: (0,) * len(shape))


def params():
    return pltpu.CompilerParams(vmem_limit_bytes=VMEM_BYTES)


def edges_body(core, q, k, v, g, mask, embed, far_perm, near_perm, far, near, top, bottom, held, packed, rows, came, gone, rows_came, rows_gone):
    sources = (q, k, v, g)
    tiles = (2 * core[0], 2 - 2 * core[0])

    def fetch(side, index):
        return pltpu.make_async_copy(
            sources[index].at[:, :, tiles[side]], held.at[side, index], came.at[side, index]
        )

    def send_off(side, index):
        return pltpu.make_async_copy(
            packed.at[side, index], (far, near)[side].at[index], gone.at[side, index]
        )

    ends = ((top, 0), (bottom, 45))

    def rows_in(end, index):
        row = ends[end][1]
        return pltpu.make_async_copy(
            sources[index].at[:, row : row + 3], rows.at[end, index], rows_came.at[end, index]
        )

    def rows_out(end, index):
        return pltpu.make_async_copy(
            rows.at[end, index], ends[end][0].at[index], rows_gone.at[end, index]
        )

    for index in range(4):
        fetch(0, index).start()
    for end in range(2):
        for index in range(4):
            rows_in(end, index).start()
    for index in range(4):
        fetch(1, index).start()
    for side in range(2):
        perm = (far_perm, near_perm)[side]
        for index in range(4):
            fetch(side, index).wait()
            for band in range(1, 8):
                lower, upper = 6 * band, 6 * band - 3
                opening = held[side, index, :, lower : lower + 3].astype(F32)
                closing = held[side, index, :, upper : upper + 3].astype(F32)
                if index == 1:
                    opening = keyed_rows(
                        opening, mask[lower : lower + 3, pl.ds(tiles[side], 1)][:, 0], embed[...]
                    )
                    closing = keyed_rows(
                        closing, mask[upper : upper + 3, pl.ds(tiles[side], 1)][:, 0], embed[...]
                    )
                tokens = jnp.concatenate(
                    [opening.reshape(48, 512), closing.reshape(48, 512)], axis=0
                )
                strip = dot(perm[0], tokens.astype(BF16))
                if index == 0:
                    strip = strip * 0.125
                packed[side, index, band - 1] = strip.astype(BF16)
            send_off(side, index).start()
        if side == 0:
            for end in range(2):
                row = ends[end][1]
                for index in range(4):
                    rows_in(end, index).wait()
                    if index == 1:
                        keyed = keyed_rows(
                            rows[end, 1].astype(F32), mask[row : row + 3], embed[...]
                        )
                        rows[end, 1] = keyed.astype(BF16)
                    rows_out(end, index).start()
    for index in range(4):
        for side in range(2):
            send_off(side, index).wait()
        for end in range(2):
            rows_out(end, index).wait()


def pack_edges(arrays, mask, embed, far_perm, near_perm, core):
    tiles = [array.reshape(2, 48, 3, 8, 512) for array in arrays]
    anywhere = pl.BlockSpec(memory_space=pl.ANY)
    strips = jax.ShapeDtypeStruct((4, 7, STRIP, 512), BF16)
    ends = jax.ShapeDtypeStruct((4, 2, 3, 3, 8, 512), BF16)
    return pl.pallas_call(
        edges_body,
        grid_spec=pltpu.PrefetchScalarGridSpec(
            num_scalar_prefetch=1,
            grid=(1,),
            in_specs=[anywhere] * 4
            + [
                fixed_spec((48, 3, 8, 128)),
                fixed_spec((1, 512)),
                side_spec((STRIP, 96)),
                side_spec((STRIP, 96)),
            ],
            out_specs=[anywhere] * 4,
            scratch_shapes=[
                pltpu.VMEM((2, 4, 2, 48, 8, 512), BF16),
                pltpu.VMEM((2, 4, 7, STRIP, 512), BF16),
                pltpu.VMEM((2, 4, 2, 3, 3, 8, 512), BF16),
                pltpu.SemaphoreType.DMA((2, 4)),
                pltpu.SemaphoreType.DMA((2, 4)),
                pltpu.SemaphoreType.DMA((2, 4)),
                pltpu.SemaphoreType.DMA((2, 4)),
            ],
        ),
        out_shape=[strips, strips, ends, ends],
        compiler_params=params(),
        cost_estimate=pl.CostEstimate(
            flops=2 * 56 * STRIP * 96 * 512, bytes_accessed=16 * MIB, transcendentals=0
        ),
        name="pack_edges",
    )(core, *tiles, mask, embed, far_perm, near_perm)


def corners_body(core, top, bottom, below, above, perm, done, far, near, mid):
    for index in range(4):
        for place, (first, second) in enumerate(((top, above), (below, bottom))):
            first = first[index].astype(F32)
            second = second[index].astype(F32)
            tokens = jnp.concatenate([first[0], first[1], second[0], second[1]], axis=0)
            strips = dot(perm[0], tokens.astype(BF16))
            if index == 0:
                strips = strips * 0.125
            far[index, place] = strips[:STRIP].astype(BF16)
            near[index, place] = strips[STRIP : 2 * STRIP].astype(BF16)
            mid[index, place] = strips[2 * STRIP :].astype(BF16)


def pack_corners(top, bottom, below, above, perm, core, done):
    sizes = (STRIP, STRIP, WIN)
    return pl.pallas_call(
        corners_body,
        grid_spec=pltpu.PrefetchScalarGridSpec(
            num_scalar_prefetch=1,
            grid=(1,),
            in_specs=[fixed_spec((4, 2, STRIP, 512))] * 4
            + [side_spec((2 * WIN, 2 * WIN)), pl.BlockSpec(memory_space=pl.ANY)],
            out_specs=[fixed_spec((4, 2, size, 512)) for size in sizes],
        ),
        out_shape=[jax.ShapeDtypeStruct((4, 2, size, 512), BF16) for size in sizes],
        compiler_params=params(),
        cost_estimate=pl.CostEstimate(
            flops=2 * 8 * 288 * 288 * 512, bytes_accessed=5 * MIB, transcendentals=0
        ),
        name="pack_corners",
    )(core, top, bottom, below, above, perm, done)


def windows(win, slots, bias, scores, grads, low, dlow, store):
    lane = lax.broadcasted_iota(jnp.int32, (1, GROUP), 1) // 64

    def spread(x):
        return jnp.concatenate(
            [x * jnp.where(lane == h, 1.0, 0.0).astype(BF16) for h in range(4)], axis=0
        )

    def by_head(wide):
        total = None
        for h in range(4):
            piece = jnp.where(lane == h, wide[WIN * h : WIN * (h + 1)], 0.0)
            total = piece if total is None else total + piece
        return total

    jobs = []
    for slot in range(slots):
        for group in range(2):
            cols = slice(GROUP * group, GROUP * (group + 1))
            q, k, v, g = (win[slot, index, :, cols] for index in range(4))
            q_wide, g_wide = spread(q), spread(g)
            place = 2 * slot + group
            scores[place] = dot(k, q_wide, 1, 1)
            grads[place] = dot(v, g_wide, 1, 1)
            jobs.append((slot, group, place, cols, k, v, q_wide, g_wide))
    for slot, group, place, cols, k, v, q_wide, g_wide in jobs:
        for start in range(0, 576, 128):
            part = slice(start, min(start + 128, 576))
            s = scores[place, :, part] + bias[0, group, :, part]
            e = jnp.exp(s - jnp.max(s, axis=0, keepdims=True))
            p = e * (1.0 / jnp.sum(e, axis=0, keepdims=True))
            gp = grads[place, :, part]
            delta = jnp.sum(p * gp, axis=0, keepdims=True)
            low[place, :, part] = p.astype(BF16)
            dlow[place, :, part] = (p * (gp - delta)).astype(BF16)
        p_low, d_low = low[place], dlow[place]
        store(slot, 0, cols, by_head(dot(p_low, v, 0, 0)))
        store(slot, 1, cols, by_head(dot(d_low, k, 0, 0)) * 0.125)
        store(slot, 2, cols, dot(d_low, q_wide))
        store(slot, 3, cols, dot(p_low, g_wide))


def place_pair(win, slot, own, halo, own_left):
    def put(left, right):
        for index in range(4):
            both = jnp.concatenate(
                [left[index, 0].astype(F32), right[index, 0].astype(F32)], axis=0
            )
            win[slot, index] = both.astype(BF16)

    @pl.when(own_left)
    def _():
        put(own, halo)

    @pl.when(jnp.logical_not(own_left))
    def _():
        put(halo, own)


def inner_body(core, q0, q1, k0, k1, v0, v1, g0, g1, m0, m1, embed, perm, own, halo, bias, back, *rest):
    outs, token, (win, result, ready, gone), work = rest[:4], rest[4], rest[5:9], rest[9:]
    s = pl.program_id(0)
    for index, pair in enumerate(((q0, q1), (k0, k1), (v0, v1), (g0, g1))):
        first, second = (source[:, 0].astype(F32) for source in pair)
        if index == 1:
            first = keyed_rows(first, m0[...].reshape(STRIP, 128), embed[...])
            second = keyed_rows(second, m1[...].reshape(STRIP, 128), embed[...])
        tokens = jnp.concatenate([first[0], first[1], second[0], second[1]], axis=0)
        packed = dot(perm[...], tokens.astype(BF16))
        if index == 0:
            packed = packed * 0.125
        win[0, index] = packed.astype(BF16)
    place_pair(win, 1, own, halo, core[0] == 0)

    starts = (pl.multiple_of(WIN * core[0], 16), pl.multiple_of(WIN * (1 - core[0]), 16))

    def keep(slot, index, cols, value):
        result[index, pl.ds(starts[slot], WIN), cols] = value.astype(BF16)

    windows(win, 2, bias, *work, keep)

    def leave(slot, step):
        copies = []
        for index, out in enumerate(outs):
            for part in range(2):
                copies.append(
                    pltpu.make_async_copy(
                        ready.at[slot, index, part],
                        out.at[:, 2 * step + 2 - part],
                        gone.at[slot, index, part],
                    )
                )
        return copies

    slot = s % 2

    @pl.when(s >= 2)
    def _():
        for copy in leave(slot, s - 2):
            copy.wait()

    used = pl.ds(pl.multiple_of(64 * core[0], 16), 224)
    for index in range(4):
        full = dot(back[0], result[index, used])
        ready[slot, index] = full.reshape(2, 2, STRIP, 512).astype(BF16)
    for copy in leave(slot, s):
        copy.start()

    @pl.when(s == 6)
    def _():
        token[...] = jnp.zeros_like(token)
        for copy in leave(1, 5) + leave(0, 6):
            copy.wait()


def work_scratch(places):
    return [
        pltpu.VMEM((places, WIN, 576), F32),
        pltpu.VMEM((places, WIN, 576), F32),
        pltpu.VMEM((places, WIN, 576), BF16),
        pltpu.VMEM((places, WIN, 576), BF16),
    ]


def window_cost(count, moved):
    return pl.CostEstimate(
        flops=count * 6 * 2 * WIN * WIN * 512 * 4,
        bytes_accessed=moved,
        transcendentals=count * 8 * WIN * WIN,
    )


def inner(arrays, mask, embed, perm, own, halo, bias, back, core):
    operands, specs = [], []
    block = (2, 1, STRIP, 512)
    for array in arrays:
        array = array.reshape(2, 16, STRIP, 512)
        operands += [array, array]
        specs += [
            pl.BlockSpec(block, lambda s, core: (0, 2 * s + 2, 0, 0)),
            pl.BlockSpec(block, lambda s, core: (0, 2 * s + 1, 0, 0)),
        ]
    anywhere = pl.BlockSpec(memory_space=pl.ANY)
    return pl.pallas_call(
        inner_body,
        grid_spec=pltpu.PrefetchScalarGridSpec(
            num_scalar_prefetch=1,
            grid=(7,),
            in_specs=specs
            + [
                pl.BlockSpec((3, 3, 8, 128), lambda s, core: (2 * s + 2, 0, 0, 0)),
                pl.BlockSpec((3, 3, 8, 128), lambda s, core: (2 * s + 1, 0, 0, 0)),
                fixed_spec((1, 512)),
                fixed_spec((WIN, 2 * WIN)),
                band_spec(),
                band_spec(),
                fixed_spec((1, 2, WIN, 576)),
                side_spec((2 * WIN, 224)),
            ],
            out_specs=[anywhere] * 4 + [fixed_spec((8, 128))],
            scratch_shapes=[
                pltpu.VMEM((2, 4, WIN, 512), BF16),
                pltpu.VMEM((4, 2 * WIN, 512), BF16),
                pltpu.VMEM((2, 4, 2, 2, STRIP, 512), BF16),
                pltpu.SemaphoreType.DMA((2, 4, 2)),
            ]
            + work_scratch(4),
        ),
        out_shape=[jax.ShapeDtypeStruct((2, 16, STRIP, 512), BF16)] * 4
        + [jax.ShapeDtypeStruct((8, 128), F32)],
        compiler_params=params(),
        cost_estimate=window_cost(14, 24 * MIB),
        name="inner_windows",
    )(core, *operands, mask, mask, embed, perm, own, halo, bias, back)


def band_spec():
    return pl.BlockSpec((4, 1, STRIP, 512), lambda s, core: (0, s, 0, 0))


def outer_body(core, own, halo, bias, back, p0, p1, p2, p3, o0, o1, o2, o3, win, result, tiles, came, gone, *work):
    s = pl.program_id(0)
    tile = 2 * core[0]
    outs = (o0, o1, o2, o3)

    def arrivals():
        return [
            pltpu.make_async_copy(out.at[:, 3:45, tile], tiles.at[index], came.at[index])
            for index, out in enumerate(outs)
        ]

    @pl.when(s == 0)
    def _():
        for copy in arrivals():
            copy.start()

    place_pair(win, 0, own, halo, core[0] == 1)

    def keep(slot, index, cols, value):
        result[index, :, cols] = value.astype(BF16)

    windows(win, 1, bias, *work, keep)

    @pl.when(s == 0)
    def _():
        for copy in arrivals():
            copy.wait()

    used = pl.ds(pl.multiple_of(64 * (1 - core[0]), 16), 80)

    def leave(step, index):
        return pltpu.make_async_copy(
            tiles.at[index, :, pl.ds(6 * step, 6)],
            outs[index].at[:, pl.ds(6 * step + 3, 6), tile],
            gone.at[step, index],
        )

    for index in range(4):
        full = dot(back[0], result[index, used]).reshape(2, 2, 3, 8, 512)
        for part in range(2):
            span = pl.ds(6 * s + 3 * (1 - part), 3)
            total = tiles[index, :, span].astype(F32) + full[part]
            tiles[index, :, span] = total.astype(BF16)
        leave(s, index).start()

    @pl.when(s == 6)
    def _():
        for index in range(4):
            for step in range(7):
                leave(step, index).wait()


def outer(partial, own, halo, bias, back, core):
    anywhere = pl.BlockSpec(memory_space=pl.ANY)
    shape = (2, 48, 3, 8, 512)
    return pl.pallas_call(
        outer_body,
        grid_spec=pltpu.PrefetchScalarGridSpec(
            num_scalar_prefetch=1,
            grid=(7,),
            in_specs=[
                band_spec(),
                band_spec(),
                fixed_spec((1, 2, WIN, 576)),
                side_spec((96, 80)),
            ]
            + [anywhere] * 4,
            out_specs=[anywhere] * 4,
            scratch_shapes=[
                pltpu.VMEM((1, 4, WIN, 512), BF16),
                pltpu.VMEM((4, WIN, 512), BF16),
                pltpu.VMEM((4, 2, 42, 8, 512), BF16),
                pltpu.SemaphoreType.DMA((4,)),
                pltpu.SemaphoreType.DMA((7, 4)),
            ]
            + work_scratch(2),
        ),
        out_shape=[jax.ShapeDtypeStruct(shape, BF16)] * 4,
        input_output_aliases={5 + index: index for index in range(4)},
        compiler_params=params(),
        cost_estimate=window_cost(7, 12 * MIB),
        name="outer_windows",
    )(core, own, halo, bias, back, *[x.reshape(shape) for x in partial])


def corner_body(core, flags, mid, near, near_halo, far, far_halo, bias, back, p0, p1, p2, p3, o0, o1, o2, o3, win, result, cut, *work):
    s = pl.program_id(0)
    left = core[0] == 0
    for index in range(4):
        win[1, index] = mid[index, 0]
    place_pair(win, 0, far, far_halo, jnp.logical_not(left))
    place_pair(win, 2, near, near_halo, left)

    key_part = lax.broadcasted_iota(jnp.int32, (WIN, 576), 0) % STRIP < HALF
    query_part = lax.broadcasted_iota(jnp.int32, (WIN, 576), 1) % STRIP < HALF
    apart = (key_part != query_part) & (flags[s] != 0)
    for group in range(2):
        cut[0, group] = jnp.where(apart, -jnp.inf, bias[0, group])

    starts = (
        pl.multiple_of(2 * WIN * core[0], 16),
        WIN,
        pl.multiple_of(2 * WIN * (1 - core[0]), 16),
    )

    def keep(slot, index, cols, value):
        result[index, pl.ds(starts[slot], WIN), cols] = value.astype(BF16)

    windows(win, 3, cut, *work, keep)
    for index, out in enumerate((o0, o1, o2, o3)):
        full = dot(back[0], result[index, 64:368])
        out[:, 0] = full.reshape(2, STRIP, 512).astype(BF16)


def corners(partial, flags, mid, near, near_halo, far, far_halo, bias, back, core):
    anywhere = pl.BlockSpec(memory_space=pl.ANY)
    shape = (2, 16, STRIP, 512)

    def edge(size):
        return pl.BlockSpec((4, 1, size, 512), lambda s, core, flags: (0, s, 0, 0))

    return pl.pallas_call(
        corner_body,
        grid_spec=pltpu.PrefetchScalarGridSpec(
            num_scalar_prefetch=2,
            grid=(2,),
            in_specs=[
                edge(WIN),
                edge(STRIP),
                edge(STRIP),
                edge(STRIP),
                edge(STRIP),
                pl.BlockSpec((1, 2, WIN, 576), lambda s, core, flags: (0, 0, 0, 0)),
                pl.BlockSpec((1, WIN, 304), lambda s, core, flags: (s, 0, 0)),
            ]
            + [anywhere] * 4,
            out_specs=[
                pl.BlockSpec((2, 1, STRIP, 512), lambda s, core, flags: (0, 15 * s, 0, 0))
            ]
            * 4,
            scratch_shapes=[
                pltpu.VMEM((3, 4, WIN, 512), BF16),
                pltpu.VMEM((4, 3 * WIN, 512), BF16),
                pltpu.VMEM((1, 2, WIN, 576), F32),
            ]
            + work_scratch(6),
        ),
        out_shape=[jax.ShapeDtypeStruct(shape, BF16)] * 4,
        input_output_aliases={9 + index: index for index in range(4)},
        compiler_params=params(),
        cost_estimate=window_cost(6, 8 * MIB),
        name="corner_windows",
    )(
        core, flags, mid, near, near_halo, far, far_halo, bias, back,
        *[x.reshape(shape) for x in partial],
    )


def bias_body(table, hot, squeeze, out, wide, part):
    for head in range(8):
        line = jnp.broadcast_to(table[head : head + 1], (8, 768))
        line = pltpu.roll(line, 0, 1, stride=1, stride_axis=0)
        for run, base in enumerate(run_bases()):
            turn = int(base - 379) % 768
            turned = pltpu.roll(line, turn, 1)
            group, cols = head // 4, slice(384 * (head % 4), 384 * (head % 4) + 384)
            wide[group, 8 * run : 8 * run + 8, cols] = turned[:, :384]
    for group in range(2):
        high = wide[group].astype(BF16)
        part[0, group] = high
        part[1, group] = (wide[group] - high.astype(F32)).astype(BF16)
    for group in range(2):
        total = None
        for order in range(2):
            spread = dot(part[order, group], hot[...]).astype(BF16)
            piece = dot(squeeze[...], spread)
            total = piece if total is None else total + piece
        out[0, group] = total


def window_bias(rel_table):
    tokens = (run_bases()[:, None] + np.arange(6)).reshape(WIN)
    hot = np.zeros((4, 384, 4, WIN), np.float32)
    for head in range(4):
        hot[head, tokens, head, np.arange(WIN)] = 1
    squeeze = np.zeros((24, 6, 24, 8), np.float32)
    for run in range(24):
        squeeze[run, np.arange(6), run, np.arange(6)] = 1
    hot = jnp.asarray(hot.reshape(4 * 384, 4 * WIN), BF16)
    squeeze = jnp.asarray(squeeze.reshape(WIN, 192), BF16)
    table = jnp.pad(rel_table, ((0, 0), (0, 768 - rel_table.shape[1])))
    return pl.pallas_call(
        bias_body,
        out_shape=jax.ShapeDtypeStruct((1, 2, WIN, 576), F32),
        scratch_shapes=[
            pltpu.VMEM((2, 192, 4 * 384), F32),
            pltpu.VMEM((2, 2, 192, 4 * 384), BF16),
        ],
        compiler_params=params(),
        cost_estimate=pl.CostEstimate(
            flops=4 * 2 * 192 * 1536 * 576, bytes_accessed=3 * MIB, transcendentals=0
        ),
        name="window_bias",
    )(table, hot, squeeze)


def side_tables():
    far_strip, near_strip = (0, 3), (3, 0)
    far, near, whole, near_back, far_back = [], [], [], [], []
    for side in range(2):
        far.append(far_matrix(far_strip[side], 2 * side))
        near.append(far_matrix(near_strip[side], 2 - 2 * side))
        whole.append(strip_matrix([far_strip[side], near_strip[side], 1, 2]))
        own = strip_matrix([near_strip[side]]).T
        middle = strip_matrix([1, 2]).T
        pad = np.zeros((2 * WIN, 8), np.float32)
        pad_far = np.zeros((96, 8), np.float32)
        if side == 0:
            near_back.append(np.concatenate([middle, own, pad], axis=1))
            far_back.append(np.concatenate([pad_far, far[0].T], axis=1))
        else:
            near_back.append(np.concatenate([pad, own, middle], axis=1))
            far_back.append(np.concatenate([far[1].T, pad_far], axis=1))
    natural = strip_matrix([0, 1, 2, 3]).T.reshape(2, WIN, 2 * WIN)
    corner_back = np.pad(natural, ((0, 0), (0, 0), (8, 8)))
    stacked = (far, near, whole, near_back, far_back, corner_back)
    return [jnp.asarray(np.stack(table), BF16) for table in stacked]


def shards(queries, key_tokens, value_tokens, out_grad, land_mask, land_embed, rel_table):
    lev, rows, cols, width = queries.shape
    lat = lax.axis_index("lat")
    core = jnp.reshape(lax.axis_index("lon") % 2, (1,))
    bands = lax.axis_size("lat")
    sectors = lax.axis_size("lon")
    arrays = (queries, key_tokens, value_tokens, out_grad)
    mask = jnp.broadcast_to(
        land_mask.astype(F32).reshape(rows, 3, 8, 1), (rows, 3, 8, 128)
    )
    embed = land_embed.reshape(1, width)
    far_perm, near_perm, all_perm, near_back, far_back, corner_back = side_tables()
    mid_perm = jnp.asarray(strip_matrix([1, 2]), BF16)

    to_far = [((2 * k + 1) % sectors, (2 * k + 2) % sectors) for k in range(sectors // 2)]
    to_far += [(b, a) for a, b in to_far]
    to_near = [(i, i ^ 1) for i in range(sectors)]

    far, near, top, bottom = pack_edges(arrays, mask, embed, far_perm, near_perm, core)
    ends = (4, 2, STRIP, width)
    top, bottom = top.reshape(ends), bottom.reshape(ends)
    far_halo = lax.ppermute(far, "lon", to_far)
    near_halo = lax.ppermute(near, "lon", to_near)
    below = lax.ppermute(top, "lat", [(i, i - 1) for i in range(1, bands)])
    above = lax.ppermute(bottom, "lat", [(i, i + 1) for i in range(bands - 1)])

    bias = window_bias(rel_table)
    *partial, done = inner(
        arrays, mask, embed, mid_perm, near, near_halo, bias, near_back, core
    )

    far_c, near_c, mid_c = pack_corners(top, bottom, below, above, all_perm, core, done)
    far_halo_c = lax.ppermute(far_c, "lon", to_far)
    near_halo_c = lax.ppermute(near_c, "lon", to_near)

    partial = outer(partial, far, far_halo, bias, far_back, core)
    flags = jnp.stack([lat == 0, lat == bands - 1]).astype(jnp.int32)
    final = corners(
        partial, flags, mid_c, near_c, near_halo_c, far_c, far_halo_c, bias, corner_back, core
    )
    return tuple(x.reshape(queries.shape) for x in final)


def solution(mesh):
    tokens = P(None, "lat", "lon", None)
    return jax.shard_map(
        shards,
        mesh=mesh,
        in_specs=(tokens, tokens, tokens, tokens, P("lat", "lon"), P(), P()),
        out_specs=(tokens,) * 4,
        check_vma=False,
    )
```

```python
import functools

import jax
import jax.numpy as jnp
import numpy as np
from jax import lax
from jax.experimental import pallas as pl
from jax.experimental.pallas import tpu as pltpu
from jax.sharding import PartitionSpec as P

F32 = jnp.float32
BF16 = jnp.bfloat16
HALF = 36
STRIP = 72
WIN = 144
GROUP = 256
MIB = 1 << 20
VMEM_BYTES = 63 * MIB


def strip_matrix(strips):
    out = np.zeros((len(strips), 2, 2, 3, 6, 2, 2, 3, 24), np.float32)
    for place, strip in enumerate(strips):
        for part in range(2):
            for lev in range(2):
                for row in range(3):
                    for col in range(6):
                        out[place, part, lev, row, col, part, lev, row, 6 * strip + col] = 1
    return out.reshape(len(strips) * STRIP, 2 * WIN)


def far_matrix(strip, tile):
    full = strip_matrix([strip]).reshape(STRIP, 2, 2, 3, 3, 8)
    return full[:, :, :, :, tile].reshape(STRIP, 96)


def run_bases():
    run = np.arange(24)
    half, part, lev, row = run // 12, run // 6 % 2, run // 3 % 2, run % 3
    return lev * 253 + (row + 3 * (1 - part)) * 23 + 6 * half


def dot(a, b, ca=1, cb=0):
    return lax.dot_general(a, b, (((ca,), (cb,)), ((), ())), preferred_element_type=F32)


def keyed_rows(key, mask, embed):
    wide = jnp.concatenate([mask] * 4, axis=-1)
    return (key + (wide * embed)[None]).astype(BF16).astype(F32)


def side_spec(shape):
    return pl.BlockSpec((1, *shape), lambda s, core: (core[0],) + (0,) * len(shape))


def fixed_spec(shape):
    return pl.BlockSpec(shape, lambda s, core: (0,) * len(shape))


def params():
    return pltpu.CompilerParams(vmem_limit_bytes=VMEM_BYTES)


def edges_body(core, q, k, v, g, mask, embed, far_perm, near_perm, far, near, top, bottom, held, packed, rows, came, gone, rows_came, rows_gone):
    sources = (q, k, v, g)
    tiles = (2 * core[0], 2 - 2 * core[0])

    def fetch(side, index):
        return pltpu.make_async_copy(
            sources[index].at[:, :, tiles[side]], held.at[side, index], came.at[side, index]
        )

    def send_off(side, index):
        return pltpu.make_async_copy(
            packed.at[side, index], (far, near)[side].at[index], gone.at[side, index]
        )

    ends = ((top, 0), (bottom, 45))

    def rows_in(end, index):
        row = ends[end][1]
        return pltpu.make_async_copy(
            sources[index].at[:, row : row + 3], rows.at[end, index], rows_came.at[end, index]
        )

    def rows_out(end, index):
        return pltpu.make_async_copy(
            rows.at[end, index], ends[end][0].at[index], rows_gone.at[end, index]
        )

    for index in range(4):
        fetch(0, index).start()
    for end in range(2):
        for index in range(4):
            rows_in(end, index).start()
    for index in range(4):
        fetch(1, index).start()
    for side in range(2):
        perm = (far_perm, near_perm)[side]
        for index in range(4):
            fetch(side, index).wait()
            for band in range(1, 8):
                lower, upper = 6 * band, 6 * band - 3
                opening = held[side, index, :, lower : lower + 3].astype(F32)
                closing = held[side, index, :, upper : upper + 3].astype(F32)
                if index == 1:
                    opening = keyed_rows(
                        opening, mask[lower : lower + 3, pl.ds(tiles[side], 1)][:, 0], embed[...]
                    )
                    closing = keyed_rows(
                        closing, mask[upper : upper + 3, pl.ds(tiles[side], 1)][:, 0], embed[...]
                    )
                tokens = jnp.concatenate(
                    [opening.reshape(48, 512), closing.reshape(48, 512)], axis=0
                )
                strip = dot(perm[0], tokens.astype(BF16))
                if index == 0:
                    strip = strip * 0.125
                packed[side, index, band - 1] = strip.astype(BF16)
            send_off(side, index).start()
        if side == 0:
            for end in range(2):
                row = ends[end][1]
                for index in range(4):
                    rows_in(end, index).wait()
                    if index == 1:
                        keyed = keyed_rows(
                            rows[end, 1].astype(F32), mask[row : row + 3], embed[...]
                        )
                        rows[end, 1] = keyed.astype(BF16)
                    rows_out(end, index).start()
    for index in range(4):
        for side in range(2):
            send_off(side, index).wait()
        for end in range(2):
            rows_out(end, index).wait()


def pack_edges(arrays, mask, embed, far_perm, near_perm, core):
    tiles = [array.reshape(2, 48, 3, 8, 512) for array in arrays]
    anywhere = pl.BlockSpec(memory_space=pl.ANY)
    strips = jax.ShapeDtypeStruct((4, 7, STRIP, 512), BF16)
    ends = jax.ShapeDtypeStruct((4, 2, 3, 3, 8, 512), BF16)
    return pl.pallas_call(
        edges_body,
        grid_spec=pltpu.PrefetchScalarGridSpec(
            num_scalar_prefetch=1,
            grid=(1,),
            in_specs=[anywhere] * 4
            + [
                fixed_spec((48, 3, 8, 128)),
                fixed_spec((1, 512)),
                side_spec((STRIP, 96)),
                side_spec((STRIP, 96)),
            ],
            out_specs=[anywhere] * 4,
            scratch_shapes=[
                pltpu.VMEM((2, 4, 2, 48, 8, 512), BF16),
                pltpu.VMEM((2, 4, 7, STRIP, 512), BF16),
                pltpu.VMEM((2, 4, 2, 3, 3, 8, 512), BF16),
                pltpu.SemaphoreType.DMA((2, 4)),
                pltpu.SemaphoreType.DMA((2, 4)),
                pltpu.SemaphoreType.DMA((2, 4)),
                pltpu.SemaphoreType.DMA((2, 4)),
            ],
        ),
        out_shape=[strips, strips, ends, ends],
        compiler_params=params(),
        cost_estimate=pl.CostEstimate(
            flops=2 * 56 * STRIP * 96 * 512, bytes_accessed=16 * MIB, transcendentals=0
        ),
        name="pack_edges",
    )(core, *tiles, mask, embed, far_perm, near_perm)


def corners_body(core, top, bottom, below, above, perm, done, far, near, mid):
    for index in range(4):
        for place, (first, second) in enumerate(((top, above), (below, bottom))):
            first = first[index].astype(F32)
            second = second[index].astype(F32)
            tokens = jnp.concatenate([first[0], first[1], second[0], second[1]], axis=0)
            strips = dot(perm[0], tokens.astype(BF16))
            if index == 0:
                strips = strips * 0.125
            far[index, place] = strips[:STRIP].astype(BF16)
            near[index, place] = strips[STRIP : 2 * STRIP].astype(BF16)
            mid[index, place] = strips[2 * STRIP :].astype(BF16)


def pack_corners(top, bottom, below, above, perm, core, done):
    sizes = (STRIP, STRIP, WIN)
    return pl.pallas_call(
        corners_body,
        grid_spec=pltpu.PrefetchScalarGridSpec(
            num_scalar_prefetch=1,
            grid=(1,),
            in_specs=[fixed_spec((4, 2, STRIP, 512))] * 4
            + [side_spec((2 * WIN, 2 * WIN)), pl.BlockSpec(memory_space=pl.ANY)],
            out_specs=[fixed_spec((4, 2, size, 512)) for size in sizes],
        ),
        out_shape=[jax.ShapeDtypeStruct((4, 2, size, 512), BF16) for size in sizes],
        compiler_params=params(),
        cost_estimate=pl.CostEstimate(
            flops=2 * 8 * 288 * 288 * 512, bytes_accessed=5 * MIB, transcendentals=0
        ),
        name="pack_corners",
    )(core, top, bottom, below, above, perm, done)


def windows(win, slots, bias, scores, grads, low, dlow, store):
    lane = lax.broadcasted_iota(jnp.int32, (1, GROUP), 1) // 64

    def spread(x):
        return jnp.concatenate(
            [x * jnp.where(lane == h, 1.0, 0.0).astype(BF16) for h in range(4)], axis=0
        )

    def by_head(wide):
        total = None
        for h in range(4):
            piece = jnp.where(lane == h, wide[WIN * h : WIN * (h + 1)], 0.0)
            total = piece if total is None else total + piece
        return total

    jobs = []
    for slot in range(slots):
        for group in range(2):
            cols = slice(GROUP * group, GROUP * (group + 1))
            q, k, v, g = (win[slot, index, :, cols] for index in range(4))
            q_wide, g_wide = spread(q), spread(g)
            place = 2 * slot + group
            scores[place] = dot(k, q_wide, 1, 1)
            grads[place] = dot(v, g_wide, 1, 1)
            jobs.append((slot, group, place, cols, k, v, q_wide, g_wide))
    for slot, group, place, cols, k, v, q_wide, g_wide in jobs:
        for start in range(0, 576, 128):
            part = slice(start, min(start + 128, 576))
            s = scores[place, :, part] + bias[0, group, :, part]
            e = jnp.exp(s - jnp.max(s, axis=0, keepdims=True))
            p = e * (1.0 / jnp.sum(e, axis=0, keepdims=True))
            gp = grads[place, :, part]
            delta = jnp.sum(p * gp, axis=0, keepdims=True)
            low[place, :, part] = p.astype(BF16)
            dlow[place, :, part] = (p * (gp - delta)).astype(BF16)
        p_low, d_low = low[place], dlow[place]
        store(slot, 0, cols, by_head(dot(p_low, v, 0, 0)))
        store(slot, 1, cols, by_head(dot(d_low, k, 0, 0)) * 0.125)
        store(slot, 2, cols, dot(d_low, q_wide))
        store(slot, 3, cols, dot(p_low, g_wide))


def place_pair(win, slot, own, halo, own_left):
    def put(left, right):
        for index in range(4):
            both = jnp.concatenate(
                [left[index, 0].astype(F32), right[index, 0].astype(F32)], axis=0
            )
            win[slot, index] = both.astype(BF16)

    @pl.when(own_left)
    def _():
        put(own, halo)

    @pl.when(jnp.logical_not(own_left))
    def _():
        put(halo, own)


def inner_body(core, q0, q1, k0, k1, v0, v1, g0, g1, m0, m1, embed, perm, own, halo, bias, back, *rest):
    outs, beside, token, (win, result, ready, gone), work = rest[:4], rest[4], rest[5], rest[6:10], rest[10:]
    s = pl.program_id(0)
    for index, pair in enumerate(((q0, q1), (k0, k1), (v0, v1), (g0, g1))):
        first, second = (source[:, 0].astype(F32) for source in pair)
        if index == 1:
            first = keyed_rows(first, m0[...].reshape(STRIP, 128), embed[...])
            second = keyed_rows(second, m1[...].reshape(STRIP, 128), embed[...])
        tokens = jnp.concatenate([first[0], first[1], second[0], second[1]], axis=0)
        packed = dot(perm[...], tokens.astype(BF16))
        if index == 0:
            packed = packed * 0.125
        win[0, index] = packed.astype(BF16)
    place_pair(win, 1, own, halo, core[0] == 0)

    starts = (pl.multiple_of(WIN * core[0], 16), pl.multiple_of(WIN * (1 - core[0]), 16))

    def keep(slot, index, cols, value):
        result[index, pl.ds(starts[slot], WIN), cols] = value.astype(BF16)

    windows(win, 2, bias, *work, keep)

    def leave(slot, step):
        copies = []
        for index, out in enumerate(outs):
            for part in range(2):
                copies.append(
                    pltpu.make_async_copy(
                        ready.at[slot, index, part],
                        out.at[:, 2 * step + 2 - part],
                        gone.at[slot, index, part],
                    )
                )
        return copies

    slot = s % 2

    @pl.when(s >= 2)
    def _():
        for copy in leave(slot, s - 2):
            copy.wait()

    used = pl.ds(pl.multiple_of(64 * core[0], 16), 224)
    near_far = pl.ds(pl.multiple_of(208 * core[0], 16), 80)
    for index in range(4):
        beside[index, 0] = result[index, near_far]
        full = dot(back[0], result[index, used])
        ready[slot, index] = full.reshape(2, 2, STRIP, 512).astype(BF16)
    for copy in leave(slot, s):
        copy.start()

    @pl.when(s == 6)
    def _():
        token[...] = jnp.zeros_like(token)
        for copy in leave(1, 5) + leave(0, 6):
            copy.wait()


def work_scratch(places):
    return [
        pltpu.VMEM((places, WIN, 576), F32),
        pltpu.VMEM((places, WIN, 576), F32),
        pltpu.VMEM((places, WIN, 576), BF16),
        pltpu.VMEM((places, WIN, 576), BF16),
    ]


def window_cost(count, moved):
    return pl.CostEstimate(
        flops=count * 6 * 2 * WIN * WIN * 512 * 4,
        bytes_accessed=moved,
        transcendentals=count * 8 * WIN * WIN,
    )


def inner(arrays, mask, embed, perm, own, halo, bias, back, core):
    operands, specs = [], []
    block = (2, 1, STRIP, 512)
    for array in arrays:
        array = array.reshape(2, 16, STRIP, 512)
        operands += [array, array]
        specs += [
            pl.BlockSpec(block, lambda s, core: (0, 2 * s + 2, 0, 0)),
            pl.BlockSpec(block, lambda s, core: (0, 2 * s + 1, 0, 0)),
        ]
    anywhere = pl.BlockSpec(memory_space=pl.ANY)
    return pl.pallas_call(
        inner_body,
        grid_spec=pltpu.PrefetchScalarGridSpec(
            num_scalar_prefetch=1,
            grid=(7,),
            in_specs=specs
            + [
                pl.BlockSpec((3, 3, 8, 128), lambda s, core: (2 * s + 2, 0, 0, 0)),
                pl.BlockSpec((3, 3, 8, 128), lambda s, core: (2 * s + 1, 0, 0, 0)),
                fixed_spec((1, 512)),
                fixed_spec((WIN, 2 * WIN)),
                band_spec(),
                band_spec(),
                fixed_spec((1, 2, WIN, 576)),
                side_spec((2 * WIN, 224)),
            ],
            out_specs=[anywhere] * 4
            + [
                pl.BlockSpec((4, 1, 80, 512), lambda s, core: (0, s, 0, 0)),
                fixed_spec((8, 128)),
            ],
            scratch_shapes=[
                pltpu.VMEM((2, 4, WIN, 512), BF16),
                pltpu.VMEM((4, 2 * WIN, 512), BF16),
                pltpu.VMEM((2, 4, 2, 2, STRIP, 512), BF16),
                pltpu.SemaphoreType.DMA((2, 4, 2)),
            ]
            + work_scratch(4),
        ),
        out_shape=[jax.ShapeDtypeStruct((2, 16, STRIP, 512), BF16)] * 4
        + [jax.ShapeDtypeStruct((4, 7, 80, 512), BF16), jax.ShapeDtypeStruct((8, 128), F32)],
        compiler_params=params(),
        cost_estimate=window_cost(14, 24 * MIB),
        name="inner_windows",
    )(core, *operands, mask, mask, embed, perm, own, halo, bias, back)


def band_spec(first=0):
    return pl.BlockSpec((4, 1, STRIP, 512), lambda s, core: (0, s + first, 0, 0))


def outer_body(first, count, core, own, halo, beside, bias, back, p0, p1, p2, p3, o0, o1, o2, o3, token, win, result, tiles, gone, *work):
    s = pl.program_id(0)
    tile = 2 * core[0]
    outs = (o0, o1, o2, o3)
    place_pair(win, 0, own, halo, core[0] == 1)

    def keep(slot, index, cols, value):
        result[index, 0:WIN, cols] = value.astype(BF16)

    windows(win, 1, bias, *work, keep)

    def leave(step, index):
        return pltpu.make_async_copy(
            tiles.at[index, :, pl.ds(6 * step, 6)],
            outs[index].at[:, pl.ds(6 * (step + first) + 3, 6), tile],
            gone.at[step, index],
        )

    used = pl.ds(pl.multiple_of(64 * (1 - core[0]), 16), 160)
    beside_at = pl.ds(pl.multiple_of(WIN - 64 * core[0], 16), 80)
    for index in range(4):
        result[index, beside_at] = beside[index, 0]
        full = dot(back[0], result[index, used]).reshape(2, 2, 3, 8, 512)
        for part in range(2):
            span = pl.ds(6 * s + 3 * (1 - part), 3)
            tiles[index, :, span] = full[part].astype(BF16)
        leave(s, index).start()

    @pl.when(s == count - 1)
    def _():
        token[...] = jnp.zeros_like(token)
        for index in range(4):
            for step in range(count):
                leave(step, index).wait()


def outer(partial, own, halo, beside, bias, back, core, first, count):
    anywhere = pl.BlockSpec(memory_space=pl.ANY)
    shape = (2, 48, 3, 8, 512)
    return pl.pallas_call(
        functools.partial(outer_body, first, count),
        grid_spec=pltpu.PrefetchScalarGridSpec(
            num_scalar_prefetch=1,
            grid=(count,),
            in_specs=[
                band_spec(first),
                band_spec(first),
                pl.BlockSpec((4, 1, 80, 512), lambda s, core: (0, s + first, 0, 0)),
                fixed_spec((1, 2, WIN, 576)),
                side_spec((96, 160)),
            ]
            + [anywhere] * 4,
            out_specs=[anywhere] * 4 + [fixed_spec((8, 128))],
            scratch_shapes=[
                pltpu.VMEM((1, 4, WIN, 512), BF16),
                pltpu.VMEM((4, WIN + 80, 512), BF16),
                pltpu.VMEM((4, 2, 6 * count, 8, 512), BF16),
                pltpu.SemaphoreType.DMA((count, 4)),
            ]
            + work_scratch(2),
        ),
        out_shape=[jax.ShapeDtypeStruct(shape, BF16)] * 4
        + [jax.ShapeDtypeStruct((8, 128), F32)],
        input_output_aliases={6 + index: index for index in range(4)},
        compiler_params=params(),
        cost_estimate=window_cost(count, count * 2 * MIB),
        name="outer_windows",
    )(core, own, halo, beside, bias, back, *[x.reshape(shape) for x in partial])


def corner_body(core, flags, mid, near, near_halo, far, far_halo, bias, back, p0, p1, p2, p3, o0, o1, o2, o3, win, result, cut, *work):
    s = pl.program_id(0)
    left = core[0] == 0
    for index in range(4):
        win[1, index] = mid[index, 0]
    place_pair(win, 0, far, far_halo, jnp.logical_not(left))
    place_pair(win, 2, near, near_halo, left)

    key_part = lax.broadcasted_iota(jnp.int32, (WIN, 576), 0) % STRIP < HALF
    query_part = lax.broadcasted_iota(jnp.int32, (WIN, 576), 1) % STRIP < HALF
    apart = (key_part != query_part) & (flags[s] != 0)
    for group in range(2):
        cut[0, group] = jnp.where(apart, -jnp.inf, bias[0, group])

    starts = (
        pl.multiple_of(2 * WIN * core[0], 16),
        WIN,
        pl.multiple_of(2 * WIN * (1 - core[0]), 16),
    )

    def keep(slot, index, cols, value):
        result[index, pl.ds(starts[slot], WIN), cols] = value.astype(BF16)

    windows(win, 3, cut, *work, keep)
    for index, out in enumerate((o0, o1, o2, o3)):
        full = dot(back[0], result[index, 64:368])
        out[:, 0] = full.reshape(2, STRIP, 512).astype(BF16)


def corners(partial, flags, mid, near, near_halo, far, far_halo, bias, back, core):
    anywhere = pl.BlockSpec(memory_space=pl.ANY)
    shape = (2, 16, STRIP, 512)

    def edge(size):
        return pl.BlockSpec((4, 1, size, 512), lambda s, core, flags: (0, s, 0, 0))

    return pl.pallas_call(
        corner_body,
        grid_spec=pltpu.PrefetchScalarGridSpec(
            num_scalar_prefetch=2,
            grid=(2,),
            in_specs=[
                edge(WIN),
                edge(STRIP),
                edge(STRIP),
                edge(STRIP),
                edge(STRIP),
                pl.BlockSpec((1, 2, WIN, 576), lambda s, core, flags: (0, 0, 0, 0)),
                pl.BlockSpec((1, WIN, 304), lambda s, core, flags: (s, 0, 0)),
            ]
            + [anywhere] * 4,
            out_specs=[
                pl.BlockSpec((2, 1, STRIP, 512), lambda s, core, flags: (0, 15 * s, 0, 0))
            ]
            * 4,
            scratch_shapes=[
                pltpu.VMEM((3, 4, WIN, 512), BF16),
                pltpu.VMEM((4, 3 * WIN, 512), BF16),
                pltpu.VMEM((1, 2, WIN, 576), F32),
            ]
            + work_scratch(6),
        ),
        out_shape=[jax.ShapeDtypeStruct(shape, BF16)] * 4,
        input_output_aliases={9 + index: index for index in range(4)},
        compiler_params=params(),
        cost_estimate=window_cost(6, 8 * MIB),
        name="corner_windows",
    )(
        core, flags, mid, near, near_halo, far, far_halo, bias, back,
        *[x.reshape(shape) for x in partial],
    )


def bias_body(table, hot, squeeze, out, wide, part):
    for head in range(8):
        line = jnp.broadcast_to(table[head : head + 1], (8, 768))
        line = pltpu.roll(line, 0, 1, stride=1, stride_axis=0)
        for run, base in enumerate(run_bases()):
            turn = int(base - 379) % 768
            turned = pltpu.roll(line, turn, 1)
            group, cols = head // 4, slice(384 * (head % 4), 384 * (head % 4) + 384)
            wide[group, 8 * run : 8 * run + 8, cols] = turned[:, :384]
    for group in range(2):
        high = wide[group].astype(BF16)
        part[0, group] = high
        part[1, group] = (wide[group] - high.astype(F32)).astype(BF16)
    for group in range(2):
        total = None
        for order in range(2):
            spread = dot(part[order, group], hot[...]).astype(BF16)
            piece = dot(squeeze[...], spread)
            total = piece if total is None else total + piece
        out[0, group] = total


def window_bias(rel_table):
    tokens = (run_bases()[:, None] + np.arange(6)).reshape(WIN)
    hot = np.zeros((4, 384, 4, WIN), np.float32)
    for head in range(4):
        hot[head, tokens, head, np.arange(WIN)] = 1
    squeeze = np.zeros((24, 6, 24, 8), np.float32)
    for run in range(24):
        squeeze[run, np.arange(6), run, np.arange(6)] = 1
    hot = jnp.asarray(hot.reshape(4 * 384, 4 * WIN), BF16)
    squeeze = jnp.asarray(squeeze.reshape(WIN, 192), BF16)
    table = jnp.pad(rel_table, ((0, 0), (0, 768 - rel_table.shape[1])))
    return pl.pallas_call(
        bias_body,
        out_shape=jax.ShapeDtypeStruct((1, 2, WIN, 576), F32),
        scratch_shapes=[
            pltpu.VMEM((2, 192, 4 * 384), F32),
            pltpu.VMEM((2, 2, 192, 4 * 384), BF16),
        ],
        compiler_params=params(),
        cost_estimate=pl.CostEstimate(
            flops=4 * 2 * 192 * 1536 * 576, bytes_accessed=3 * MIB, transcendentals=0
        ),
        name="window_bias",
    )(table, hot, squeeze)


def side_tables():
    far_strip, near_strip = (0, 3), (3, 0)
    far, near, whole, near_back, far_back = [], [], [], [], []
    for side in range(2):
        far.append(far_matrix(far_strip[side], 2 * side))
        near.append(far_matrix(near_strip[side], 2 - 2 * side))
        whole.append(strip_matrix([far_strip[side], near_strip[side], 1, 2]))
        own = strip_matrix([near_strip[side]]).T
        middle = strip_matrix([1, 2]).T
        pad = np.zeros((2 * WIN, 8), np.float32)
        pad_far = np.zeros((96, 8), np.float32)
        inside = far_matrix(1 + side, 2 * side).T
        if side == 0:
            near_back.append(np.concatenate([middle, own, pad], axis=1))
            far_back.append(np.concatenate([pad_far, far[0].T, inside, pad_far], axis=1))
        else:
            near_back.append(np.concatenate([pad, own, middle], axis=1))
            far_back.append(np.concatenate([far[1].T, pad_far, pad_far, inside], axis=1))
    natural = strip_matrix([0, 1, 2, 3]).T.reshape(2, WIN, 2 * WIN)
    corner_back = np.pad(natural, ((0, 0), (0, 0), (8, 8)))
    stacked = (far, near, whole, near_back, far_back, corner_back)
    return [jnp.asarray(np.stack(table), BF16) for table in stacked]


def shards(queries, key_tokens, value_tokens, out_grad, land_mask, land_embed, rel_table):
    lev, rows, cols, width = queries.shape
    lat = lax.axis_index("lat")
    core = jnp.reshape(lax.axis_index("lon") % 2, (1,))
    bands = lax.axis_size("lat")
    sectors = lax.axis_size("lon")
    arrays = (queries, key_tokens, value_tokens, out_grad)
    mask = jnp.broadcast_to(
        land_mask.astype(F32).reshape(rows, 3, 8, 1), (rows, 3, 8, 128)
    )
    embed = land_embed.reshape(1, width)
    far_perm, near_perm, all_perm, near_back, far_back, corner_back = side_tables()
    mid_perm = jnp.asarray(strip_matrix([1, 2]), BF16)

    to_far = [((2 * k + 1) % sectors, (2 * k + 2) % sectors) for k in range(sectors // 2)]
    to_far += [(b, a) for a, b in to_far]
    to_near = [(i, i ^ 1) for i in range(sectors)]

    far, near, top, bottom = pack_edges(arrays, mask, embed, far_perm, near_perm, core)
    ends = (4, 2, STRIP, width)
    top, bottom = top.reshape(ends), bottom.reshape(ends)
    far_halo = lax.ppermute(far, "lon", to_far)
    near_halo = lax.ppermute(near, "lon", to_near)
    below = lax.ppermute(top, "lat", [(i, i - 1) for i in range(1, bands)])
    above = lax.ppermute(bottom, "lat", [(i, i + 1) for i in range(bands - 1)])

    bias = window_bias(rel_table)
    *partial, beside, _ = inner(
        arrays, mask, embed, mid_perm, near, near_halo, bias, near_back, core
    )
    *partial, done = outer(partial, far, far_halo, beside, bias, far_back, core, 0, 4)

    far_c, near_c, mid_c = pack_corners(top, bottom, below, above, all_perm, core, done)
    far_halo_c = lax.ppermute(far_c, "lon", to_far)
    near_halo_c = lax.ppermute(near_c, "lon", to_near)
    *partial, _ = outer(partial, far, far_halo, beside, bias, far_back, core, 4, 3)
    flags = jnp.stack([lat == 0, lat == bands - 1]).astype(jnp.int32)
    final = corners(
        partial, flags, mid_c, near_c, near_halo_c, far_c, far_halo_c, bias, corner_back, core
    )
    return tuple(x.reshape(queries.shape) for x in final)


def solution(mesh):
    tokens = P(None, "lat", "lon", None)
    return jax.shard_map(
        shards,
        mesh=mesh,
        in_specs=(tokens, tokens, tokens, tokens, P("lat", "lon"), P(), P()),
        out_specs=(tokens,) * 4,
        check_vma=False,
    )
```

```python
import functools

import jax
import jax.numpy as jnp
import numpy as np
from jax import lax
from jax.experimental import pallas as pl
from jax.experimental.pallas import tpu as pltpu
from jax.sharding import PartitionSpec as P

F32 = jnp.float32
BF16 = jnp.bfloat16
HALF = 36
STRIP = 72
WIN = 144
GROUP = 256
MIB = 1 << 20
VMEM_BYTES = 63 * MIB


def strip_matrix(strips):
    out = np.zeros((len(strips), 2, 2, 3, 6, 2, 2, 3, 24), np.float32)
    for place, strip in enumerate(strips):
        for part in range(2):
            for lev in range(2):
                for row in range(3):
                    for col in range(6):
                        out[place, part, lev, row, col, part, lev, row, 6 * strip + col] = 1
    return out.reshape(len(strips) * STRIP, 2 * WIN)


def far_matrix(strip, tile):
    full = strip_matrix([strip]).reshape(STRIP, 2, 2, 3, 3, 8)
    return full[:, :, :, :, tile].reshape(STRIP, 96)


def run_bases():
    run = np.arange(24)
    half, part, lev, row = run // 12, run // 6 % 2, run // 3 % 2, run % 3
    return lev * 253 + (row + 3 * (1 - part)) * 23 + 6 * half


def dot(a, b, ca=1, cb=0):
    return lax.dot_general(a, b, (((ca,), (cb,)), ((), ())), preferred_element_type=F32)


def keyed_rows(key, mask, embed):
    wide = jnp.concatenate([mask] * 4, axis=-1)
    return (key + (wide * embed)[None]).astype(BF16).astype(F32)


def side_spec(shape):
    return pl.BlockSpec((1, *shape), lambda s, core: (core[0],) + (0,) * len(shape))


def fixed_spec(shape):
    return pl.BlockSpec(shape, lambda s, core: (0,) * len(shape))


def params():
    return pltpu.CompilerParams(vmem_limit_bytes=VMEM_BYTES)


def edges_body(bands, q, k, v, g, mask, embed, far_perm, near_perm, far_a, far_b, near, top, bottom, below, above, held, packed, rows, came, gone, rows_came, rows_gone, sent, received):
    core = lax.axis_index("lon") % 2
    lat, lon = lax.axis_index("lat"), lax.axis_index("lon")
    neighbours = ((lat + bands - 1) % bands, (lat + 1) % bands)
    barrier = pltpu.get_barrier_semaphore()
    for neighbour in neighbours:
        pl.semaphore_signal(
            barrier, inc=1, device_id=(neighbour, lon), device_id_type=pl.DeviceIdType.MESH
        )
    sources = (q, k, v, g)
    tiles = (2 * core, 2 - 2 * core)
    ends = ((top, 0), (bottom, 45))

    def rows_in(end, index):
        row = ends[end][1]
        return pltpu.make_async_copy(
            sources[index].at[:, row : row + 3], rows.at[end, index], rows_came.at[end, index]
        )

    def rows_out(end, index):
        return pltpu.make_async_copy(
            rows.at[end, index], ends[end][0].at[index], rows_gone.at[end, index]
        )

    def rows_over(end, index):
        return pltpu.make_async_remote_copy(
            src_ref=rows.at[end, index],
            dst_ref=(below, above)[end].at[index],
            send_sem=sent.at[end, index],
            recv_sem=received.at[end, index],
            device_id=(neighbours[end], lon),
            device_id_type=pl.DeviceIdType.MESH,
        )

    def fetch(side, index):
        return pltpu.make_async_copy(
            sources[index].at[:, :, tiles[side]], held.at[side, index], came.at[side, index]
        )

    def send_off(side, index):
        if side == 0:
            return [
                pltpu.make_async_copy(
                    packed.at[0, index, 0:4], far_a.at[index], gone.at[0, index]
                ),
                pltpu.make_async_copy(
                    packed.at[0, index, 4:7], far_b.at[index], gone.at[2, index]
                ),
            ]
        return [pltpu.make_async_copy(packed.at[1, index], near.at[index], gone.at[1, index])]

    for end in range(2):
        for index in range(4):
            rows_in(end, index).start()
    for side in range(2):
        for index in range(4):
            fetch(side, index).start()
    pl.semaphore_wait(barrier, 2)
    for end in range(2):
        row = ends[end][1]
        for index in (0, 2, 3, 1):
            rows_in(end, index).wait()
            if index == 1:
                keyed = keyed_rows(rows[end, 1].astype(F32), mask[row : row + 3], embed[...])
                rows[end, 1] = keyed.astype(BF16)
            rows_over(end, index).start()
            rows_out(end, index).start()
    for side in range(2):
        perm = (far_perm, near_perm)[side]
        for index in range(4):
            fetch(side, index).wait()

            def pack_band(step, carry, side=side, index=index, perm=perm):
                lower, upper = pl.ds(6 * step + 6, 3), pl.ds(6 * step + 3, 3)
                opening = held[side, index, :, lower].astype(F32)
                closing = held[side, index, :, upper].astype(F32)
                if index == 1:
                    column = pl.ds(tiles[side], 1)
                    opening = keyed_rows(opening, mask[lower, column][:, 0], embed[...])
                    closing = keyed_rows(closing, mask[upper, column][:, 0], embed[...])
                tokens = jnp.concatenate(
                    [opening.reshape(48, 512), closing.reshape(48, 512)], axis=0
                )
                strip = dot(perm[core], tokens.astype(BF16))
                if index == 0:
                    strip = strip * 0.125
                packed[side, index, step] = strip.astype(BF16)
                return carry

            lax.fori_loop(0, 7, pack_band, 0)
            for copy in send_off(side, index):
                copy.start()
    for index in range(4):
        for copy in send_off(0, index) + send_off(1, index):
            copy.wait()
        for end in range(2):
            rows_out(end, index).wait()
            rows_over(end, index).wait()


def pack_edges(arrays, mask, embed, far_perm, near_perm, bands):
    tiles = [array.reshape(2, 48, 3, 8, 512) for array in arrays]
    anywhere = pl.BlockSpec(memory_space=pl.ANY)
    local = pl.BlockSpec(memory_space=pltpu.VMEM)
    far_a, far_b, near = (
        jax.ShapeDtypeStruct((4, count, STRIP, 512), BF16) for count in (4, 3, 7)
    )
    ends = jax.ShapeDtypeStruct((4, 2, 3, 3, 8, 512), BF16)
    return pl.pallas_call(
        functools.partial(edges_body, bands),
        in_specs=[anywhere] * 4 + [local] * 4,
        out_specs=[anywhere] * 7,
        scratch_shapes=[
            pltpu.VMEM((2, 4, 2, 48, 8, 512), BF16),
            pltpu.VMEM((2, 4, 7, STRIP, 512), BF16),
            pltpu.VMEM((2, 4, 2, 3, 3, 8, 512), BF16),
            pltpu.SemaphoreType.DMA((2, 4)),
            pltpu.SemaphoreType.DMA((3, 4)),
            pltpu.SemaphoreType.DMA((2, 4)),
            pltpu.SemaphoreType.DMA((2, 4)),
            pltpu.SemaphoreType.DMA((2, 4)),
            pltpu.SemaphoreType.DMA((2, 4)),
        ],
        out_shape=[far_a, far_b, near, ends, ends, ends, ends],
        compiler_params=pltpu.CompilerParams(
            vmem_limit_bytes=VMEM_BYTES, collective_id=0, has_side_effects=True
        ),
        cost_estimate=pl.CostEstimate(
            flops=2 * 56 * STRIP * 96 * 512, bytes_accessed=16 * MIB, transcendentals=0
        ),
        name="pack_edges",
    )(*tiles, mask, embed, far_perm, near_perm)


def corners_body(core, top, bottom, below, above, perm, far, near, mid):
    for index in range(4):
        for place, (first, second) in enumerate(((top, above), (below, bottom))):
            first = first[index].astype(F32)
            second = second[index].astype(F32)
            tokens = jnp.concatenate([first[0], first[1], second[0], second[1]], axis=0)
            strips = dot(perm[0], tokens.astype(BF16))
            if index == 0:
                strips = strips * 0.125
            far[index, place] = strips[:STRIP].astype(BF16)
            near[index, place] = strips[STRIP : 2 * STRIP].astype(BF16)
            mid[index, place] = strips[2 * STRIP :].astype(BF16)


def pack_corners(top, bottom, below, above, perm, core):
    sizes = (STRIP, STRIP, WIN)
    return pl.pallas_call(
        corners_body,
        grid_spec=pltpu.PrefetchScalarGridSpec(
            num_scalar_prefetch=1,
            grid=(1,),
            in_specs=[fixed_spec((4, 2, STRIP, 512))] * 4 + [side_spec((2 * WIN, 2 * WIN))],
            out_specs=[fixed_spec((4, 2, size, 512)) for size in sizes],
        ),
        out_shape=[jax.ShapeDtypeStruct((4, 2, size, 512), BF16) for size in sizes],
        compiler_params=params(),
        cost_estimate=pl.CostEstimate(
            flops=2 * 8 * 288 * 288 * 512, bytes_accessed=5 * MIB, transcendentals=0
        ),
        name="pack_corners",
    )(core, top, bottom, below, above, perm)


def windows(win, slots, bias, scores, grads, low, dlow, store):
    lane = lax.broadcasted_iota(jnp.int32, (1, GROUP), 1) // 64

    def spread(x):
        return jnp.concatenate(
            [x * jnp.where(lane == h, 1.0, 0.0).astype(BF16) for h in range(4)], axis=0
        )

    def by_head(wide):
        total = None
        for h in range(4):
            piece = jnp.where(lane == h, wide[WIN * h : WIN * (h + 1)], 0.0)
            total = piece if total is None else total + piece
        return total

    jobs = []
    for slot in range(slots):
        for group in range(2):
            cols = slice(GROUP * group, GROUP * (group + 1))
            q, k, v, g = (win[slot, index, :, cols] for index in range(4))
            q_wide, g_wide = spread(q), spread(g)
            place = 2 * slot + group
            scores[place] = dot(k, q_wide, 1, 1)
            grads[place] = dot(v, g_wide, 1, 1)
            jobs.append((slot, group, place, cols, k, v, q_wide, g_wide))
    for slot, group, place, cols, k, v, q_wide, g_wide in jobs:
        for start in range(0, 576, 128):
            part = slice(start, min(start + 128, 576))
            s = scores[place, :, part] + bias[0, group, :, part]
            e = jnp.exp(s - jnp.max(s, axis=0, keepdims=True))
            p = e * (1.0 / jnp.sum(e, axis=0, keepdims=True))
            gp = grads[place, :, part]
            delta = jnp.sum(p * gp, axis=0, keepdims=True)
            low[place, :, part] = p.astype(BF16)
            dlow[place, :, part] = (p * (gp - delta)).astype(BF16)
        p_low, d_low = low[place], dlow[place]
        store(slot, 0, cols, by_head(dot(p_low, v, 0, 0)))
        store(slot, 1, cols, by_head(dot(d_low, k, 0, 0)) * 0.125)
        store(slot, 2, cols, dot(d_low, q_wide))
        store(slot, 3, cols, dot(p_low, g_wide))


def place_pair(win, slot, own, halo, own_left):
    def put(left, right):
        for index in range(4):
            both = jnp.concatenate(
                [left[index, 0].astype(F32), right[index, 0].astype(F32)], axis=0
            )
            win[slot, index] = both.astype(BF16)

    @pl.when(own_left)
    def _():
        put(own, halo)

    @pl.when(jnp.logical_not(own_left))
    def _():
        put(halo, own)


def inner_body(core, q0, q1, k0, k1, v0, v1, g0, g1, m0, m1, embed, perm, own, halo, bias, back, *rest):
    outs, beside, token, (win, result, ready, gone), work = rest[:4], rest[4], rest[5], rest[6:10], rest[10:]
    s = pl.program_id(0)
    for index, pair in enumerate(((q0, q1), (k0, k1), (v0, v1), (g0, g1))):
        first, second = (source[:, 0].astype(F32) for source in pair)
        if index == 1:
            first = keyed_rows(first, m0[...].reshape(STRIP, 128), embed[...])
            second = keyed_rows(second, m1[...].reshape(STRIP, 128), embed[...])
        tokens = jnp.concatenate([first[0], first[1], second[0], second[1]], axis=0)
        packed = dot(perm[...], tokens.astype(BF16))
        if index == 0:
            packed = packed * 0.125
        win[0, index] = packed.astype(BF16)
    place_pair(win, 1, own, halo, core[0] == 0)

    starts = (pl.multiple_of(WIN * core[0], 16), pl.multiple_of(WIN * (1 - core[0]), 16))

    def keep(slot, index, cols, value):
        result[index, pl.ds(starts[slot], WIN), cols] = value.astype(BF16)

    windows(win, 2, bias, *work, keep)

    def leave(slot, step):
        copies = []
        for index, out in enumerate(outs):
            for part in range(2):
                copies.append(
                    pltpu.make_async_copy(
                        ready.at[slot, index, part],
                        out.at[:, 2 * step + 2 - part],
                        gone.at[slot, index, part],
                    )
                )
        return copies

    slot = s % 2

    @pl.when(s >= 2)
    def _():
        for copy in leave(slot, s - 2):
            copy.wait()

    used = pl.ds(pl.multiple_of(64 * core[0], 16), 224)
    near_far = pl.ds(pl.multiple_of(208 * core[0], 16), 80)
    for index in range(4):
        beside[index, 0] = result[index, near_far]
        full = dot(back[0], result[index, used])
        ready[slot, index] = full.reshape(2, 2, STRIP, 512).astype(BF16)
    for copy in leave(slot, s):
        copy.start()

    @pl.when(s == 6)
    def _():
        token[...] = jnp.zeros_like(token)
        for copy in leave(1, 5) + leave(0, 6):
            copy.wait()


def work_scratch(places):
    return [
        pltpu.VMEM((places, WIN, 576), F32),
        pltpu.VMEM((places, WIN, 576), F32),
        pltpu.VMEM((places, WIN, 576), BF16),
        pltpu.VMEM((places, WIN, 576), BF16),
    ]


def window_cost(count, moved):
    return pl.CostEstimate(
        flops=count * 6 * 2 * WIN * WIN * 512 * 4,
        bytes_accessed=moved,
        transcendentals=count * 8 * WIN * WIN,
    )


def inner(arrays, mask, embed, perm, own, halo, bias, back, core):
    operands, specs = [], []
    block = (2, 1, STRIP, 512)
    for array in arrays:
        array = array.reshape(2, 16, STRIP, 512)
        operands += [array, array]
        specs += [
            pl.BlockSpec(block, lambda s, core: (0, 2 * s + 2, 0, 0)),
            pl.BlockSpec(block, lambda s, core: (0, 2 * s + 1, 0, 0)),
        ]
    anywhere = pl.BlockSpec(memory_space=pl.ANY)
    return pl.pallas_call(
        inner_body,
        grid_spec=pltpu.PrefetchScalarGridSpec(
            num_scalar_prefetch=1,
            grid=(7,),
            in_specs=specs
            + [
                pl.BlockSpec((3, 3, 8, 128), lambda s, core: (2 * s + 2, 0, 0, 0)),
                pl.BlockSpec((3, 3, 8, 128), lambda s, core: (2 * s + 1, 0, 0, 0)),
                fixed_spec((1, 512)),
                fixed_spec((WIN, 2 * WIN)),
                band_spec(),
                band_spec(),
                fixed_spec((1, 2, WIN, 576)),
                side_spec((2 * WIN, 224)),
            ],
            out_specs=[anywhere] * 4
            + [
                pl.BlockSpec((4, 1, 80, 512), lambda s, core: (0, s, 0, 0)),
                fixed_spec((8, 128)),
            ],
            scratch_shapes=[
                pltpu.VMEM((2, 4, WIN, 512), BF16),
                pltpu.VMEM((4, 2 * WIN, 512), BF16),
                pltpu.VMEM((2, 4, 2, 2, STRIP, 512), BF16),
                pltpu.SemaphoreType.DMA((2, 4, 2)),
            ]
            + work_scratch(4),
        ),
        out_shape=[jax.ShapeDtypeStruct((2, 16, STRIP, 512), BF16)] * 4
        + [jax.ShapeDtypeStruct((4, 7, 80, 512), BF16), jax.ShapeDtypeStruct((8, 128), F32)],
        compiler_params=params(),
        cost_estimate=window_cost(14, 24 * MIB),
        name="inner_windows",
    )(core, *operands, mask, mask, embed, perm, own, halo, bias, back)


def band_spec():
    return pl.BlockSpec((4, 1, STRIP, 512), lambda s, core: (0, s, 0, 0))


def outer_body(first, count, core, own, halo, beside, bias, back, p0, p1, p2, p3, o0, o1, o2, o3, token, win, result, tiles, gone, *work):
    s = pl.program_id(0)
    tile = 2 * core[0]
    outs = (o0, o1, o2, o3)
    place_pair(win, 0, own, halo, core[0] == 1)

    def keep(slot, index, cols, value):
        result[index, 0:WIN, cols] = value.astype(BF16)

    windows(win, 1, bias, *work, keep)

    def leave(step, index):
        return pltpu.make_async_copy(
            tiles.at[index, :, pl.ds(6 * step, 6)],
            outs[index].at[:, pl.ds(6 * (step + first) + 3, 6), tile],
            gone.at[step, index],
        )

    used = pl.ds(pl.multiple_of(64 * (1 - core[0]), 16), 160)
    beside_at = pl.ds(pl.multiple_of(WIN - 64 * core[0], 16), 80)
    for index in range(4):
        result[index, beside_at] = beside[index, 0]
        full = dot(back[0], result[index, used]).reshape(2, 2, 3, 8, 512)
        for part in range(2):
            span = pl.ds(6 * s + 3 * (1 - part), 3)
            tiles[index, :, span] = full[part].astype(BF16)
        leave(s, index).start()

    @pl.when(s == count - 1)
    def _():
        token[...] = jnp.zeros_like(token)
        for index in range(4):
            for step in range(count):
                leave(step, index).wait()


def outer(partial, own, halo, beside, bias, back, core, first, count):
    anywhere = pl.BlockSpec(memory_space=pl.ANY)
    shape = (2, 48, 3, 8, 512)
    return pl.pallas_call(
        functools.partial(outer_body, first, count),
        grid_spec=pltpu.PrefetchScalarGridSpec(
            num_scalar_prefetch=1,
            grid=(count,),
            in_specs=[
                band_spec(),
                band_spec(),
                pl.BlockSpec((4, 1, 80, 512), lambda s, core: (0, s + first, 0, 0)),
                fixed_spec((1, 2, WIN, 576)),
                side_spec((96, 160)),
            ]
            + [anywhere] * 4,
            out_specs=[anywhere] * 4 + [fixed_spec((8, 128))],
            scratch_shapes=[
                pltpu.VMEM((1, 4, WIN, 512), BF16),
                pltpu.VMEM((4, WIN + 80, 512), BF16),
                pltpu.VMEM((4, 2, 6 * count, 8, 512), BF16),
                pltpu.SemaphoreType.DMA((count, 4)),
            ]
            + work_scratch(2),
        ),
        out_shape=[jax.ShapeDtypeStruct(shape, BF16)] * 4
        + [jax.ShapeDtypeStruct((8, 128), F32)],
        input_output_aliases={6 + index: index for index in range(4)},
        compiler_params=params(),
        cost_estimate=window_cost(count, count * 2 * MIB),
        name="outer_windows",
    )(core, own, halo, beside, bias, back, *[x.reshape(shape) for x in partial])


def corner_body(core, flags, mid, near, near_halo, far, far_halo, bias, back, p0, p1, p2, p3, o0, o1, o2, o3, win, result, cut, *work):
    s = pl.program_id(0)
    left = core[0] == 0
    for index in range(4):
        win[1, index] = mid[index, 0]
    place_pair(win, 0, far, far_halo, jnp.logical_not(left))
    place_pair(win, 2, near, near_halo, left)

    key_part = lax.broadcasted_iota(jnp.int32, (WIN, 576), 0) % STRIP < HALF
    query_part = lax.broadcasted_iota(jnp.int32, (WIN, 576), 1) % STRIP < HALF
    apart = (key_part != query_part) & (flags[s] != 0)
    for group in range(2):
        cut[0, group] = jnp.where(apart, -jnp.inf, bias[0, group])

    starts = (
        pl.multiple_of(2 * WIN * core[0], 16),
        WIN,
        pl.multiple_of(2 * WIN * (1 - core[0]), 16),
    )

    def keep(slot, index, cols, value):
        result[index, pl.ds(starts[slot], WIN), cols] = value.astype(BF16)

    windows(win, 3, cut, *work, keep)
    for index, out in enumerate((o0, o1, o2, o3)):
        full = dot(back[0], result[index, 64:368])
        out[:, 0] = full.reshape(2, STRIP, 512).astype(BF16)


def corners(partial, flags, mid, near, near_halo, far, far_halo, bias, back, core):
    anywhere = pl.BlockSpec(memory_space=pl.ANY)
    shape = (2, 16, STRIP, 512)

    def edge(size):
        return pl.BlockSpec((4, 1, size, 512), lambda s, core, flags: (0, s, 0, 0))

    return pl.pallas_call(
        corner_body,
        grid_spec=pltpu.PrefetchScalarGridSpec(
            num_scalar_prefetch=2,
            grid=(2,),
            in_specs=[
                edge(WIN),
                edge(STRIP),
                edge(STRIP),
                edge(STRIP),
                edge(STRIP),
                pl.BlockSpec((1, 2, WIN, 576), lambda s, core, flags: (0, 0, 0, 0)),
                pl.BlockSpec((1, WIN, 304), lambda s, core, flags: (s, 0, 0)),
            ]
            + [anywhere] * 4,
            out_specs=[
                pl.BlockSpec((2, 1, STRIP, 512), lambda s, core, flags: (0, 15 * s, 0, 0))
            ]
            * 4,
            scratch_shapes=[
                pltpu.VMEM((3, 4, WIN, 512), BF16),
                pltpu.VMEM((4, 3 * WIN, 512), BF16),
                pltpu.VMEM((1, 2, WIN, 576), F32),
            ]
            + work_scratch(6),
        ),
        out_shape=[jax.ShapeDtypeStruct(shape, BF16)] * 4,
        input_output_aliases={9 + index: index for index in range(4)},
        compiler_params=params(),
        cost_estimate=window_cost(6, 8 * MIB),
        name="corner_windows",
    )(
        core, flags, mid, near, near_halo, far, far_halo, bias, back,
        *[x.reshape(shape) for x in partial],
    )


def bias_body(table, hot, squeeze, out, wide, part):
    for head in range(8):
        line = jnp.broadcast_to(table[head : head + 1], (8, 768))
        line = pltpu.roll(line, 0, 1, stride=1, stride_axis=0)
        for run, base in enumerate(run_bases()):
            turn = int(base - 379) % 768
            turned = pltpu.roll(line, turn, 1)
            group, cols = head // 4, slice(384 * (head % 4), 384 * (head % 4) + 384)
            wide[group, 8 * run : 8 * run + 8, cols] = turned[:, :384]
    for group in range(2):
        high = wide[group].astype(BF16)
        part[0, group] = high
        part[1, group] = (wide[group] - high.astype(F32)).astype(BF16)
    for group in range(2):
        total = None
        for order in range(2):
            spread = dot(part[order, group], hot[...]).astype(BF16)
            piece = dot(squeeze[...], spread)
            total = piece if total is None else total + piece
        out[0, group] = total


def window_bias(rel_table):
    tokens = (run_bases()[:, None] + np.arange(6)).reshape(WIN)
    hot = np.zeros((4, 384, 4, WIN), np.float32)
    for head in range(4):
        hot[head, tokens, head, np.arange(WIN)] = 1
    squeeze = np.zeros((24, 6, 24, 8), np.float32)
    for run in range(24):
        squeeze[run, np.arange(6), run, np.arange(6)] = 1
    hot = jnp.asarray(hot.reshape(4 * 384, 4 * WIN), BF16)
    squeeze = jnp.asarray(squeeze.reshape(WIN, 192), BF16)
    table = jnp.pad(rel_table, ((0, 0), (0, 768 - rel_table.shape[1])))
    return pl.pallas_call(
        bias_body,
        out_shape=jax.ShapeDtypeStruct((1, 2, WIN, 576), F32),
        scratch_shapes=[
            pltpu.VMEM((2, 192, 4 * 384), F32),
            pltpu.VMEM((2, 2, 192, 4 * 384), BF16),
        ],
        compiler_params=params(),
        cost_estimate=pl.CostEstimate(
            flops=4 * 2 * 192 * 1536 * 576, bytes_accessed=3 * MIB, transcendentals=0
        ),
        name="window_bias",
    )(table, hot, squeeze)


def side_tables():
    far_strip, near_strip = (0, 3), (3, 0)
    far, near, whole, near_back, far_back = [], [], [], [], []
    for side in range(2):
        far.append(far_matrix(far_strip[side], 2 * side))
        near.append(far_matrix(near_strip[side], 2 - 2 * side))
        whole.append(strip_matrix([far_strip[side], near_strip[side], 1, 2]))
        own = strip_matrix([near_strip[side]]).T
        middle = strip_matrix([1, 2]).T
        pad = np.zeros((2 * WIN, 8), np.float32)
        pad_far = np.zeros((96, 8), np.float32)
        inside = far_matrix(1 + side, 2 * side).T
        if side == 0:
            near_back.append(np.concatenate([middle, own, pad], axis=1))
            far_back.append(np.concatenate([pad_far, far[0].T, inside, pad_far], axis=1))
        else:
            near_back.append(np.concatenate([pad, own, middle], axis=1))
            far_back.append(np.concatenate([far[1].T, pad_far, pad_far, inside], axis=1))
    natural = strip_matrix([0, 1, 2, 3]).T.reshape(2, WIN, 2 * WIN)
    corner_back = np.pad(natural, ((0, 0), (0, 0), (8, 8)))
    stacked = (far, near, whole, near_back, far_back, corner_back)
    return [jnp.asarray(np.stack(table), BF16) for table in stacked]


def shards(queries, key_tokens, value_tokens, out_grad, land_mask, land_embed, rel_table):
    lev, rows, cols, width = queries.shape
    lat = lax.axis_index("lat")
    core = jnp.reshape(lax.axis_index("lon") % 2, (1,))
    bands = lax.axis_size("lat")
    sectors = lax.axis_size("lon")
    arrays = (queries, key_tokens, value_tokens, out_grad)
    mask = jnp.broadcast_to(
        land_mask.astype(F32).reshape(rows, 3, 8, 1), (rows, 3, 8, 128)
    )
    embed = land_embed.reshape(1, width)
    far_perm, near_perm, all_perm, near_back, far_back, corner_back = side_tables()
    mid_perm = jnp.asarray(strip_matrix([1, 2]), BF16)

    to_far = [((2 * k + 1) % sectors, (2 * k + 2) % sectors) for k in range(sectors // 2)]
    to_far += [(b, a) for a, b in to_far]
    to_near = [(i, i ^ 1) for i in range(sectors)]

    far_a, far_b, near, *edge_rows = pack_edges(arrays, mask, embed, far_perm, near_perm, bands)
    top, bottom, below, above = (x.reshape(4, 2, STRIP, width) for x in edge_rows)
    far_halo_a = lax.ppermute(far_a, "lon", to_far)
    far_halo_b = lax.ppermute(far_b, "lon", to_far)
    near_halo = lax.ppermute(near, "lon", to_near)

    far_c, near_c, mid_c = pack_corners(top, bottom, below, above, all_perm, core)
    far_halo_c = lax.ppermute(far_c, "lon", to_far)
    near_halo_c = lax.ppermute(near_c, "lon", to_near)

    bias = window_bias(rel_table)
    *partial, beside, _ = inner(
        arrays, mask, embed, mid_perm, near, near_halo, bias, near_back, core
    )
    *partial, _ = outer(partial, far_a, far_halo_a, beside, bias, far_back, core, 0, 4)
    *partial, _ = outer(partial, far_b, far_halo_b, beside, bias, far_back, core, 4, 3)
    flags = jnp.stack([lat == 0, lat == bands - 1]).astype(jnp.int32)
    final = corners(
        partial, flags, mid_c, near_c, near_halo_c, far_c, far_halo_c, bias, corner_back, core
    )
    return tuple(x.reshape(queries.shape) for x in final)


def solution(mesh):
    tokens = P(None, "lat", "lon", None)
    return jax.shard_map(
        shards,
        mesh=mesh,
        in_specs=(tokens, tokens, tokens, tokens, P("lat", "lon"), P(), P()),
        out_specs=(tokens,) * 4,
        check_vma=False,
    )
```

```python
import functools

import jax
import jax.numpy as jnp
import numpy as np
from jax import lax
from jax.experimental import pallas as pl
from jax.experimental.pallas import tpu as pltpu
from jax.sharding import PartitionSpec as P

F32 = jnp.float32
BF16 = jnp.bfloat16
HALF = 36
STRIP = 72
WIN = 144
GROUP = 256
MIB = 1 << 20
VMEM_BYTES = 63 * MIB


def strip_matrix(strips):
    out = np.zeros((len(strips), 2, 2, 3, 6, 2, 2, 3, 24), np.float32)
    for place, strip in enumerate(strips):
        for part in range(2):
            for lev in range(2):
                for row in range(3):
                    for col in range(6):
                        out[place, part, lev, row, col, part, lev, row, 6 * strip + col] = 1
    return out.reshape(len(strips) * STRIP, 2 * WIN)


def far_matrix(strip, tile):
    full = strip_matrix([strip]).reshape(STRIP, 2, 2, 3, 3, 8)
    return full[:, :, :, :, tile].reshape(STRIP, 96)


def run_bases():
    run = np.arange(24)
    half, part, lev, row = run // 12, run // 6 % 2, run // 3 % 2, run % 3
    return lev * 253 + (row + 3 * (1 - part)) * 23 + 6 * half


def dot(a, b, ca=1, cb=0):
    return lax.dot_general(a, b, (((ca,), (cb,)), ((), ())), preferred_element_type=F32)


def keyed_rows(key, mask, embed):
    wide = jnp.concatenate([mask] * 4, axis=-1)
    return (key + (wide * embed)[None]).astype(BF16).astype(F32)


def side_spec(shape):
    return pl.BlockSpec((1, *shape), lambda s, core: (core[0],) + (0,) * len(shape))


def fixed_spec(shape):
    return pl.BlockSpec(shape, lambda s, core: (0,) * len(shape))


def params():
    return pltpu.CompilerParams(vmem_limit_bytes=VMEM_BYTES)


def edges_body(bands, q, k, v, g, mask, embed, perm, table, hot, squeeze, far_a, far_b, near, mid, top, bottom, below, above, bias, held, packed, interior, rows, came, gone, rows_came, rows_gone, sent, received, wide, part):
    core = lax.axis_index("lon") % 2
    lat, lon = lax.axis_index("lat"), lax.axis_index("lon")
    neighbours = ((lat + bands - 1) % bands, (lat + 1) % bands)
    barrier = pltpu.get_barrier_semaphore()
    for neighbour in neighbours:
        pl.semaphore_signal(
            barrier, inc=1, device_id=(neighbour, lon), device_id_type=pl.DeviceIdType.MESH
        )
    sources = (q, k, v, g)
    tiles = (2 * core, 2 - 2 * core, 1)
    ends = ((top, 0), (bottom, 45))

    def rows_in(end, index):
        row = ends[end][1]
        return pltpu.make_async_copy(
            sources[index].at[:, row : row + 3], rows.at[end, index], rows_came.at[end, index]
        )

    def rows_out(end, index):
        return pltpu.make_async_copy(
            rows.at[end, index], ends[end][0].at[index], rows_gone.at[end, index]
        )

    def rows_over(end, index):
        return pltpu.make_async_remote_copy(
            src_ref=rows.at[end, index],
            dst_ref=(below, above)[end].at[index],
            send_sem=sent.at[end, index],
            recv_sem=received.at[end, index],
            device_id=(neighbours[end], lon),
            device_id_type=pl.DeviceIdType.MESH,
        )

    def fetch(side, index):
        return pltpu.make_async_copy(
            sources[index].at[:, :, tiles[side]], held.at[side, index], came.at[side, index]
        )

    def send_off(side, index):
        if side == 0:
            return [
                pltpu.make_async_copy(
                    packed.at[0, index, 0:4], far_a.at[index], gone.at[0, index]
                ),
                pltpu.make_async_copy(
                    packed.at[0, index, 4:7], far_b.at[index], gone.at[2, index]
                ),
            ]
        if side == 1:
            return [pltpu.make_async_copy(packed.at[1, index], near.at[index], gone.at[1, index])]
        return [pltpu.make_async_copy(interior.at[index], mid.at[index], gone.at[3, index])]

    for end in range(2):
        for index in range(4):
            rows_in(end, index).start()
    for index in range(4):
        for side in range(3):
            fetch(side, index).start()
    pl.semaphore_wait(barrier, 2)
    for end in range(2):
        row = ends[end][1]
        for index in (0, 2, 3, 1):
            rows_in(end, index).wait()
            if index == 1:
                keyed = keyed_rows(rows[end, 1].astype(F32), mask[row : row + 3], embed[...])
                rows[end, 1] = keyed.astype(BF16)
            rows_over(end, index).start()
            rows_out(end, index).start()
    for index in range(4):
        for side in range(3):
            fetch(side, index).wait()

        def pack_band(step, carry, index=index):
            lower, upper = pl.ds(6 * step + 6, 3), pl.ds(6 * step + 3, 3)
            pieces = []
            for side in range(3):
                for span in (lower, upper):
                    piece = held[side, index, :, span].astype(F32)
                    if index == 1:
                        column = mask[span, pl.ds(tiles[side], 1)][:, 0]
                        piece = keyed_rows(piece, column, embed[...])
                    pieces.append(piece.reshape(48, 512))
            strips = dot(perm[core], jnp.concatenate(pieces, axis=0).astype(BF16))
            if index == 0:
                strips = strips * 0.125
            packed[0, index, step] = strips[:STRIP].astype(BF16)
            packed[1, index, step] = strips[STRIP : 2 * STRIP].astype(BF16)
            interior[index, step] = strips[2 * STRIP :].astype(BF16)
            return carry

        lax.fori_loop(0, 7, pack_band, 0)
        for side in range(3):
            for copy in send_off(side, index):
                copy.start()
    bias_body(table, hot, squeeze, bias, wide, part)
    for index in range(4):
        for side in range(3):
            for copy in send_off(side, index):
                copy.wait()
        for end in range(2):
            rows_out(end, index).wait()
            rows_over(end, index).wait()


def pack_edges(arrays, mask, embed, perm, bias_operands, bands):
    tiles = [array.reshape(2, 48, 3, 8, 512) for array in arrays]
    anywhere = pl.BlockSpec(memory_space=pl.ANY)
    local = pl.BlockSpec(memory_space=pltpu.VMEM)
    far_a, far_b, near = (
        jax.ShapeDtypeStruct((4, count, STRIP, 512), BF16) for count in (4, 3, 7)
    )
    ends = jax.ShapeDtypeStruct((4, 2, 3, 3, 8, 512), BF16)
    interior = jax.ShapeDtypeStruct((4, 7, WIN, 512), BF16)
    return pl.pallas_call(
        functools.partial(edges_body, bands),
        in_specs=[anywhere] * 4 + [local] * 6,
        out_specs=[anywhere] * 8 + [local],
        scratch_shapes=[
            pltpu.VMEM((3, 4, 2, 48, 8, 512), BF16),
            pltpu.VMEM((2, 4, 7, STRIP, 512), BF16),
            pltpu.VMEM((4, 7, WIN, 512), BF16),
            pltpu.VMEM((2, 4, 2, 3, 3, 8, 512), BF16),
            pltpu.SemaphoreType.DMA((3, 4)),
            pltpu.SemaphoreType.DMA((4, 4)),
            pltpu.SemaphoreType.DMA((2, 4)),
            pltpu.SemaphoreType.DMA((2, 4)),
            pltpu.SemaphoreType.DMA((2, 4)),
            pltpu.SemaphoreType.DMA((2, 4)),
            pltpu.VMEM((2, 192, 4 * 384), F32),
            pltpu.VMEM((2, 2, 192, 4 * 384), BF16),
        ],
        out_shape=[far_a, far_b, near, interior, ends, ends, ends, ends]
        + [jax.ShapeDtypeStruct((1, 2, WIN, 576), F32)],
        compiler_params=pltpu.CompilerParams(
            vmem_limit_bytes=VMEM_BYTES, collective_id=0, has_side_effects=True
        ),
        cost_estimate=pl.CostEstimate(
            flops=2 * 28 * 288 * 288 * 512, bytes_accessed=24 * MIB, transcendentals=0
        ),
        name="pack_edges",
    )(*tiles, mask, embed, perm, *bias_operands)


def corners_body(core, top, bottom, below, above, perm, far, near, mid):
    for index in range(4):
        for place, (first, second) in enumerate(((top, above), (below, bottom))):
            first = first[index].astype(F32)
            second = second[index].astype(F32)
            tokens = jnp.concatenate([first[0], first[1], second[0], second[1]], axis=0)
            strips = dot(perm[0], tokens.astype(BF16))
            if index == 0:
                strips = strips * 0.125
            far[index, place] = strips[:STRIP].astype(BF16)
            near[index, place] = strips[STRIP : 2 * STRIP].astype(BF16)
            mid[index, place] = strips[2 * STRIP :].astype(BF16)


def pack_corners(top, bottom, below, above, perm, core):
    sizes = (STRIP, STRIP, WIN)
    return pl.pallas_call(
        corners_body,
        grid_spec=pltpu.PrefetchScalarGridSpec(
            num_scalar_prefetch=1,
            grid=(1,),
            in_specs=[fixed_spec((4, 2, STRIP, 512))] * 4 + [side_spec((2 * WIN, 2 * WIN))],
            out_specs=[fixed_spec((4, 2, size, 512)) for size in sizes],
        ),
        out_shape=[jax.ShapeDtypeStruct((4, 2, size, 512), BF16) for size in sizes],
        compiler_params=params(),
        cost_estimate=pl.CostEstimate(
            flops=2 * 8 * 288 * 288 * 512, bytes_accessed=5 * MIB, transcendentals=0
        ),
        name="pack_corners",
    )(core, top, bottom, below, above, perm)


def windows(win, slots, bias, scores, grads, low, dlow, store):
    lane = lax.broadcasted_iota(jnp.int32, (1, GROUP), 1) // 64

    def spread(x):
        return jnp.concatenate(
            [x * jnp.where(lane == h, 1.0, 0.0).astype(BF16) for h in range(4)], axis=0
        )

    def by_head(wide):
        total = None
        for h in range(4):
            piece = jnp.where(lane == h, wide[WIN * h : WIN * (h + 1)], 0.0)
            total = piece if total is None else total + piece
        return total

    jobs = []
    for slot in range(slots):
        for group in range(2):
            cols = slice(GROUP * group, GROUP * (group + 1))
            q, k, v, g = (win[slot, index, :, cols] for index in range(4))
            q_wide, g_wide = spread(q), spread(g)
            place = 2 * slot + group
            scores[place] = dot(k, q_wide, 1, 1)
            grads[place] = dot(v, g_wide, 1, 1)
            jobs.append((slot, group, place, cols, k, v, q_wide, g_wide))
    for slot, group, place, cols, k, v, q_wide, g_wide in jobs:
        for start in range(0, 576, 128):
            part = slice(start, min(start + 128, 576))
            s = scores[place, :, part] + bias[0, group, :, part]
            e = jnp.exp(s - jnp.max(s, axis=0, keepdims=True))
            p = e * (1.0 / jnp.sum(e, axis=0, keepdims=True))
            gp = grads[place, :, part]
            delta = jnp.sum(p * gp, axis=0, keepdims=True)
            low[place, :, part] = p.astype(BF16)
            dlow[place, :, part] = (p * (gp - delta)).astype(BF16)
        p_low, d_low = low[place], dlow[place]
        store(slot, 0, cols, by_head(dot(p_low, v, 0, 0)))
        store(slot, 1, cols, by_head(dot(d_low, k, 0, 0)) * 0.125)
        store(slot, 2, cols, dot(d_low, q_wide))
        store(slot, 3, cols, dot(p_low, g_wide))


def place_pair(win, slot, own, halo, own_left):
    def put(left, right):
        for index in range(4):
            both = jnp.concatenate(
                [left[index, 0].astype(F32), right[index, 0].astype(F32)], axis=0
            )
            win[slot, index] = both.astype(BF16)

    @pl.when(own_left)
    def _():
        put(own, halo)

    @pl.when(jnp.logical_not(own_left))
    def _():
        put(halo, own)


def inner_body(core, mid, own, halo, bias, back, *rest):
    outs, beside, token, (win, result, ready, gone), work = rest[:4], rest[4], rest[5], rest[6:10], rest[10:]
    s = pl.program_id(0)
    for index in range(4):
        win[0, index] = mid[index, 0]
    place_pair(win, 1, own, halo, core[0] == 0)

    starts = (pl.multiple_of(WIN * core[0], 16), pl.multiple_of(WIN * (1 - core[0]), 16))

    def keep(slot, index, cols, value):
        result[index, pl.ds(starts[slot], WIN), cols] = value.astype(BF16)

    windows(win, 2, bias, *work, keep)

    def leave(slot, step):
        copies = []
        for index, out in enumerate(outs):
            for part in range(2):
                copies.append(
                    pltpu.make_async_copy(
                        ready.at[slot, index, part],
                        out.at[:, 2 * step + 2 - part],
                        gone.at[slot, index, part],
                    )
                )
        return copies

    slot = s % 2

    @pl.when(s >= 2)
    def _():
        for copy in leave(slot, s - 2):
            copy.wait()

    used = pl.ds(pl.multiple_of(64 * core[0], 16), 224)
    near_far = pl.ds(pl.multiple_of(208 * core[0], 16), 80)
    for index in range(4):
        beside[index, 0] = result[index, near_far]
        full = dot(back[0], result[index, used])
        ready[slot, index] = full.reshape(2, 2, STRIP, 512).astype(BF16)
    for copy in leave(slot, s):
        copy.start()

    @pl.when(s == 6)
    def _():
        token[...] = jnp.zeros_like(token)
        for copy in leave(1, 5) + leave(0, 6):
            copy.wait()


def work_scratch(places):
    return [
        pltpu.VMEM((places, WIN, 576), F32),
        pltpu.VMEM((places, WIN, 576), F32),
        pltpu.VMEM((places, WIN, 576), BF16),
        pltpu.VMEM((places, WIN, 576), BF16),
    ]


def window_cost(count, moved):
    return pl.CostEstimate(
        flops=count * 6 * 2 * WIN * WIN * 512 * 4,
        bytes_accessed=moved,
        transcendentals=count * 8 * WIN * WIN,
    )


def inner(mid, own, halo, bias, back, core):
    anywhere = pl.BlockSpec(memory_space=pl.ANY)
    return pl.pallas_call(
        inner_body,
        grid_spec=pltpu.PrefetchScalarGridSpec(
            num_scalar_prefetch=1,
            grid=(7,),
            in_specs=[
                pl.BlockSpec((4, 1, WIN, 512), lambda s, core: (0, s, 0, 0)),
                band_spec(),
                band_spec(),
                fixed_spec((1, 2, WIN, 576)),
                side_spec((2 * WIN, 224)),
            ],
            out_specs=[anywhere] * 4
            + [
                pl.BlockSpec((4, 1, 80, 512), lambda s, core: (0, s, 0, 0)),
                fixed_spec((8, 128)),
            ],
            scratch_shapes=[
                pltpu.VMEM((2, 4, WIN, 512), BF16),
                pltpu.VMEM((4, 2 * WIN, 512), BF16),
                pltpu.VMEM((2, 4, 2, 2, STRIP, 512), BF16),
                pltpu.SemaphoreType.DMA((2, 4, 2)),
            ]
            + work_scratch(4),
        ),
        out_shape=[jax.ShapeDtypeStruct((2, 16, STRIP, 512), BF16)] * 4
        + [jax.ShapeDtypeStruct((4, 7, 80, 512), BF16), jax.ShapeDtypeStruct((8, 128), F32)],
        compiler_params=params(),
        cost_estimate=window_cost(14, 24 * MIB),
        name="inner_windows",
    )(core, mid, own, halo, bias, back)


def band_spec():
    return pl.BlockSpec((4, 1, STRIP, 512), lambda s, core: (0, s, 0, 0))


def cut_bias(cut, bias, flag):
    key_part = lax.broadcasted_iota(jnp.int32, (WIN, 576), 0) % STRIP < HALF
    query_part = lax.broadcasted_iota(jnp.int32, (WIN, 576), 1) % STRIP < HALF
    apart = (key_part != query_part) & (flag != 0)
    for group in range(2):
        cut[0, group] = jnp.where(apart, -jnp.inf, bias[0, group])


def outer_body(first, count, edge, core, flags, own, halo, beside, bias, back, p0, p1, p2, p3, o0, o1, o2, o3, win, result, tiles, gone, cut, *work):
    s = pl.program_id(0)
    tile = 2 * core[0]
    outs = (o0, o1, o2, o3)
    place_pair(win, 0, own, halo, core[0] == 1)

    def keep(slot, index, cols, value):
        result[index, 0:WIN, cols] = value.astype(BF16)

    if edge:
        cut_bias(cut, bias, flags[s])
    windows(win, 1, cut if edge else bias, *work, keep)

    def leave(step, index):
        size, row = (3, 45 * step) if edge else (6, 6 * (step + first) + 3)
        return pltpu.make_async_copy(
            tiles.at[index, :, pl.ds(6 * step, size)],
            outs[index].at[:, pl.ds(row, size), tile],
            gone.at[step, index],
        )

    used = pl.ds(pl.multiple_of(64 * (1 - core[0]), 16), 160)
    beside_at = pl.ds(pl.multiple_of(WIN - 64 * core[0], 16), 80)
    for index in range(4):
        result[index, beside_at] = beside[index, 0]
        full = dot(back[0], result[index, used]).reshape(2, 2, 3, 8, 512)
        for part in range(2):
            if edge:

                @pl.when(s == part)
                def _(part=part, full=full, index=index):
                    tiles[index, :, 6 * part : 6 * part + 3] = full[part].astype(BF16)

                continue
            span = pl.ds(6 * s + 3 * (1 - part), 3)
            tiles[index, :, span] = full[part].astype(BF16)
        leave(s, index).start()

    @pl.when(s == count - 1)
    def _():
        for index in range(4):
            for step in range(count):
                leave(step, index).wait()


def outer(partial, own, halo, beside, bias, back, core, flags, first, count, edge=False):
    anywhere = pl.BlockSpec(memory_space=pl.ANY)
    shape = (2, 48, 3, 8, 512)
    return pl.pallas_call(
        functools.partial(outer_body, first, count, edge),
        grid_spec=pltpu.PrefetchScalarGridSpec(
            num_scalar_prefetch=2,
            grid=(count,),
            in_specs=[
                pl.BlockSpec((4, 1, STRIP, 512), lambda s, core, flags: (0, s, 0, 0)),
                pl.BlockSpec((4, 1, STRIP, 512), lambda s, core, flags: (0, s, 0, 0)),
                pl.BlockSpec((4, 1, 80, 512), lambda s, core, flags: (0, s + first, 0, 0)),
                pl.BlockSpec((1, 2, WIN, 576), lambda s, core, flags: (0, 0, 0, 0)),
                pl.BlockSpec((1, 96, 160), lambda s, core, flags: (core[0], 0, 0)),
            ]
            + [anywhere] * 4,
            out_specs=[anywhere] * 4,
            scratch_shapes=[
                pltpu.VMEM((1, 4, WIN, 512), BF16),
                pltpu.VMEM((4, WIN + 80, 512), BF16),
                pltpu.VMEM((4, 2, 6 * count, 8, 512), BF16),
                pltpu.SemaphoreType.DMA((count, 4)),
                pltpu.VMEM((1, 2, WIN, 576), F32),
            ]
            + work_scratch(2),
        ),
        out_shape=[jax.ShapeDtypeStruct(shape, BF16)] * 4,
        input_output_aliases={7 + index: index for index in range(4)},
        compiler_params=params(),
        cost_estimate=window_cost(count, count * 2 * MIB),
        name="outer_windows",
    )(core, flags, own, halo, beside, bias, back, *[x.reshape(shape) for x in partial])


def corner_body(core, flags, mid, near, near_halo, bias, back, p0, p1, p2, p3, o0, o1, o2, o3, beside, win, result, cut, *work):
    s = pl.program_id(0)
    for index in range(4):
        win[0, index] = mid[index, 0]
    place_pair(win, 1, near, near_halo, core[0] == 0)
    cut_bias(cut, bias, flags[s])
    starts = (pl.multiple_of(WIN * core[0], 16), pl.multiple_of(WIN * (1 - core[0]), 16))

    def keep(slot, index, cols, value):
        result[index, pl.ds(starts[slot], WIN), cols] = value.astype(BF16)

    windows(win, 2, cut, *work, keep)
    used = pl.ds(pl.multiple_of(64 * core[0], 16), 224)
    near_far = pl.ds(pl.multiple_of(208 * core[0], 16), 80)
    for index, out in enumerate((o0, o1, o2, o3)):
        beside[index, 0] = result[index, near_far]
        full = dot(back[0], result[index, used])
        out[:, 0] = full.reshape(2, STRIP, 512).astype(BF16)


def corners(partial, flags, mid, near, near_halo, bias, back, core):
    anywhere = pl.BlockSpec(memory_space=pl.ANY)
    shape = (2, 16, STRIP, 512)

    def edge(size):
        return pl.BlockSpec((4, 1, size, 512), lambda s, core, flags: (0, s, 0, 0))

    return pl.pallas_call(
        corner_body,
        grid_spec=pltpu.PrefetchScalarGridSpec(
            num_scalar_prefetch=2,
            grid=(2,),
            in_specs=[
                edge(WIN),
                edge(STRIP),
                edge(STRIP),
                pl.BlockSpec((1, 2, WIN, 576), lambda s, core, flags: (0, 0, 0, 0)),
                pl.BlockSpec((1, WIN, 224), lambda s, core, flags: (core[0], s, 0)),
            ]
            + [anywhere] * 4,
            out_specs=[
                pl.BlockSpec((2, 1, STRIP, 512), lambda s, core, flags: (0, 15 * s, 0, 0))
            ]
            * 4
            + [edge(80)],
            scratch_shapes=[
                pltpu.VMEM((2, 4, WIN, 512), BF16),
                pltpu.VMEM((4, 2 * WIN, 512), BF16),
                pltpu.VMEM((1, 2, WIN, 576), F32),
            ]
            + work_scratch(4),
        ),
        out_shape=[jax.ShapeDtypeStruct(shape, BF16)] * 4
        + [jax.ShapeDtypeStruct((4, 2, 80, 512), BF16)],
        input_output_aliases={7 + index: index for index in range(4)},
        compiler_params=params(),
        cost_estimate=window_cost(4, 8 * MIB),
        name="corner_windows",
    )(core, flags, mid, near, near_halo, bias, back, *[x.reshape(shape) for x in partial])


def bias_body(table, hot, squeeze, out, wide, part):
    for head in range(8):
        line = jnp.broadcast_to(table[head : head + 1], (8, 768))
        line = pltpu.roll(line, 0, 1, stride=1, stride_axis=0)
        for run, base in enumerate(run_bases()):
            turn = int(base - 379) % 768
            turned = pltpu.roll(line, turn, 1)
            group, cols = head // 4, slice(384 * (head % 4), 384 * (head % 4) + 384)
            wide[group, 8 * run : 8 * run + 8, cols] = turned[:, :384]
    for group in range(2):
        high = wide[group].astype(BF16)
        part[0, group] = high
        part[1, group] = (wide[group] - high.astype(F32)).astype(BF16)
    for group in range(2):
        total = None
        for order in range(2):
            spread = dot(part[order, group], hot[...]).astype(BF16)
            piece = dot(squeeze[...], spread)
            total = piece if total is None else total + piece
        out[0, group] = total


def bias_operands(rel_table):
    tokens = (run_bases()[:, None] + np.arange(6)).reshape(WIN)
    hot = np.zeros((4, 384, 4, WIN), np.float32)
    for head in range(4):
        hot[head, tokens, head, np.arange(WIN)] = 1
    squeeze = np.zeros((24, 6, 24, 8), np.float32)
    for run in range(24):
        squeeze[run, np.arange(6), run, np.arange(6)] = 1
    hot = jnp.asarray(hot.reshape(4 * 384, 4 * WIN), BF16)
    squeeze = jnp.asarray(squeeze.reshape(WIN, 192), BF16)
    table = jnp.pad(rel_table, ((0, 0), (0, 768 - rel_table.shape[1])))
    return table, hot, squeeze


def side_tables():
    far_strip, near_strip = (0, 3), (3, 0)
    far, tiled, whole, near_back, far_back = [], [], [], [], []
    for side in range(2):
        far.append(far_matrix(far_strip[side], 2 * side))
        whole.append(strip_matrix([far_strip[side], near_strip[side], 1, 2]))
        by_tile = whole[side].reshape(2 * WIN, 12, 3, 8)[:, :, [2 * side, 2 - 2 * side, 1]]
        tiled.append(by_tile.transpose(0, 2, 1, 3).reshape(2 * WIN, 2 * WIN))
        own = strip_matrix([near_strip[side]]).T
        middle = strip_matrix([1, 2]).T
        pad = np.zeros((2 * WIN, 8), np.float32)
        pad_far = np.zeros((96, 8), np.float32)
        inside = far_matrix(1 + side, 2 * side).T
        if side == 0:
            near_back.append(np.concatenate([middle, own, pad], axis=1))
            far_back.append(np.concatenate([pad_far, far[0].T, inside, pad_far], axis=1))
        else:
            near_back.append(np.concatenate([pad, own, middle], axis=1))
            far_back.append(np.concatenate([far[1].T, pad_far, pad_far, inside], axis=1))
    stacked = (tiled, whole, near_back, far_back)
    return [jnp.asarray(np.stack(table), BF16) for table in stacked]


def shards(queries, key_tokens, value_tokens, out_grad, land_mask, land_embed, rel_table):
    lev, rows, cols, width = queries.shape
    lat = lax.axis_index("lat")
    core = jnp.reshape(lax.axis_index("lon") % 2, (1,))
    bands = lax.axis_size("lat")
    sectors = lax.axis_size("lon")
    arrays = (queries, key_tokens, value_tokens, out_grad)
    mask = jnp.broadcast_to(
        land_mask.astype(F32).reshape(rows, 3, 8, 1), (rows, 3, 8, 128)
    )
    embed = land_embed.reshape(1, width)
    edge_perm, all_perm, near_back, far_back = side_tables()

    to_far = [((2 * k + 1) % sectors, (2 * k + 2) % sectors) for k in range(sectors // 2)]
    to_far += [(b, a) for a, b in to_far]
    to_near = [(i, i ^ 1) for i in range(sectors)]

    far_a, far_b, near, mid, *edge_rows, bias = pack_edges(
        arrays, mask, embed, edge_perm, bias_operands(rel_table), bands
    )
    top, bottom, below, above = (x.reshape(4, 2, STRIP, width) for x in edge_rows)
    far_halo_a = lax.ppermute(far_a, "lon", to_far)
    far_halo_b = lax.ppermute(far_b, "lon", to_far)
    near_halo = lax.ppermute(near, "lon", to_near)

    far_c, near_c, mid_c = pack_corners(top, bottom, below, above, all_perm, core)
    far_halo_c = lax.ppermute(far_c, "lon", to_far)
    near_halo_c = lax.ppermute(near_c, "lon", to_near)

    *partial, beside, _ = inner(mid, near, near_halo, bias, near_back, core)
    flags = jnp.stack([lat == 0, lat == bands - 1]).astype(jnp.int32)
    *partial, beside_c = corners(
        partial, flags, mid_c, near_c, near_halo_c, bias, near_back, core
    )
    partial = outer(partial, far_a, far_halo_a, beside, bias, far_back, core, flags, 0, 4)
    partial = outer(partial, far_b, far_halo_b, beside, bias, far_back, core, flags, 4, 3)
    final = outer(
        partial, far_c, far_halo_c, beside_c, bias, far_back, core, flags, 0, 2, edge=True
    )
    return tuple(x.reshape(queries.shape) for x in final)


def solution(mesh):
    tokens = P(None, "lat", "lon", None)
    return jax.shard_map(
        shards,
        mesh=mesh,
        in_specs=(tokens, tokens, tokens, tokens, P("lat", "lon"), P(), P()),
        out_specs=(tokens,) * 4,
        check_vma=False,
    )
```

```python
import functools

import jax
import jax.numpy as jnp
import numpy as np
from jax import lax
from jax.experimental import pallas as pl
from jax.experimental.pallas import tpu as pltpu
from jax.sharding import PartitionSpec as P

F32 = jnp.float32
BF16 = jnp.bfloat16
HALF = 36
STRIP = 72
WIN = 144
GROUP = 256
MIB = 1 << 20
VMEM_BYTES = 63 * MIB


def strip_matrix(strips):
    out = np.zeros((len(strips), 2, 2, 3, 6, 2, 2, 3, 24), np.float32)
    for place, strip in enumerate(strips):
        for part in range(2):
            for lev in range(2):
                for row in range(3):
                    for col in range(6):
                        out[place, part, lev, row, col, part, lev, row, 6 * strip + col] = 1
    return out.reshape(len(strips) * STRIP, 2 * WIN)


def far_matrix(strip, tile):
    full = strip_matrix([strip]).reshape(STRIP, 2, 2, 3, 3, 8)
    return full[:, :, :, :, tile].reshape(STRIP, 96)


def run_bases():
    run = np.arange(24)
    half, part, lev, row = run // 12, run // 6 % 2, run // 3 % 2, run % 3
    return lev * 253 + (row + 3 * (1 - part)) * 23 + 6 * half


def dot(a, b, ca=1, cb=0):
    return lax.dot_general(a, b, (((ca,), (cb,)), ((), ())), preferred_element_type=F32)


def keyed_rows(key, mask, embed):
    wide = jnp.concatenate([mask] * 4, axis=-1)
    return (key + (wide * embed)[None]).astype(BF16).astype(F32)


def side_spec(shape):
    return pl.BlockSpec((1, *shape), lambda s, core: (core[0],) + (0,) * len(shape))


def fixed_spec(shape):
    return pl.BlockSpec(shape, lambda s, core: (0,) * len(shape))


def params():
    return pltpu.CompilerParams(vmem_limit_bytes=VMEM_BYTES)


def edges_body(bands, q, k, v, g, mask, embed, perm, table, hot, squeeze, far_a, far_b, near, mid, top, bottom, below, above, bias, held, packed, interior, rows, came, gone, rows_came, rows_gone, sent, received, wide, part):
    core = lax.axis_index("lon") % 2
    lat, lon = lax.axis_index("lat"), lax.axis_index("lon")
    neighbours = ((lat + bands - 1) % bands, (lat + 1) % bands)
    barrier = pltpu.get_barrier_semaphore()
    for neighbour in neighbours:
        pl.semaphore_signal(
            barrier, inc=1, device_id=(neighbour, lon), device_id_type=pl.DeviceIdType.MESH
        )
    sources = (q, k, v, g)
    tiles = (2 * core, 2 - 2 * core, 1)
    ends = ((top, 0), (bottom, 45))

    def rows_in(end, index):
        row = ends[end][1]
        return pltpu.make_async_copy(
            sources[index].at[:, row : row + 3], rows.at[end, index], rows_came.at[end, index]
        )

    def rows_out(end, index):
        return pltpu.make_async_copy(
            rows.at[end, index], ends[end][0].at[index], rows_gone.at[end, index]
        )

    def rows_over(end, index):
        return pltpu.make_async_remote_copy(
            src_ref=rows.at[end, index],
            dst_ref=(below, above)[end].at[index],
            send_sem=sent.at[end, index],
            recv_sem=received.at[end, index],
            device_id=(neighbours[end], lon),
            device_id_type=pl.DeviceIdType.MESH,
        )

    def fetch(side, index):
        return pltpu.make_async_copy(
            sources[index].at[:, :, tiles[side]], held.at[side, index], came.at[side, index]
        )

    def send_off(side, index):
        if side == 0:
            return [
                pltpu.make_async_copy(
                    packed.at[0, index, 0:4], far_a.at[index], gone.at[0, index]
                ),
                pltpu.make_async_copy(
                    packed.at[0, index, 4:7], far_b.at[index], gone.at[2, index]
                ),
            ]
        if side == 1:
            return [pltpu.make_async_copy(packed.at[1, index], near.at[index], gone.at[1, index])]
        return [pltpu.make_async_copy(interior.at[index], mid.at[index], gone.at[3, index])]

    for end in range(2):
        for index in range(4):
            rows_in(end, index).start()
    for index in range(4):
        for side in range(3):
            fetch(side, index).start()
    pl.semaphore_wait(barrier, 2)
    for end in range(2):
        row = ends[end][1]
        for index in (0, 2, 3, 1):
            rows_in(end, index).wait()
            if index == 1:
                keyed = keyed_rows(rows[end, 1].astype(F32), mask[row : row + 3], embed[...])
                rows[end, 1] = keyed.astype(BF16)
            rows_over(end, index).start()
            rows_out(end, index).start()
    for index in range(4):
        for side in range(3):
            fetch(side, index).wait()

        def pack_band(step, carry, index=index):
            lower, upper = pl.ds(6 * step + 6, 3), pl.ds(6 * step + 3, 3)
            pieces = []
            for side in range(3):
                for span in (lower, upper):
                    piece = held[side, index, :, span].astype(F32)
                    if index == 1:
                        column = mask[span, pl.ds(tiles[side], 1)][:, 0]
                        piece = keyed_rows(piece, column, embed[...])
                    pieces.append(piece.reshape(48, 512))
            strips = dot(perm[core], jnp.concatenate(pieces, axis=0).astype(BF16))
            if index == 0:
                strips = strips * 0.125
            packed[0, index, step] = strips[:STRIP].astype(BF16)
            packed[1, index, step] = strips[STRIP : 2 * STRIP].astype(BF16)
            interior[index, step] = strips[2 * STRIP :].astype(BF16)
            return carry

        lax.fori_loop(0, 7, pack_band, 0)
        for side in range(3):
            for copy in send_off(side, index):
                copy.start()
    bias_body(table, hot, squeeze, bias, wide, part)
    for index in range(4):
        for side in range(3):
            for copy in send_off(side, index):
                copy.wait()
        for end in range(2):
            rows_out(end, index).wait()
            rows_over(end, index).wait()


def pack_edges(arrays, mask, embed, perm, bias_operands, bands):
    tiles = [array.reshape(2, 48, 3, 8, 512) for array in arrays]
    anywhere = pl.BlockSpec(memory_space=pl.ANY)
    local = pl.BlockSpec(memory_space=pltpu.VMEM)
    far_a, far_b, near = (
        jax.ShapeDtypeStruct((4, count, STRIP, 512), BF16) for count in (4, 3, 7)
    )
    ends = jax.ShapeDtypeStruct((4, 2, 3, 3, 8, 512), BF16)
    interior = jax.ShapeDtypeStruct((4, 7, WIN, 512), BF16)
    return pl.pallas_call(
        functools.partial(edges_body, bands),
        in_specs=[anywhere] * 4 + [local] * 6,
        out_specs=[anywhere] * 8 + [local],
        scratch_shapes=[
            pltpu.VMEM((3, 4, 2, 48, 8, 512), BF16),
            pltpu.VMEM((2, 4, 7, STRIP, 512), BF16),
            pltpu.VMEM((4, 7, WIN, 512), BF16),
            pltpu.VMEM((2, 4, 2, 3, 3, 8, 512), BF16),
            pltpu.SemaphoreType.DMA((3, 4)),
            pltpu.SemaphoreType.DMA((4, 4)),
            pltpu.SemaphoreType.DMA((2, 4)),
            pltpu.SemaphoreType.DMA((2, 4)),
            pltpu.SemaphoreType.DMA((2, 4)),
            pltpu.SemaphoreType.DMA((2, 4)),
            pltpu.VMEM((2, 192, 4 * 384), F32),
            pltpu.VMEM((2, 2, 192, 4 * 384), BF16),
        ],
        out_shape=[far_a, far_b, near, interior, ends, ends, ends, ends]
        + [jax.ShapeDtypeStruct((1, 2, WIN, 576), F32)],
        compiler_params=pltpu.CompilerParams(
            vmem_limit_bytes=VMEM_BYTES, collective_id=0, has_side_effects=True
        ),
        cost_estimate=pl.CostEstimate(
            flops=2 * 28 * 288 * 288 * 512, bytes_accessed=24 * MIB, transcendentals=0
        ),
        name="pack_edges",
    )(*tiles, mask, embed, perm, *bias_operands)


def corners_body(core, top, bottom, below, above, perm, far, near, mid):
    for index in range(4):
        for place, (first, second) in enumerate(((top, above), (below, bottom))):
            first = first[index].astype(F32)
            second = second[index].astype(F32)
            tokens = jnp.concatenate([first[0], first[1], second[0], second[1]], axis=0)
            strips = dot(perm[0], tokens.astype(BF16))
            if index == 0:
                strips = strips * 0.125
            far[index, place] = strips[:STRIP].astype(BF16)
            near[index, place] = strips[STRIP : 2 * STRIP].astype(BF16)
            mid[index, place] = strips[2 * STRIP :].astype(BF16)


def pack_corners(top, bottom, below, above, perm, core):
    sizes = (STRIP, STRIP, WIN)
    return pl.pallas_call(
        corners_body,
        grid_spec=pltpu.PrefetchScalarGridSpec(
            num_scalar_prefetch=1,
            grid=(1,),
            in_specs=[fixed_spec((4, 2, STRIP, 512))] * 4 + [side_spec((2 * WIN, 2 * WIN))],
            out_specs=[fixed_spec((4, 2, size, 512)) for size in sizes],
        ),
        out_shape=[jax.ShapeDtypeStruct((4, 2, size, 512), BF16) for size in sizes],
        compiler_params=params(),
        cost_estimate=pl.CostEstimate(
            flops=2 * 8 * 288 * 288 * 512, bytes_accessed=5 * MIB, transcendentals=0
        ),
        name="pack_corners",
    )(core, top, bottom, below, above, perm)


def windows(win, slots, bias, scores, grads, low, dlow, store):
    lane = lax.broadcasted_iota(jnp.int32, (1, GROUP), 1) // 64

    def spread(x):
        return jnp.concatenate(
            [x * jnp.where(lane == h, 1.0, 0.0).astype(BF16) for h in range(4)], axis=0
        )

    def by_head(wide):
        total = None
        for h in range(4):
            piece = jnp.where(lane == h, wide[WIN * h : WIN * (h + 1)], 0.0)
            total = piece if total is None else total + piece
        return total

    jobs = []
    for slot in range(slots):
        for group in range(2):
            cols = slice(GROUP * group, GROUP * (group + 1))
            q, k, v, g = (win[slot, index, :, cols] for index in range(4))
            q_wide, g_wide = spread(q), spread(g)
            place = 2 * slot + group
            scores[place] = dot(k, q_wide, 1, 1)
            grads[place] = dot(v, g_wide, 1, 1)
            jobs.append((slot, group, place, cols, k, v, q_wide, g_wide))
    for slot, group, place, cols, k, v, q_wide, g_wide in jobs:
        for start in range(0, 576, 128):
            part = slice(start, min(start + 128, 576))
            s = scores[place, :, part] + bias[0, group, :, part]
            e = jnp.exp(s - jnp.max(s, axis=0, keepdims=True))
            p = e * (1.0 / jnp.sum(e, axis=0, keepdims=True))
            gp = grads[place, :, part]
            delta = jnp.sum(p * gp, axis=0, keepdims=True)
            low[place, :, part] = p.astype(BF16)
            dlow[place, :, part] = (p * (gp - delta)).astype(BF16)
        p_low, d_low = low[place], dlow[place]
        store(slot, 0, cols, by_head(dot(p_low, v, 0, 0)))
        store(slot, 1, cols, by_head(dot(d_low, k, 0, 0)) * 0.125)
        store(slot, 2, cols, dot(d_low, q_wide))
        store(slot, 3, cols, dot(p_low, g_wide))


def place_pair(win, slot, own, halo, own_left):
    def put(left, right):
        for index in range(4):
            both = jnp.concatenate(
                [left[index, 0].astype(F32), right[index, 0].astype(F32)], axis=0
            )
            win[slot, index] = both.astype(BF16)

    @pl.when(own_left)
    def _():
        put(own, halo)

    @pl.when(jnp.logical_not(own_left))
    def _():
        put(halo, own)


def inner_body(core, mid, own, halo, bias, back, *rest):
    outs, beside, token, (win, result, ready, gone), work = rest[:4], rest[4], rest[5], rest[6:10], rest[10:]
    s = pl.program_id(0)
    for index in range(4):
        win[0, index] = mid[index, 0]
    place_pair(win, 1, own, halo, core[0] == 0)

    starts = (pl.multiple_of(WIN * core[0], 16), pl.multiple_of(WIN * (1 - core[0]), 16))

    def keep(slot, index, cols, value):
        result[index, pl.ds(starts[slot], WIN), cols] = value.astype(BF16)

    windows(win, 2, bias, *work, keep)

    def leave(slot, step):
        copies = []
        for index, out in enumerate(outs):
            for part in range(2):
                copies.append(
                    pltpu.make_async_copy(
                        ready.at[slot, index, part],
                        out.at[:, 2 * step + 2 - part],
                        gone.at[slot, index, part],
                    )
                )
        return copies

    slot = s % 2

    @pl.when(s >= 2)
    def _():
        for copy in leave(slot, s - 2):
            copy.wait()

    used = pl.ds(pl.multiple_of(64 * core[0], 16), 224)
    near_far = pl.ds(pl.multiple_of(208 * core[0], 16), 80)
    for index in range(4):
        beside[index, 0] = result[index, near_far]
        full = dot(back[0], result[index, used])
        ready[slot, index] = full.reshape(2, 2, STRIP, 512).astype(BF16)
    for copy in leave(slot, s):
        copy.start()

    @pl.when(s == 6)
    def _():
        token[...] = jnp.zeros_like(token)
        for copy in leave(1, 5) + leave(0, 6):
            copy.wait()


def work_scratch(places):
    return [
        pltpu.VMEM((places, WIN, 576), F32),
        pltpu.VMEM((places, WIN, 576), F32),
        pltpu.VMEM((places, WIN, 576), BF16),
        pltpu.VMEM((places, WIN, 576), BF16),
    ]


def window_cost(count, moved):
    return pl.CostEstimate(
        flops=count * 6 * 2 * WIN * WIN * 512 * 4,
        bytes_accessed=moved,
        transcendentals=count * 8 * WIN * WIN,
    )


def inner(mid, own, halo, bias, back, core):
    anywhere = pl.BlockSpec(memory_space=pl.ANY)
    return pl.pallas_call(
        inner_body,
        grid_spec=pltpu.PrefetchScalarGridSpec(
            num_scalar_prefetch=1,
            grid=(7,),
            in_specs=[
                pl.BlockSpec((4, 1, WIN, 512), lambda s, core: (0, s, 0, 0)),
                band_spec(),
                band_spec(),
                fixed_spec((1, 2, WIN, 576)),
                side_spec((2 * WIN, 224)),
            ],
            out_specs=[anywhere] * 4
            + [
                pl.BlockSpec((4, 1, 80, 512), lambda s, core: (0, s, 0, 0)),
                fixed_spec((8, 128)),
            ],
            scratch_shapes=[
                pltpu.VMEM((2, 4, WIN, 512), BF16),
                pltpu.VMEM((4, 2 * WIN, 512), BF16),
                pltpu.VMEM((2, 4, 2, 2, STRIP, 512), BF16),
                pltpu.SemaphoreType.DMA((2, 4, 2)),
            ]
            + work_scratch(4),
        ),
        out_shape=[jax.ShapeDtypeStruct((2, 16, STRIP, 512), BF16)] * 4
        + [jax.ShapeDtypeStruct((4, 7, 80, 512), BF16), jax.ShapeDtypeStruct((8, 128), F32)],
        compiler_params=params(),
        cost_estimate=window_cost(14, 24 * MIB),
        name="inner_windows",
    )(core, mid, own, halo, bias, back)


def band_spec():
    return pl.BlockSpec((4, 1, STRIP, 512), lambda s, core: (0, s, 0, 0))


def cut_bias(cut, bias, flag):
    key_part = lax.broadcasted_iota(jnp.int32, (WIN, 576), 0) % STRIP < HALF
    query_part = lax.broadcasted_iota(jnp.int32, (WIN, 576), 1) % STRIP < HALF
    apart = (key_part != query_part) & (flag != 0)
    for group in range(2):
        cut[0, group] = jnp.where(apart, -jnp.inf, bias[0, group])


def outer_body(first, count, edge, core, flags, *refs):
    inputs = 6 if edge else 3
    strips, (bias, back) = refs[:inputs], refs[inputs : inputs + 2]
    outs = refs[inputs + 6 : inputs + 10]
    win, result, tiles, gone, cut, *work = refs[inputs + 10 :]
    s = pl.program_id(0)
    tile = 2 * core[0]
    left = core[0] == 1
    whole = s < count
    if edge:

        @pl.when(whole)
        def _():
            place_pair(win, 0, strips[0], strips[1], left)

        @pl.when(s == 0)
        def _():
            cut[...] = bias[...]

        @pl.when(jnp.logical_not(whole))
        def _():
            place_pair(win, 0, strips[3], strips[4], left)
            cut_bias(cut, bias, flags[jnp.maximum(s - count, 0)])
    else:
        place_pair(win, 0, strips[0], strips[1], left)

    def keep(slot, index, cols, value):
        result[index, 0:WIN, cols] = value.astype(BF16)

    windows(win, 1, cut if edge else bias, *work, keep)

    def leave(step, index):
        return pltpu.make_async_copy(
            tiles.at[index, :, pl.ds(6 * step, 6)],
            outs[index].at[:, pl.ds(6 * (step + first) + 3, 6), tile],
            gone.at[step, index],
        )

    def leave_edge(part, index):
        return pltpu.make_async_copy(
            tiles.at[index, :, 6 * count + 3 * part : 6 * count + 3 * part + 3],
            outs[index].at[:, 45 * part : 45 * part + 3, tile],
            gone.at[count + part, index],
        )

    used = pl.ds(pl.multiple_of(64 * (1 - core[0]), 16), 160)
    beside_at = pl.ds(pl.multiple_of(WIN - 64 * core[0], 16), 80)
    if edge:

        @pl.when(whole)
        def _():
            for index in range(4):
                result[index, beside_at] = strips[2][index, 0]

        @pl.when(jnp.logical_not(whole))
        def _():
            for index in range(4):
                result[index, beside_at] = strips[5][index, 0]
    else:
        for index in range(4):
            result[index, beside_at] = strips[2][index, 0]

    for index in range(4):
        full = dot(back[0], result[index, used]).reshape(2, 2, 3, 8, 512).astype(BF16)

        def put_band(index=index, full=full):
            for part in range(2):
                tiles[index, :, pl.ds(6 * s + 3 * (1 - part), 3)] = full[part]
            leave(s, index).start()

        if not edge:
            put_band()
            continue
        pl.when(whole)(put_band)
        for part in range(2):

            @pl.when(s == count + part)
            def _(part=part, index=index, full=full):
                row = 6 * count + 3 * part
                tiles[index, :, row : row + 3] = full[part]
                leave_edge(part, index).start()

    @pl.when(s == count + (2 if edge else 0) - 1)
    def _():
        for index in range(4):
            for step in range(count):
                leave(step, index).wait()
            if edge:
                for part in range(2):
                    leave_edge(part, index).wait()


def outer(partial, strips, bias, back, core, flags, first, count):
    edge = len(strips) == 6
    steps = count + (2 if edge else 0)
    anywhere = pl.BlockSpec(memory_space=pl.ANY)
    shape = (2, 48, 3, 8, 512)

    def band(size, shift=0):
        return pl.BlockSpec(
            (4, 1, size, 512), lambda s, core, flags: (0, jnp.minimum(s, count - 1) + shift, 0, 0)
        )

    def corner(size):
        return pl.BlockSpec(
            (4, 1, size, 512), lambda s, core, flags: (0, jnp.maximum(s - count, 0), 0, 0)
        )

    specs = [band(STRIP), band(STRIP), band(80, first)]
    if edge:
        specs += [corner(STRIP), corner(STRIP), corner(80)]
    return pl.pallas_call(
        functools.partial(outer_body, first, count, edge),
        grid_spec=pltpu.PrefetchScalarGridSpec(
            num_scalar_prefetch=2,
            grid=(steps,),
            in_specs=specs
            + [
                pl.BlockSpec((1, 2, WIN, 576), lambda s, core, flags: (0, 0, 0, 0)),
                pl.BlockSpec((1, 96, 160), lambda s, core, flags: (core[0], 0, 0)),
            ]
            + [anywhere] * 4,
            out_specs=[anywhere] * 4,
            scratch_shapes=[
                pltpu.VMEM((1, 4, WIN, 512), BF16),
                pltpu.VMEM((4, WIN + 80, 512), BF16),
                pltpu.VMEM((4, 2, 6 * steps, 8, 512), BF16),
                pltpu.SemaphoreType.DMA((steps, 4)),
                pltpu.VMEM((1, 2, WIN, 576), F32),
            ]
            + work_scratch(2),
        ),
        out_shape=[jax.ShapeDtypeStruct(shape, BF16)] * 4,
        input_output_aliases={len(strips) + 4 + index: index for index in range(4)},
        compiler_params=params(),
        cost_estimate=window_cost(steps, steps * 2 * MIB),
        name="outer_windows",
    )(core, flags, *strips, bias, back, *[x.reshape(shape) for x in partial])


def corner_body(core, flags, mid, near, near_halo, bias, back, p0, p1, p2, p3, o0, o1, o2, o3, beside, win, result, cut, *work):
    s = pl.program_id(0)
    for index in range(4):
        win[0, index] = mid[index, 0]
    place_pair(win, 1, near, near_halo, core[0] == 0)
    cut_bias(cut, bias, flags[s])
    starts = (pl.multiple_of(WIN * core[0], 16), pl.multiple_of(WIN * (1 - core[0]), 16))

    def keep(slot, index, cols, value):
        result[index, pl.ds(starts[slot], WIN), cols] = value.astype(BF16)

    windows(win, 2, cut, *work, keep)
    used = pl.ds(pl.multiple_of(64 * core[0], 16), 224)
    near_far = pl.ds(pl.multiple_of(208 * core[0], 16), 80)
    for index, out in enumerate((o0, o1, o2, o3)):
        beside[index, 0] = result[index, near_far]
        full = dot(back[0], result[index, used])
        out[:, 0] = full.reshape(2, STRIP, 512).astype(BF16)


def corners(partial, flags, mid, near, near_halo, bias, back, core):
    anywhere = pl.BlockSpec(memory_space=pl.ANY)
    shape = (2, 16, STRIP, 512)

    def edge(size):
        return pl.BlockSpec((4, 1, size, 512), lambda s, core, flags: (0, s, 0, 0))

    return pl.pallas_call(
        corner_body,
        grid_spec=pltpu.PrefetchScalarGridSpec(
            num_scalar_prefetch=2,
            grid=(2,),
            in_specs=[
                edge(WIN),
                edge(STRIP),
                edge(STRIP),
                pl.BlockSpec((1, 2, WIN, 576), lambda s, core, flags: (0, 0, 0, 0)),
                pl.BlockSpec((1, WIN, 224), lambda s, core, flags: (core[0], s, 0)),
            ]
            + [anywhere] * 4,
            out_specs=[
                pl.BlockSpec((2, 1, STRIP, 512), lambda s, core, flags: (0, 15 * s, 0, 0))
            ]
            * 4
            + [edge(80)],
            scratch_shapes=[
                pltpu.VMEM((2, 4, WIN, 512), BF16),
                pltpu.VMEM((4, 2 * WIN, 512), BF16),
                pltpu.VMEM((1, 2, WIN, 576), F32),
            ]
            + work_scratch(4),
        ),
        out_shape=[jax.ShapeDtypeStruct(shape, BF16)] * 4
        + [jax.ShapeDtypeStruct((4, 2, 80, 512), BF16)],
        input_output_aliases={7 + index: index for index in range(4)},
        compiler_params=params(),
        cost_estimate=window_cost(4, 8 * MIB),
        name="corner_windows",
    )(core, flags, mid, near, near_halo, bias, back, *[x.reshape(shape) for x in partial])


def bias_body(table, hot, squeeze, out, wide, part):
    for head in range(8):
        line = jnp.broadcast_to(table[head : head + 1], (8, 768))
        line = pltpu.roll(line, 0, 1, stride=1, stride_axis=0)
        for run, base in enumerate(run_bases()):
            turn = int(base - 379) % 768
            turned = pltpu.roll(line, turn, 1)
            group, cols = head // 4, slice(384 * (head % 4), 384 * (head % 4) + 384)
            wide[group, 8 * run : 8 * run + 8, cols] = turned[:, :384]
    for group in range(2):
        high = wide[group].astype(BF16)
        part[0, group] = high
        part[1, group] = (wide[group] - high.astype(F32)).astype(BF16)
    for group in range(2):
        total = None
        for order in range(2):
            spread = dot(part[order, group], hot[...]).astype(BF16)
            piece = dot(squeeze[...], spread)
            total = piece if total is None else total + piece
        out[0, group] = total


def bias_operands(rel_table):
    tokens = (run_bases()[:, None] + np.arange(6)).reshape(WIN)
    hot = np.zeros((4, 384, 4, WIN), np.float32)
    for head in range(4):
        hot[head, tokens, head, np.arange(WIN)] = 1
    squeeze = np.zeros((24, 6, 24, 8), np.float32)
    for run in range(24):
        squeeze[run, np.arange(6), run, np.arange(6)] = 1
    hot = jnp.asarray(hot.reshape(4 * 384, 4 * WIN), BF16)
    squeeze = jnp.asarray(squeeze.reshape(WIN, 192), BF16)
    table = jnp.pad(rel_table, ((0, 0), (0, 768 - rel_table.shape[1])))
    return table, hot, squeeze


def side_tables():
    far_strip, near_strip = (0, 3), (3, 0)
    far, tiled, whole, near_back, far_back = [], [], [], [], []
    for side in range(2):
        far.append(far_matrix(far_strip[side], 2 * side))
        whole.append(strip_matrix([far_strip[side], near_strip[side], 1, 2]))
        by_tile = whole[side].reshape(2 * WIN, 12, 3, 8)[:, :, [2 * side, 2 - 2 * side, 1]]
        tiled.append(by_tile.transpose(0, 2, 1, 3).reshape(2 * WIN, 2 * WIN))
        own = strip_matrix([near_strip[side]]).T
        middle = strip_matrix([1, 2]).T
        pad = np.zeros((2 * WIN, 8), np.float32)
        pad_far = np.zeros((96, 8), np.float32)
        inside = far_matrix(1 + side, 2 * side).T
        if side == 0:
            near_back.append(np.concatenate([middle, own, pad], axis=1))
            far_back.append(np.concatenate([pad_far, far[0].T, inside, pad_far], axis=1))
        else:
            near_back.append(np.concatenate([pad, own, middle], axis=1))
            far_back.append(np.concatenate([far[1].T, pad_far, pad_far, inside], axis=1))
    stacked = (tiled, whole, near_back, far_back)
    return [jnp.asarray(np.stack(table), BF16) for table in stacked]


def shards(queries, key_tokens, value_tokens, out_grad, land_mask, land_embed, rel_table):
    lev, rows, cols, width = queries.shape
    lat = lax.axis_index("lat")
    core = jnp.reshape(lax.axis_index("lon") % 2, (1,))
    bands = lax.axis_size("lat")
    sectors = lax.axis_size("lon")
    arrays = (queries, key_tokens, value_tokens, out_grad)
    mask = jnp.broadcast_to(
        land_mask.astype(F32).reshape(rows, 3, 8, 1), (rows, 3, 8, 128)
    )
    embed = land_embed.reshape(1, width)
    edge_perm, all_perm, near_back, far_back = side_tables()

    to_far = [((2 * k + 1) % sectors, (2 * k + 2) % sectors) for k in range(sectors // 2)]
    to_far += [(b, a) for a, b in to_far]
    to_near = [(i, i ^ 1) for i in range(sectors)]

    far_a, far_b, near, mid, *edge_rows, bias = pack_edges(
        arrays, mask, embed, edge_perm, bias_operands(rel_table), bands
    )
    top, bottom, below, above = (x.reshape(4, 2, STRIP, width) for x in edge_rows)
    far_halo_a = lax.ppermute(far_a, "lon", to_far)
    far_halo_b = lax.ppermute(far_b, "lon", to_far)
    near_halo = lax.ppermute(near, "lon", to_near)

    far_c, near_c, mid_c = pack_corners(top, bottom, below, above, all_perm, core)
    far_halo_c = lax.ppermute(far_c, "lon", to_far)
    near_halo_c = lax.ppermute(near_c, "lon", to_near)

    *partial, beside, _ = inner(mid, near, near_halo, bias, near_back, core)
    flags = jnp.stack([lat == 0, lat == bands - 1]).astype(jnp.int32)
    *partial, beside_c = corners(
        partial, flags, mid_c, near_c, near_halo_c, bias, near_back, core
    )
    partial = outer(
        partial, (far_a, far_halo_a, beside), bias, far_back, core, flags, 0, 4
    )
    late = (far_b, far_halo_b, beside, far_c, far_halo_c, beside_c)
    final = outer(partial, late, bias, far_back, core, flags, 4, 3)
    return tuple(x.reshape(queries.shape) for x in final)


def solution(mesh):
    tokens = P(None, "lat", "lon", None)
    return jax.shard_map(
        shards,
        mesh=mesh,
        in_specs=(tokens, tokens, tokens, tokens, P("lat", "lon"), P(), P()),
        out_specs=(tokens,) * 4,
        check_vma=False,
    )
```
